32 devices in a mesh: batch: 16 (over z, y, x), ffn: 2 (over core).
Axes of the slice: x: 2, y: 2, z: 4, core: 2. Of those that a mesh axis runs over, the one named last changes fastest.
Arguments:
- source: bfloat16 [32, 1024, 512], P(('batch', 'ffn')), may hold values from -6 to 6
- target: bfloat16 [32, 1024, 512], P(('batch', 'ffn')), may hold values from -6 to 6
- routes: int32 [32, 3, 1024, 2], P(('batch', 'ffn')), may hold values from 0 to 7, as said below
- overflow: int32 [32, 3, 1024, 2], P(('batch', 'ffn')), may hold values from 0 to 1, as said below
- pairs: int32 [32, 2, 1024], P(('batch', 'ffn')), may hold values from 0 to 3, as said below
- gains: float32 [5, 512], replicated, may hold values from 0.5 to 1.5
- router: bfloat16 [3, 512, 8], replicated, may hold values from -0.4375 to 0.4375
- query: bfloat16 [3, 512, 512], replicated, may hold values from -0.25 to 0.25
- keyval: bfloat16 [3, 512, 128], replicated, may hold values from -0.25 to 0.25
- output: bfloat16 [3, 512, 512], replicated, may hold values from -6 to 6
- ffn_in: bfloat16 [2, 512, 2048], P(None, None, 'ffn'), may hold values from -0.25 to 0.25
- ffn_out: bfloat16 [2, 2048, 512], P(None, 'ffn'), may hold values from -0.125 to 0.125
- cot_source: bfloat16 [32, 1024, 512], P(('batch', 'ffn')), may hold values from -6 to 6
- cot_target: bfloat16 [32, 1024, 512], P(('batch', 'ffn')), may hold values from -6 to 6
Outputs:
- encoded_out: bfloat16 [32, 1024, 512], P(('batch', 'ffn'))
- decoded_out: bfloat16 [32, 1024, 512], P(('batch', 'ffn'))
- grad_source: float32 [32, 1024, 512], P(('batch', 'ffn'))
- grad_target: float32 [32, 1024, 512], P(('batch', 'ffn'))
- grad_gains: float32 [5, 512], replicated
- grad_router: float32 [3, 512, 8], replicated
- grad_query: float32 [3, 512, 512], replicated
- grad_keyval: float32 [3, 512, 128], replicated
- grad_output: float32 [3, 512, 512], replicated
- grad_ffn_in: float32 [2, 512, 2048], P(None, None, 'ffn')
- grad_ffn_out: float32 [2, 2048, 512], P(None, 'ffn')
The draws below stay inside these ranges and needn't reach their ends.
Inputs may be any that keep to these rules, and one draw needn't show every extreme that they name: `routes`: the two experts of a token differ. overflow[r, l, t, k] is 1 exactly when 256 or more pairs of row r and layer l name the same expert before pair (t, k), in the order of tokens with k = 0 before k = 1. In each row, pairs[r, 0] (source) and pairs[r, 1] (target) never fall and take every number from 0 to 3; target pair k belongs with source pair k.
All inputs are finite; a program needn't handle non-finite values.
Results may differ from the reference program's by a relative error of at most 0.025.
Values may be sent and summed in bfloat16 or wider, within the bound.
No kernel may reach another device: no remote copies, remote signals or barrier semaphores. Data moves between devices by JAX's collectives and lax.ppermute only.
A program may use at most 320 MiB of HBM per device.

```python
import jax
import jax.numpy as jnp
from jax import lax

D = 512
EXPERT_COUNT = 8
HEAD = 64
FF = 2048
ROW_LENGTH = 1024
CAPACITY = 256
PAIRS = 4
ROW_COUNT = 32


def route_table(key):
    crowd_key, ranking_score_key = jax.random.split(jax.random.fold_in(key, 11))
    layer_keys = jax.random.split(crowd_key, 3)
    overfull_slots = jnp.stack([jax.random.permutation(layer_keys[index], EXPERT_COUNT)[:2] for index in range(3)])
    expert_choices = jnp.arange(EXPERT_COUNT, dtype=jnp.int32)
    extra_score = jnp.sum((expert_choices[None, None, :] == overfull_slots[:, :, None]).astype(jnp.int32), axis=1) * 30
    router_scores = jax.random.randint(ranking_score_key, (ROW_COUNT, 3, ROW_LENGTH, EXPERT_COUNT), 0, 100) + extra_score[None, :, None, :]
    router_scores = router_scores * EXPERT_COUNT + expert_choices
    return lax.top_k(router_scores, 2)[1].astype(jnp.int32)


def draw_routes(key, part):
    return route_table(key)


def draw_overflow(key, part):
    routes = route_table(key)
    hits = (routes[..., None] == jnp.arange(EXPERT_COUNT, dtype=jnp.int32)).astype(jnp.int32)
    flat_hits = hits.reshape(ROW_COUNT, 3, ROW_LENGTH * 2, EXPERT_COUNT)
    earlier = jnp.cumsum(flat_hits, axis=2) - flat_hits
    ranks = jnp.sum(earlier * flat_hits, axis=-1).reshape(ROW_COUNT, 3, ROW_LENGTH, 2)
    return (ranks >= CAPACITY).astype(jnp.int32)


def draw_pairs(key, part):
    cut_keys = jax.random.split(jax.random.fold_in(key, 23), ROW_COUNT * 2)
    cuts = jax.vmap(lambda one_key: jax.random.permutation(one_key, ROW_LENGTH - 1)[:PAIRS - 1] + 1)(cut_keys)
    cuts = cuts.reshape(ROW_COUNT, 2, PAIRS - 1)
    positions = jnp.arange(ROW_LENGTH, dtype=jnp.int32)
    return jnp.sum((positions[None, None, :, None] >= cuts[:, :, None, :]).astype(jnp.int32), axis=-1)


def block_scale(rng, dims, pieces, least, high):
    loudness = 1.0
    for axis_at, parts in pieces:
        heights = jax.random.uniform(jax.random.fold_in(jax.random.fold_in(rng, 6), axis_at), (parts,), jnp.float32, least / len(pieces), high / len(pieces))
        loudness = loudness * jnp.repeat(jnp.exp(heights), dims[axis_at] // parts).reshape((-1,) + (1,) * (len(dims) - 1 - axis_at))
    return loudness


def gaussian(key, dims, spread, most, cuts=(), held_as=jnp.bfloat16):
    drawn = spread * jax.random.normal(key, dims, jnp.float32)
    if cuts:
        drawn = drawn * block_scale(key, dims, cuts, -0.22, 0.18)
    return jnp.clip(drawn, -most, most).astype(held_as)


def setup_inputs(seed: int = 0) -> dict:
    streams_of = jax.random.split(jax.random.key(seed), 15)
    source = gaussian(streams_of[0], (ROW_COUNT, ROW_LENGTH, D), 1.0, 6.0, ((0, 32),))
    target = gaussian(streams_of[1], (ROW_COUNT, ROW_LENGTH, D), 1.0, 6.0, ((0, 32),))
    routes = draw_routes(jax.random.fold_in(streams_of[14], 71), 0)
    overflow = draw_overflow(jax.random.fold_in(streams_of[14], 71), 0)
    pairs = draw_pairs(jax.random.fold_in(streams_of[14], 71), 0)
    gains = jnp.clip(1.0 + 0.1 * jax.random.normal(streams_of[5], (5, D), jnp.float32), 0.5, 1.5)
    router = gaussian(streams_of[6], (3, D, EXPERT_COUNT), (0.7 * D ** -0.5), 0.4375)
    query = gaussian(streams_of[7], (3, D, EXPERT_COUNT * HEAD), D ** -0.5, 0.25)
    keyval = gaussian(streams_of[8], (3, D, 2 * HEAD), D ** -0.5, 0.25)
    output = gaussian(streams_of[9], (3, EXPERT_COUNT * HEAD, D), 1.0, 6.0)
    ffn_in = gaussian(streams_of[10], (2, D, FF), D ** -0.5, 0.25, ((2, 2),))
    ffn_out = gaussian(streams_of[11], (2, FF, D), FF ** -0.5, 0.125, ((1, 2),))
    cot_source = gaussian(streams_of[12], (ROW_COUNT, ROW_LENGTH, D), 1.0, 6.0, ((0, 32),))
    cot_target = gaussian(streams_of[13], (ROW_COUNT, ROW_LENGTH, D), 1.0, 6.0, ((0, 32),))
    return {"source": source, "target": target, "routes": routes, "overflow": overflow, "pairs": pairs, "gains": gains, "router": router, "query": query, "keyval": keyval, "output": output, "ffn_in": ffn_in, "ffn_out": ffn_out, "cot_source": cot_source, "cot_target": cot_target}


EPSILON = 1e-05
MASKED = -1000000000.0

@jax.custom_vjp
def low(v):
    return lax.optimization_barrier(v.astype(jnp.bfloat16)).astype(jnp.float32)

@jax.custom_vjp
def low_back(v):
    return v

def low_keep(v):
    return (low(v), None)

def low_pass(kept, grad):
    return (grad,)

def back_keep(v):
    return (v, None)

def back_low(kept, grad):
    return (low(grad),)
low.defvjp(low_keep, low_pass)
low_back.defvjp(back_keep, back_low)

def layer_norm(rows, gain):
    centered = rows - lax.optimization_barrier(jnp.mean(rows, axis=-1, keepdims=True))
    return centered * lax.rsqrt(lax.optimization_barrier(jnp.mean(centered * centered, axis=-1, keepdims=True)) + EPSILON) * gain

def routing_tables(routes, overflow, query_pairs):
    length = routes.shape[0]
    expert_choices = jnp.arange(EXPERT_COUNT, dtype=jnp.int32)
    hits = (routes[:, :, None] == expert_choices).astype(jnp.int32)
    flat_hits = hits.reshape(2 * length, EXPERT_COUNT)
    earlier = jnp.cumsum(flat_hits, axis=0) - flat_hits
    ranks = lax.optimization_barrier(jnp.sum(earlier * flat_hits, axis=1)).reshape(length, 2)
    slot_ids = jnp.arange(CAPACITY, dtype=jnp.int32)
    kept = overflow == 0

    def slot_hits(pick):
        return (routes[None, None, :, pick] == expert_choices[:, None, None]) & (ranks[None, None, :, pick] == slot_ids[None, :, None]) & kept[None, None, :, pick]
    matches = slot_hits(0) | slot_hits(1)
    positions = jnp.arange(length, dtype=jnp.int32)
    slot_token = lax.optimization_barrier(jnp.sum(jnp.where(matches, positions, 0), axis=-1)).astype(jnp.int32)
    slot_pairs = lax.optimization_barrier(jnp.sum(jnp.where(matches, query_pairs, 0), axis=-1)).astype(jnp.int32)
    valid = jnp.any(matches, axis=-1)
    return (hits, slot_token, slot_pairs, valid)

def allowed_keys(slot_token, slot_pairs, valid, key_pairs, causal):
    allowed = slot_pairs[:, :, None] == key_pairs[None, None, :]
    if causal:
        key_positions = jnp.arange(key_pairs.shape[0], dtype=jnp.int32)
        allowed = allowed & (key_positions[None, None, :] <= slot_token[:, :, None])
    return allowed | jnp.logical_not(valid)[:, :, None]

def attend(normed, source, routes, overflow, query_pairs, key_pairs, causal, router, query, keyval, output):
    length = normed.shape[0]
    scale = HEAD ** (-0.5)
    hits, slot_token, slot_pairs, valid = routing_tables(routes, overflow, query_pairs)
    logits = low_back(jnp.dot(normed, router, precision=lax.Precision.HIGHEST))
    gates = jax.nn.softmax(jnp.take_along_axis(logits, routes, axis=1), axis=-1)
    kept = (1 - overflow).astype(jnp.float32)
    token_weights = lax.optimization_barrier(jnp.sum((gates * kept)[:, :, None] * hits.astype(jnp.float32), axis=1))
    queries = low(low_back(jnp.dot(normed, query, precision=lax.Precision.HIGHEST))).reshape(length, EXPERT_COUNT, HEAD)
    expert_index = jnp.arange(EXPERT_COUNT, dtype=jnp.int32)[:, None]
    slot_queries = queries[slot_token, expert_index]
    keys_values = low(low_back(jnp.dot(source, keyval, precision=lax.Precision.HIGHEST)))
    allowed = allowed_keys(slot_token, slot_pairs, valid, key_pairs, causal)
    router_scores = jnp.einsum('ech,kh->eck', slot_queries, keys_values[:, :HEAD], precision=lax.Precision.HIGHEST) * scale
    router_scores = low_back(jnp.where(allowed, router_scores, MASKED))
    probs = jax.nn.softmax(router_scores, axis=-1)
    attended = low(low_back(jnp.einsum('eck,kh->ech', low(probs), keys_values[:, HEAD:], precision=lax.Precision.HIGHEST)))
    target_rows = jnp.where(valid, slot_token, length)
    token_heads = jnp.zeros((length + 1, EXPERT_COUNT, HEAD), jnp.float32).at[target_rows, expert_index].add(attended)[:length]
    projected = low_back(jnp.einsum('leh,ehd->led', token_heads, output.reshape(EXPERT_COUNT, HEAD, -1), precision=lax.Precision.HIGHEST))
    return lax.optimization_barrier(jnp.sum(token_weights[:, :, None] * projected, axis=1))

def feed_forward(normed, ffn_in, ffn_out):
    hidden_in = low_back(jnp.dot(normed, ffn_in, precision=lax.Precision.HIGHEST))
    hidden = low(jax.nn.gelu(hidden_in, approximate=False))
    return low_back(jnp.dot(hidden, ffn_out, precision=lax.Precision.HIGHEST))

def layers(source, target, routes, overflow, pairs, gains, router, query, keyval, output, ffn_in, ffn_out):

    def branch(index, normed, keys_from, query_side, key_side, causal):
        return attend(normed, keys_from, routes[index], overflow[index], pairs[query_side], pairs[key_side], causal, router[index], query[index], keyval[index], output[index])
    normed = low(layer_norm(source, gains[0]))
    hidden = source + branch(0, normed, normed, 0, 0, False)
    encoded = hidden + feed_forward(low(layer_norm(hidden, gains[1])), ffn_in[0], ffn_out[0])
    normed = low(layer_norm(target, gains[2]))
    decoded = target + branch(1, normed, normed, 1, 1, True)
    normed = low(layer_norm(decoded, gains[3]))
    decoded = decoded + branch(2, normed, low(encoded), 1, 0, False)
    decoded = decoded + feed_forward(low(layer_norm(decoded, gains[4])), ffn_in[1], ffn_out[1])
    return (encoded, decoded)

def reference(source, target, routes, overflow, pairs, gains, router, query, keyval, output, ffn_in, ffn_out, cot_source, cot_target):
    weights = tuple((item.astype(jnp.float32) for item in (gains, router, query, keyval, output, ffn_in, ffn_out)))

    def one_row(totals, items):
        source_row, target_row, route_row, over_row, pair_row, cot_first, cot_second = items

        def forward(source_in, target_in, *params):
            return layers(source_in, target_in, route_row, over_row, pair_row, *params)
        outputs, pullback = jax.vjp(forward, source_row.astype(jnp.float32), target_row.astype(jnp.float32), *weights)
        grads = pullback((cot_first.astype(jnp.float32), cot_second.astype(jnp.float32)))
        totals = tuple((total + piece for total, piece in zip(totals, grads[2:])))
        return (totals, (outputs[0].astype(jnp.bfloat16), outputs[1].astype(jnp.bfloat16), grads[0], grads[1]))
    zeros = tuple((jnp.zeros_like(item) for item in weights))
    totals, per_row = lax.scan(one_row, zeros, (source, target, routes, overflow, pairs, cot_source, cot_target))
    return (per_row[0], per_row[1], per_row[2], per_row[3], totals[0], totals[1], totals[2], totals[3], totals[4], totals[5], totals[6])
```

```python
import functools

import jax
import jax.numpy as jnp
from jax import lax
from jax.experimental import pallas as pl
from jax.experimental.pallas import tpu as pltpu
from jax.sharding import PartitionSpec as P

CAPACITY = 256
EPSILON = 1e-05
MASKED = -1000000000.0
PENALTY = -(2.0**30)
ROOT_HALF = 0.7071067811865476
INV_ROOT_TWO_PI = 0.3989422804014327
F32 = jnp.float32
BF16 = jnp.bfloat16
NN = ((1,), (0,))
NT = ((1,), (1,))
TN = ((0,), (0,))
CHUNK = 256
VMEM_LIMIT = 52 * 2**20


def mm(left, right, dims=NN):
    return lax.dot_general(left, right, (dims, ((), ())), preferred_element_type=F32)


def normalize(values):
    centered = values - jnp.mean(values, axis=0, keepdims=True)
    inverse = lax.rsqrt(jnp.mean(centered * centered, axis=0, keepdims=True) + EPSILON)
    return centered * inverse, inverse


def normalize_back(grad, normed, inverse, gain):
    scaled = normed.astype(F32) * (1.0 / gain)
    gain_grad = jnp.sum(grad * scaled, axis=1, keepdims=True)
    grad_scaled = grad * gain
    back = inverse * (
        grad_scaled
        - jnp.mean(grad_scaled, axis=0, keepdims=True)
        - scaled * jnp.mean(grad_scaled * scaled, axis=0, keepdims=True)
    )
    return back, gain_grad


def column_to_row(column):
    return jnp.broadcast_to(column, (column.shape[0], 128)).T[0:1]


def route_hits(codes_ref, layer, experts):
    length = codes_ref.shape[2]
    expert = lax.broadcasted_iota(jnp.int32, (experts, length), 0)
    hits, kept = [], []
    for pick in range(2):
        code = codes_ref[layer, pick : pick + 1, :]
        dropped = code >= experts
        route = jnp.where(dropped, code - experts, code)
        hits.append(jnp.where(expert == route, 1.0, 0.0))
        kept.append(jnp.where(dropped, 0.0, 1.0))
    return hits, kept


def prefix_before(values):
    length = values.shape[1]
    lane = lax.broadcasted_iota(jnp.int32, values.shape, 1)
    total = values
    step = 1
    while step < length:
        total = total + jnp.where(lane >= step, pltpu.roll(total, step, 1), 0.0)
        step *= 2
    return total - values


def slot_matrix(position_row):
    slot = lax.broadcasted_iota(jnp.int32, (CAPACITY, position_row.shape[1]), 0).astype(F32)
    return jnp.where(slot == position_row, 1.0, 0.0).astype(BF16)


def slot_matrix_t(position_column):
    slot = lax.broadcasted_iota(jnp.int32, (position_column.shape[0], CAPACITY), 1).astype(F32)
    return jnp.where(slot == position_column, 1.0, 0.0).astype(BF16)


def attend_forward_kernel(
    layer, causal, cross, from_rows, query_side, key_side, gain_at, *refs
):
    if cross:
        (v_ref, s_ref, gains_ref, codes_ref, pairs_ref, router_ref, query_ref, keyval_ref,
         output_ref, h_out, x_out, tables_out, e_out, linv_out, slots_out, heads_out, kv_out,
         e_buf, q_buf, hw_buf, sem) = refs
    else:
        (v_ref, gains_ref, codes_ref, pairs_ref, router_ref, query_ref, keyval_ref,
         output_ref, h_out, x_out, tables_out, e_out, linv_out, slots_out, heads_out, kv_out,
         e_buf, q_buf, hw_buf, sem) = refs
        s_ref = x_out
    width, length = x_out.shape
    experts = router_ref.shape[2]
    head = keyval_ref.shape[2] // 2
    gain = gains_ref[:, gain_at : gain_at + 1]
    inverses = []
    for at in range(0, length, CHUNK):
        cols = slice(at, at + CHUNK)
        part = v_ref[cols, :].astype(F32).T if from_rows else v_ref[:, cols]
        scaled, inverse = normalize(part)
        x_out[:, cols] = (scaled * gain).astype(BF16)
        inverses.append(inverse)
        if from_rows:
            h_out[:, cols] = part
    inverse = jnp.concatenate(inverses, axis=1)

    hits, kept = route_hits(codes_ref, layer, experts)
    rank = prefix_before(hits[0] + hits[1])
    placed = hits[0] * kept[0] + hits[1] * kept[1]
    position = jnp.where(placed > 0.0, rank, -1.0)
    position_t = position.T

    normed = x_out[...]
    logits = mm(router_ref[0], normed, TN)
    picked = [jnp.sum(hit * logits, axis=0, keepdims=True) for hit in hits]
    top = jnp.maximum(picked[0], picked[1])
    raised = [jnp.exp(item - top) for item in picked]
    total = raised[0] + raised[1]
    gates = [item / total for item in raised]
    weights = gates[0] * kept[0] * hits[0] + gates[1] * kept[1] * hits[1]
    tables_out[...] = jnp.concatenate(
        [position, weights, gates[0], gates[1], inverse, jnp.zeros((5, length), F32)], axis=0
    )

    q_buf[...] = (mm(query_ref[0], normed, TN) * (head**-0.5)).astype(BF16)
    kv = mm(keyval_ref[0], s_ref[...], TN).astype(BF16)
    kv_out[...] = kv
    values_t = kv[head:]
    row = lax.broadcasted_iota(jnp.int32, (head, length), 0)
    key_pair = pairs_ref[key_side : key_side + 1, :]
    penalties = jnp.where((row < 8) & (row != key_pair), PENALTY, 0.0)
    keys = jnp.concatenate([kv[:head].astype(F32), penalties], axis=0).T.astype(BF16)
    row = lax.broadcasted_iota(jnp.int32, (16, length), 0)
    token = lax.broadcasted_iota(jnp.int32, (16, length), 1)
    low = jnp.bitwise_and(token, 7)
    query_pair = pairs_ref[query_side : query_side + 1, :]
    extras = jnp.where(row < 8, jnp.where(row == query_pair, 1, 0), 0)
    extras = jnp.where(row == 8, token - low, extras)
    extras = jnp.where(row == 9, low, extras)
    extras = jnp.where(row == 10, 1, extras)
    extras = extras.astype(F32).astype(BF16)

    copies = []
    for e in range(experts):
        rows = slice(e * head, (e + 1) * head)
        placed_t = slot_matrix_t(position_t[:, e : e + 1])
        gathered = mm(jnp.concatenate([q_buf[rows], extras], axis=0), placed_t)
        slots = gathered.astype(BF16)
        slots_out[e, :head] = slots[:head]
        padded = jnp.concatenate(
            [slots, jnp.zeros((2 * head - slots.shape[0], CAPACITY), BF16)], axis=0
        )
        scores = mm(keys, padded)
        if causal:
            limit = (
                gathered[head + 8 : head + 9]
                + gathered[head + 9 : head + 10]
                + (1.0 - gathered[head + 10 : head + 11]) * length
            )
            key_at = lax.broadcasted_iota(jnp.int32, (length, CAPACITY), 0).astype(F32)
            scores = jnp.where(key_at <= limit, scores, MASKED)
        top = jnp.max(scores, axis=0, keepdims=True)
        exponent = jnp.exp(scores - top)
        linv = 1.0 / jnp.sum(exponent, axis=0, keepdims=True)
        linv_out[e : e + 1] = linv
        exponent = exponent.astype(BF16)
        e_buf[e] = exponent
        copies.append(pltpu.make_async_copy(e_buf.at[e], e_out.at[e], sem.at[e]))
        copies[-1].start()
        attended = (mm(values_t, exponent) * linv).astype(BF16)
        slots_out[e, head:] = attended
        placed_rows = slot_matrix(position[e : e + 1])
        heads = mm(attended, placed_rows)
        heads_out[rows] = heads.astype(BF16)
        hw_buf[rows] = (heads * weights[e : e + 1]).astype(BF16)
    branch = mm(output_ref[0], hw_buf[...], TN)
    if from_rows:
        h_out[...] += branch
    else:
        h_out[...] = v_ref[...] + branch
    for copy in copies:
        copy.wait()


def attend_backward_kernel(layer, cross, gain_at, *refs):
    if cross:
        (g_ref, x_ref, s_ref, gains_ref, codes_ref, tables_ref, linv_ref, slots_ref, heads_ref,
         kv_ref, router_ref, query_ref, keyval_ref, output_ref, e_in,
         g_out, s_out, packed_out, small_out, e_buf, gt_buf, gl_buf, d_buf, sem) = refs
    else:
        (g_ref, x_ref, gains_ref, codes_ref, tables_ref, linv_ref, slots_ref, heads_ref,
         kv_ref, router_ref, query_ref, keyval_ref, output_ref, e_in,
         g_out, packed_out, small_out, e_buf, gt_buf, gl_buf, d_buf, sem) = refs
        s_ref = x_ref
    width, length = x_ref.shape
    experts = router_ref.shape[2]
    head = keyval_ref.shape[2] // 2
    copies = []
    for e in range(experts):
        copies.append(pltpu.make_async_copy(e_in.at[e], e_buf.at[e], sem.at[e]))
        copies[-1].start()
    inner = experts * head
    hits, kept = route_hits(codes_ref, layer, experts)
    position = tables_ref[0:experts]
    weights = tables_ref[experts : 2 * experts]
    gates = [tables_ref[2 * experts + k : 2 * experts + k + 1] for k in range(2)]
    inverse = tables_ref[2 * experts + 2 : 2 * experts + 3]
    position_t = position.T

    gl_buf[...] = g_ref[...].astype(BF16)
    gt_buf[...] = mm(output_ref[0], gl_buf[...])
    keys_t = kv_ref[:head]
    values = kv_ref[head:].astype(F32).T.astype(BF16)
    weight_grads = []
    key_grad = jnp.zeros((head, length), F32)
    value_grad = jnp.zeros((head, length), F32)
    for e in range(experts):
        rows = slice(e * head, (e + 1) * head)
        back = gt_buf[rows]
        weight_grads.append(jnp.sum(back * heads_ref[rows].astype(F32), axis=0, keepdims=True))
        heads_grad = (back * weights[e : e + 1]).astype(BF16)
        placed_t = slot_matrix_t(position_t[:, e : e + 1])
        linv = linv_ref[e : e + 1]
        slot_grad = (mm(heads_grad, placed_t) * linv).astype(BF16)
        delta = jnp.sum(
            slot_grad.astype(F32) * slots_ref[e, head:].astype(F32), axis=0, keepdims=True
        )
        probs_grad = mm(values, slot_grad)
        copies[e].wait()
        exponent = e_buf[e]
        scores_grad = (exponent.astype(F32) * (probs_grad - delta)).astype(BF16)
        query_grad = (mm(keys_t, scores_grad) * (head**-0.5)).astype(BF16)
        placed_rows = slot_matrix(position[e : e + 1])
        d_buf[rows] = mm(query_grad, placed_rows).astype(BF16)
        key_grad = key_grad + mm(slots_ref[e, :head], scores_grad, NT)
        value_grad = value_grad + mm(slot_grad, exponent, NT)
    d_buf[inner : inner + head] = key_grad.astype(BF16)
    d_buf[inner + head : inner + 2 * head] = value_grad.astype(BF16)

    weight_grad = jnp.concatenate(weight_grads, axis=0)
    chosen = [
        jnp.sum(hit * weight_grad, axis=0, keepdims=True) * keep for hit, keep in zip(hits, kept)
    ]
    mean = gates[0] * chosen[0] + gates[1] * chosen[1]
    logit_grad = sum(
        gate * (item - mean) * hit for gate, item, hit in zip(gates, chosen, hits)
    ).astype(BF16)

    packed_out[:, :inner] = mm(x_ref[...], d_buf[:inner], NT).astype(BF16)
    for e in range(experts):
        rows = slice(e * head, (e + 1) * head)
        weighted = (heads_ref[rows].astype(F32) * weights[e : e + 1]).astype(BF16)
        heads_part = weighted
        packed_out[rows, inner : inner + width] = mm(heads_part, gl_buf[...], NT).astype(BF16)
    packed_out[:, inner + width :] = mm(s_ref[...], d_buf[inner:], NT).astype(BF16)
    router_grad = mm(logit_grad, x_ref[...], NT)

    grad = mm(query_ref[0], d_buf[:inner]) + mm(router_ref[0], logit_grad)
    source_grad = mm(keyval_ref[0], d_buf[inner:])
    if cross:
        s_out[...] = source_grad
    else:
        grad = grad + source_grad
    gain = gains_ref[:, gain_at : gain_at + 1]
    back, gain_grad = normalize_back(grad, x_ref[...], inverse, gain)
    small_out[...] = jnp.concatenate(
        [router_grad, column_to_row(gain_grad), jnp.zeros((7, width), F32)], axis=0
    )
    total = g_ref[...] + back
    if cross:
        g_out[...] = total
    else:
        g_out[...] = total.T


def gelu_parts(values):
    half = 0.5 * (1.0 + lax.erf(values * ROOT_HALF))
    slope = half + values * jnp.exp(-0.5 * values * values) * INV_ROOT_TWO_PI
    return values * half, slope


def hidden_chunks(own, other, axis):
    size = own.shape[axis]
    found = []
    for part, ref in enumerate((own, other)):
        for at in range(0, size, CHUNK):
            found.append(
                (part, slice(at, at + CHUNK), slice(part * size + at, part * size + at + CHUNK))
            )
    return found


def feed_forward_into(x, win_refs, wout_refs, hidden_ref, slope_ref):
    for part, here, there in hidden_chunks(win_refs[0], win_refs[1], 1):
        inner = mm(win_refs[part][:, here], x, TN)
        hidden, slope = gelu_parts(inner)
        hidden_ref[there] = hidden.astype(BF16)
        slope_ref[there] = slope.astype(BF16)
    size = wout_refs[0].shape[0]
    return mm(wout_refs[0][...], hidden_ref[:size], TN) + mm(
        wout_refs[1][...], hidden_ref[size:], TN
    )


def feed_backward_into(
    grad_low, grad_dims, x_ref, win_refs, wout_refs, hidden_ref, slope_ref, inner_ref, packed_refs
):
    width = x_ref.shape[0]
    size = wout_refs[0].shape[0]
    for part, here, there in hidden_chunks(win_refs[0], win_refs[1], 1):
        grad = mm(wout_refs[part][here, :], grad_low, NT if grad_dims else NN)
        inner = (grad * slope_ref[there].astype(F32)).astype(BF16)
        inner_ref[there] = inner
        packed = packed_refs[part]
        packed[:width, here] = mm(x_ref[...], inner, NT).astype(BF16)
        out_grad = mm(hidden_ref[there], grad_low, NN if grad_dims else NT).astype(BF16)
        fold = here.start // (size // 2)
        at = here.start - fold * (size // 2)
        packed[width + at : width + at + CHUNK, fold * width : (fold + 1) * width] = out_grad
    return mm(win_refs[0][...], inner_ref[:size]) + mm(win_refs[1][...], inner_ref[size:])


def feed_encoder_kernel(
    gain_at, h_ref, gains_ref, win_own, win_other, wout_own, wout_other,
    low_out, rows_out, x_out, inverse_out, hidden_out, slope_out,
):
    gain = gains_ref[:, gain_at : gain_at + 1]
    scaled, inverse = normalize(h_ref[...])
    x_out[...] = (scaled * gain).astype(BF16)
    inverse_out[...] = inverse
    result = feed_forward_into(
        x_out[...], (win_own, win_other), (wout_own, wout_other), hidden_out, slope_out
    )
    encoded = h_ref[...] + result
    low_out[...] = encoded.astype(BF16)
    rows_out[...] = encoded.T.astype(BF16)


def feed_encoder_back_kernel(
    gain_at, cot_ref, s_ref, gains_ref, x_ref, inverse_ref, hidden_ref, slope_ref,
    win_own, win_other, wout_own, wout_other,
    g_out, own_out, other_out, small_out, low_buf, inner_buf,
):
    gain = gains_ref[:, gain_at : gain_at + 1]
    g_out[...] = cot_ref[...].astype(F32).T + s_ref[...]
    low_buf[...] = g_out[...].astype(BF16)
    grad = feed_backward_into(
        low_buf[...], False, x_ref, (win_own, win_other), (wout_own, wout_other),
        hidden_ref, slope_ref, inner_buf, (own_out, other_out),
    )
    back, gain_grad = normalize_back(grad, x_ref[...], inverse_ref[...], gain)
    g_out[...] += back
    small_out[...] = jnp.broadcast_to(column_to_row(gain_grad), small_out.shape)


def feed_decoder_kernel(
    gain_at, h_ref, cot_ref, gains_ref, win_own, win_other, wout_own, wout_other,
    rows_out, g_out, own_out, other_out, small_out, x_buf, hidden_buf, slope_buf, inner_buf,
):
    gain = gains_ref[:, gain_at : gain_at + 1]
    scaled, inverse = normalize(h_ref[...])
    x_buf[...] = (scaled * gain).astype(BF16)
    result = feed_forward_into(
        x_buf[...], (win_own, win_other), (wout_own, wout_other), hidden_buf, slope_buf
    )
    rows_out[...] = (h_ref[...] + result).T.astype(BF16)
    grad = feed_backward_into(
        cot_ref[...], True, x_buf, (win_own, win_other), (wout_own, wout_other),
        hidden_buf, slope_buf, inner_buf, (own_out, other_out),
    )
    back, gain_grad = normalize_back(grad, x_buf[...], inverse, gain)
    g_out[...] = cot_ref[...].astype(F32).T + back
    small_out[...] = jnp.broadcast_to(column_to_row(gain_grad), small_out.shape)


WHOLE = pl.BlockSpec(memory_space=pltpu.VMEM)
LEFT = pl.BlockSpec(memory_space=pl.ANY)


def layer_spec(array, layer):
    shape = (1,) + array.shape[1:]
    return pl.BlockSpec(
        shape, lambda i: (layer,) + (0,) * (len(shape) - 1), pipeline_mode=pl.Buffered(1)
    )


def call(kernel, name, outs, args, in_specs, out_specs, scratch, flops):
    shapes = [jax.ShapeDtypeStruct(shape, dtype) for shape, dtype in outs]
    moved = sum(a.size * a.dtype.itemsize for a in args) + sum(
        s.size * s.dtype.itemsize for s in shapes
    )
    return pl.pallas_call(
        kernel,
        name=name,
        grid=(1,),
        out_shape=shapes,
        in_specs=in_specs,
        out_specs=out_specs,
        scratch_shapes=scratch,
        compiler_params=pltpu.CompilerParams(vmem_limit_bytes=VMEM_LIMIT),
        cost_estimate=pl.CostEstimate(flops=flops, bytes_accessed=moved, transcendentals=0),
    )(*args)


def body(
    source, target, routes, overflow, pairs, gains, router, query, keyval, output,
    ffn_in, ffn_out, cot_source, cot_target,
):
    _, length, width = source.shape
    experts = router.shape[2]
    head = keyval.shape[2] // 2
    inner = experts * head
    hidden = ffn_in.shape[2] * lax.axis_size("ffn")
    codes = jnp.transpose(routes[0] + experts * overflow[0], (0, 2, 1))
    pair_rows = pairs[0]
    gains_t = gains.T
    swap = [(0, 1), (1, 0)]
    win_other = lax.ppermute(ffn_in, "ffn", swap)
    wout_other = lax.ppermute(ffn_out, "ffn", swap)

    def layer_args(layer):
        arrays = (router, query, keyval, output)
        return arrays, [layer_spec(item, layer) for item in arrays]

    def attend(layer, gain_at, values, from_rows, keys, query_side, key_side, causal):
        cross = keys is not None
        weights, weight_specs = layer_args(layer)
        args = [values] + ([keys] if cross else []) + [gains_t, codes, pair_rows]
        outs = [
            ((width, length), F32),
            ((width, length), BF16),
            ((3 * experts, length), F32),
            ((experts, length, CAPACITY), BF16),
            ((experts, CAPACITY), F32),
            ((experts, 2 * head, CAPACITY), BF16),
            ((inner, length), BF16),
            ((2 * head, length), BF16),
        ]
        specs = [WHOLE] * len(outs)
        specs[3] = LEFT
        return call(
            functools.partial(
                attend_forward_kernel, layer, causal, cross, from_rows, query_side, key_side,
                gain_at,
            ),
            f"attend{layer}", outs, args + list(weights), [WHOLE] * len(args) + weight_specs, specs,
            [
                pltpu.VMEM((experts, length, CAPACITY), BF16),
                pltpu.VMEM((inner, length), BF16),
                pltpu.VMEM((inner, length), BF16),
                pltpu.SemaphoreType.DMA((experts,)),
            ],
            8 * 10**9,
        )

    def attend_back(layer, gain_at, grad, saved, keys):
        cross = keys is not None
        _, normed, tables, exponents, linv, slots, heads, kv = saved
        weights, weight_specs = layer_args(layer)
        args = (
            [grad, normed] + ([keys] if cross else [])
            + [gains_t, codes, tables, linv, slots, heads, kv]
        )
        outs = [((width, length) if cross else (length, width), F32)]
        outs += [((width, length), F32)] if cross else []
        outs += [((width, inner + width + 2 * head), BF16), ((2 * experts, width), F32)]
        return call(
            functools.partial(attend_backward_kernel, layer, cross, gain_at),
            f"attend_back{layer}", outs, args + list(weights) + [exponents],
            [WHOLE] * len(args) + weight_specs + [LEFT], [WHOLE] * len(outs),
            [
                pltpu.VMEM((experts, length, CAPACITY), BF16),
                pltpu.VMEM((inner, length), F32),
                pltpu.VMEM((width, length), BF16),
                pltpu.VMEM((inner + 2 * head, length), BF16),
                pltpu.SemaphoreType.DMA((experts,)),
            ],
            12 * 10**9,
        )

    def half_spec(array, index):
        return pl.BlockSpec(
            (None,) + array.shape[1:], lambda i: (index, 0, 0), pipeline_mode=pl.Buffered(1)
        )

    def ffn_args(index):
        arrays = [ffn_in, win_other, ffn_out, wout_other]
        return arrays, [half_spec(item, index) for item in arrays]

    packed_shape = (2 * width, hidden // 2)
    saved_a = attend(0, 0, source[0], True, None, 0, 0, False)
    saved_c = attend(1, 2, target[0], True, None, 1, 1, True)
    weights, weight_specs = ffn_args(0)
    encoded_low, encoded_rows, normed_b, inverse_b, hidden_b, slope_b = call(
        functools.partial(feed_encoder_kernel, 1), "feed_encoder",
        [
            ((width, length), BF16), ((length, width), BF16), ((width, length), BF16),
            ((1, length), F32), ((hidden, length), BF16), ((hidden, length), BF16),
        ],
        [saved_a[0], gains_t] + weights, [WHOLE] * 2 + weight_specs, [WHOLE] * 6, [], 5 * 10**9,
    )
    saved_d = attend(2, 3, saved_c[0], False, encoded_low, 1, 0, False)
    weights, weight_specs = ffn_args(1)
    decoded_rows, grad_e, own_e, other_e, small_e = call(
        functools.partial(feed_decoder_kernel, 4), "feed_decoder",
        [
            ((length, width), BF16), ((width, length), F32),
            (packed_shape, BF16), (packed_shape, BF16), ((8, width), F32),
        ],
        [saved_d[0], cot_target[0], gains_t] + weights, [WHOLE] * 3 + weight_specs, [WHOLE] * 5,
        [
            pltpu.VMEM((width, length), BF16), pltpu.VMEM((hidden, length), BF16),
            pltpu.VMEM((hidden, length), BF16), pltpu.VMEM((hidden, length), BF16),
        ],
        15 * 10**9,
    )
    grad_d, source_grad, packed_d, small_d = attend_back(2, 3, grad_e, saved_d, encoded_low)
    weights, weight_specs = ffn_args(0)
    grad_b, own_b, other_b, small_b = call(
        functools.partial(feed_encoder_back_kernel, 1), "feed_encoder_back",
        [
            ((width, length), F32), (packed_shape, BF16), (packed_shape, BF16), ((8, width), F32),
        ],
        [cot_source[0], source_grad, gains_t, normed_b, inverse_b, hidden_b, slope_b] + weights,
        [WHOLE] * 7 + weight_specs, [WHOLE] * 4,
        [pltpu.VMEM((width, length), BF16), pltpu.VMEM((hidden, length), BF16)],
        10 * 10**9,
    )
    grad_target, packed_c, small_c = attend_back(1, 2, grad_d, saved_c, None)
    grad_source, packed_a, small_a = attend_back(0, 0, grad_b, saved_a, None)

    def ffn_total(own, other):
        return reduce_all(own + lax.ppermute(other, "ffn", swap), ("batch",))

    def mixture_total(packed):
        return reduce_all(packed, ("ffn", "batch"))

    feed = [ffn_total(own_b, other_b), ffn_total(own_e, other_e)]
    mixture = [mixture_total(item) for item in (packed_a, packed_c, packed_d)]
    smalls = jnp.concatenate(
        [
            small_a[: experts], small_c[: experts], small_d[: experts],
            small_a[experts : experts + 1], small_b[:1], small_c[experts : experts + 1],
            small_d[experts : experts + 1], small_e[:1], jnp.zeros((3, width), F32),
        ],
        axis=0,
    )
    smalls = reduce_all(smalls, ("ffn", "batch"), scatter=False)
    wide = [item.astype(F32) for item in feed]
    grad_in = jnp.stack([item[:width] for item in wide])
    grad_out = jnp.stack(
        [jnp.concatenate([item[width:, :width], item[width:, width:]], axis=0) for item in wide]
    )
    stacked = jnp.stack(mixture).astype(F32)
    return (
        encoded_rows[None],
        decoded_rows[None],
        grad_source[None],
        grad_target[None],
        smalls[3 * experts : 3 * experts + 5],
        jnp.transpose(smalls[: 3 * experts].reshape(3, experts, width), (0, 2, 1)),
        stacked[:, :, :inner],
        stacked[:, :, inner + width :],
        stacked[:, :, inner : inner + width],
        grad_in,
        grad_out,
    )


def reduce_all(values, axes, scatter=True):
    steps = []
    for axis in axes:
        size = lax.axis_size(axis)
        bit = 1
        while bit < size:
            steps.append((axis, bit, [(i, i ^ bit) for i in range(size)]))
            bit *= 2
    if not scatter:
        for axis, bit, pairs in steps:
            values = values + lax.ppermute(values, axis, pairs)
        return values
    uppers = []
    for axis, bit, pairs in steps:
        upper = (lax.axis_index(axis) & bit) != 0
        half = values.shape[0] // 2
        low, high = values[:half], values[half:]
        keep = jnp.where(upper, high, low)
        send = jnp.where(upper, low, high)
        values = keep + lax.ppermute(send, axis, pairs)
        uppers.append(upper)
    for (axis, bit, pairs), upper in zip(reversed(steps), reversed(uppers)):
        other = lax.ppermute(values, axis, pairs)
        values = jnp.concatenate(
            [jnp.where(upper, other, values), jnp.where(upper, values, other)], axis=0
        )
    return values


def solution(mesh):
    tokens = P(("batch", "ffn"), None, None)
    return jax.shard_map(
        body,
        mesh=mesh,
        in_specs=(
            tokens, tokens, P(("batch", "ffn"), None, None, None),
            P(("batch", "ffn"), None, None, None), tokens,
            P(), P(), P(), P(), P(),
            P(None, None, "ffn"), P(None, "ffn", None), tokens, tokens,
        ),
        out_specs=(
            tokens, tokens, tokens, tokens,
            P(), P(), P(), P(), P(),
            P(None, None, "ffn"), P(None, "ffn", None),
        ),
        check_vma=False,
    )
```

```python
import functools

import jax
import jax.numpy as jnp
from jax import lax
from jax.experimental import pallas as pl
from jax.experimental.pallas import tpu as pltpu
from jax.sharding import PartitionSpec as P

CAPACITY = 256
EPSILON = 1e-05
MASKED = -1000000000.0
PENALTY = -(2.0**30)
ROOT_HALF = 0.7071067811865476
INV_ROOT_TWO_PI = 0.3989422804014327
F32 = jnp.float32
BF16 = jnp.bfloat16
NN = ((1,), (0,))
NT = ((1,), (1,))
TN = ((0,), (0,))
CHUNK = 256
VMEM_LIMIT = 52 * 2**20
MIDDLE_VMEM = 58 * 2**20


def mm(left, right, dims=NN):
    return lax.dot_general(left, right, (dims, ((), ())), preferred_element_type=F32)


def normalize(values):
    centered = values - jnp.mean(values, axis=0, keepdims=True)
    inverse = lax.rsqrt(jnp.mean(centered * centered, axis=0, keepdims=True) + EPSILON)
    return centered * inverse, inverse


def normalize_back(grad, normed, inverse, gain):
    scaled = normed.astype(F32) * (1.0 / gain)
    gain_grad = jnp.sum(grad * scaled, axis=1, keepdims=True)
    grad_scaled = grad * gain
    back = inverse * (
        grad_scaled
        - jnp.mean(grad_scaled, axis=0, keepdims=True)
        - scaled * jnp.mean(grad_scaled * scaled, axis=0, keepdims=True)
    )
    return back, gain_grad


def column_to_row(column):
    return jnp.broadcast_to(column, (column.shape[0], 128)).T[0:1]


def route_hits(codes_ref, layer, experts):
    length = codes_ref.shape[2]
    expert = lax.broadcasted_iota(jnp.int32, (experts, length), 0)
    hits, kept = [], []
    for pick in range(2):
        code = codes_ref[layer, pick : pick + 1, :]
        dropped = code >= experts
        route = jnp.where(dropped, code - experts, code)
        hits.append(jnp.where(expert == route, 1.0, 0.0))
        kept.append(jnp.where(dropped, 0.0, 1.0))
    return hits, kept


def prefix_before(values):
    length = values.shape[1]
    lane = lax.broadcasted_iota(jnp.int32, values.shape, 1)
    total = values
    step = 1
    while step < length:
        total = total + jnp.where(lane >= step, pltpu.roll(total, step, 1), 0.0)
        step *= 2
    return total - values


def slot_matrix(position_row):
    slot = lax.broadcasted_iota(jnp.int32, (CAPACITY, position_row.shape[1]), 0).astype(F32)
    return jnp.where(slot == position_row, 1.0, 0.0).astype(BF16)


def slot_matrix_t(position_column):
    slot = lax.broadcasted_iota(jnp.int32, (position_column.shape[0], CAPACITY), 1).astype(F32)
    return jnp.where(slot == position_column, 1.0, 0.0).astype(BF16)


def attend_forward_kernel(
    layer, causal, cross, from_rows, query_side, key_side, gain_at, *refs
):
    if cross:
        (v_ref, s_ref, gains_ref, codes_ref, pairs_ref, router_ref, query_ref, keyval_ref,
         output_ref, h_out, x_out, tables_out, e_out, linv_out, slots_out, heads_out, kv_out,
         e_buf, q_buf, hw_buf, sem) = refs
    else:
        (v_ref, gains_ref, codes_ref, pairs_ref, router_ref, query_ref, keyval_ref,
         output_ref, h_out, x_out, tables_out, e_out, linv_out, slots_out, heads_out, kv_out,
         e_buf, q_buf, hw_buf, sem) = refs
        s_ref = x_out
    width, length = x_out.shape
    experts = router_ref.shape[2]
    head = keyval_ref.shape[2] // 2
    gain = gains_ref[:, gain_at : gain_at + 1]
    inverses = []
    for at in range(0, length, CHUNK):
        cols = slice(at, at + CHUNK)
        part = v_ref[cols, :].astype(F32).T if from_rows else v_ref[:, cols]
        scaled, inverse = normalize(part)
        x_out[:, cols] = (scaled * gain).astype(BF16)
        inverses.append(inverse)
        if from_rows:
            h_out[:, cols] = part
    inverse = jnp.concatenate(inverses, axis=1)
    flush(x_out)

    hits, kept = route_hits(codes_ref, layer, experts)
    rank = prefix_before(hits[0] + hits[1])
    placed = hits[0] * kept[0] + hits[1] * kept[1]
    position = jnp.where(placed > 0.0, rank, -1.0)
    position_t = position.T

    normed = x_out[...]
    logits = mm(router_ref[0], normed, TN)
    picked = [jnp.sum(hit * logits, axis=0, keepdims=True) for hit in hits]
    top = jnp.maximum(picked[0], picked[1])
    raised = [jnp.exp(item - top) for item in picked]
    total = raised[0] + raised[1]
    gates = [item / total for item in raised]
    weights = gates[0] * kept[0] * hits[0] + gates[1] * kept[1] * hits[1]
    tables_out[...] = jnp.concatenate(
        [position, weights, gates[0], gates[1], inverse, jnp.zeros((5, length), F32)], axis=0
    )

    q_buf[...] = (mm(query_ref[0], normed, TN) * (head**-0.5)).astype(BF16)
    kv = mm(keyval_ref[0], s_ref[...], TN).astype(BF16)
    kv_out[...] = kv
    values_t = kv[head:]
    row = lax.broadcasted_iota(jnp.int32, (head, length), 0)
    key_pair = pairs_ref[key_side : key_side + 1, :]
    penalties = jnp.where((row < 8) & (row != key_pair), PENALTY, 0.0)
    keys = jnp.concatenate([kv[:head].astype(F32), penalties], axis=0).T.astype(BF16)
    row = lax.broadcasted_iota(jnp.int32, (16, length), 0)
    token = lax.broadcasted_iota(jnp.int32, (16, length), 1)
    low = jnp.bitwise_and(token, 7)
    query_pair = pairs_ref[query_side : query_side + 1, :]
    extras = jnp.where(row < 8, jnp.where(row == query_pair, 1, 0), 0)
    extras = jnp.where(row == 8, token - low, extras)
    extras = jnp.where(row == 9, low, extras)
    extras = jnp.where(row == 10, 1, extras)
    extras = extras.astype(F32).astype(BF16)

    copies = []

    def scores_of(e):
        rows = slice(e * head, (e + 1) * head)
        placed_t = slot_matrix_t(position_t[:, e : e + 1])
        gathered = mm(jnp.concatenate([q_buf[rows], extras], axis=0), placed_t)
        slots = gathered.astype(BF16)
        slots_out[e, :head] = slots[:head]
        padded = jnp.concatenate(
            [slots, jnp.zeros((2 * head - slots.shape[0], CAPACITY), BF16)], axis=0
        )
        scores = mm(keys, padded)
        if causal:
            limit = (
                gathered[head + 8 : head + 9]
                + gathered[head + 9 : head + 10]
                + (1.0 - gathered[head + 10 : head + 11]) * length
            )
            key_at = lax.broadcasted_iota(jnp.int32, (length, CAPACITY), 0).astype(F32)
            scores = jnp.where(key_at <= limit, scores, MASKED)
        return scores

    ahead = scores_of(0)
    for e in range(experts):
        rows = slice(e * head, (e + 1) * head)
        scores = ahead
        if e + 1 < experts:
            ahead = scores_of(e + 1)
        top = jnp.max(scores, axis=0, keepdims=True)
        exponent = jnp.exp(scores - top)
        linv = 1.0 / jnp.sum(exponent, axis=0, keepdims=True)
        linv_out[e : e + 1] = linv
        exponent = exponent.astype(BF16)
        e_buf[e] = exponent
        copies.append(pltpu.make_async_copy(e_buf.at[e], e_out.at[e], sem.at[e]))
        copies[-1].start()
        attended = (mm(values_t, exponent) * linv).astype(BF16)
        slots_out[e, head:] = attended
        placed_rows = slot_matrix(position[e : e + 1])
        heads = mm(attended, placed_rows)
        heads_out[rows] = heads.astype(BF16)
        hw_buf[rows] = (heads * weights[e : e + 1]).astype(BF16)
    flush(heads_out)
    flush(slots_out)
    for at in range(0, length, length // 2):
        cols = slice(at, at + length // 2)
        branch = mm(output_ref[0], hw_buf[:, cols], TN)
        h_out[:, cols] = (h_out if from_rows else v_ref)[:, cols] + branch
        flush(h_out, (slice(None), cols))
    for copy in copies:
        copy.wait()


def attend_backward_kernel(layer, cross, gain_at, first, last, *refs):
    refs = list(refs)
    take = lambda count: [refs.pop(0) for _ in range(count)]
    (g_ref, gains_ref, codes_ref, tables_ref, linv_ref, slots_ref, heads_ref, kv_ref, output_ref,
     e_in) = take(10)
    experts, head = slots_ref.shape[0], slots_ref.shape[1] // 2
    width, length = g_ref.shape
    inner = experts * head
    finish = last == experts
    if first:
        d_in, kv_grad_in, hits_in = take(3)
    if finish:
        (x_ref,) = take(1)
        s_ref = take(1)[0] if cross else x_ref
        router_ref, query_ref, keyval_ref, feed_gain_ref = take(4)
        if first:
            (packed_in,) = take(1)
        (g_out,) = take(1)
        if cross:
            (s_out,) = take(1)
        (packed_out,) = take(1)
    else:
        d_out, kv_grad_out, hits_out, packed_out = take(4)
    e_buf, gt_buf, gl_buf, d_buf, sem = refs
    copies = []
    for e in range(first, last):
        copies.append(pltpu.make_async_copy(e_in.at[e], e_buf.at[e - first], sem.at[e - first]))
        copies[-1].start()
    position = tables_ref[0:experts]
    weights = tables_ref[experts : 2 * experts]
    position_t = position.T
    mine = slice(first * head, last * head)

    gl_buf[...] = g_ref[...].astype(BF16)
    gt_buf[...] = mm(output_ref[0, mine, :], gl_buf[...])
    keys_t = kv_ref[:head]
    values = kv_ref[head:].astype(F32).T.astype(BF16)
    weight_grads = []
    if first:
        key_grad, value_grad = kv_grad_in[:head], kv_grad_in[head:]
        d_buf[: first * head] = d_in[...]
        weight_grads.append(hits_in[:first])
    else:
        key_grad = jnp.zeros((head, length), F32)
        value_grad = jnp.zeros((head, length), F32)
    def probs_grad_of(e):
        rows = slice(e * head, (e + 1) * head)
        back = gt_buf[(e - first) * head : (e - first + 1) * head]
        weight_grads.append(jnp.sum(back * heads_ref[rows].astype(F32), axis=0, keepdims=True))
        heads_grad = (back * weights[e : e + 1]).astype(BF16)
        placed_t = slot_matrix_t(position_t[:, e : e + 1])
        slot_grad = (mm(heads_grad, placed_t) * linv_ref[e : e + 1]).astype(BF16)
        delta = jnp.sum(
            slot_grad.astype(F32) * slots_ref[e, head:].astype(F32), axis=0, keepdims=True
        )
        return slot_grad, delta, mm(values, slot_grad)

    ahead = probs_grad_of(first)
    for e in range(first, last):
        slot_grad, delta, probs_grad = ahead
        if e + 1 < last:
            ahead = probs_grad_of(e + 1)
        copies[e - first].wait()
        exponent = e_buf[e - first]
        scores_grad = (exponent.astype(F32) * (probs_grad - delta)).astype(BF16)
        query_grad = (mm(keys_t, scores_grad) * (head**-0.5)).astype(BF16)
        rows = slice(e * head, (e + 1) * head)
        d_buf[rows] = mm(query_grad, slot_matrix(position[e : e + 1])).astype(BF16)
        key_grad = key_grad + mm(slots_ref[e, :head], scores_grad, NT)
        value_grad = value_grad + mm(slot_grad, exponent, NT)

    out_columns = slice(inner, inner + width)
    if finish and first:
        packed_out[: first * head, out_columns] = packed_in[...]
    for e in range(first, last):
        rows = slice(e * head, (e + 1) * head)
        weighted = (heads_ref[rows].astype(F32) * weights[e : e + 1]).astype(BF16)
        out_grad = mm(weighted, gl_buf[...], NT).astype(BF16)
        if finish:
            packed_out[rows, out_columns] = out_grad
        else:
            packed_out[rows] = out_grad
    weight_grad = jnp.concatenate(weight_grads, axis=0)
    if not finish:
        d_out[...] = d_buf[mine]
        kv_grad_out[:head] = key_grad
        kv_grad_out[head:] = value_grad
        hits_out[:last] = weight_grad
        hits_out[last:] = jnp.zeros((experts - last, length), F32)
        return

    d_buf[inner : inner + head] = key_grad.astype(BF16)
    d_buf[inner + head : inner + 2 * head] = value_grad.astype(BF16)
    hits, kept = route_hits(codes_ref, layer, experts)
    gates = [tables_ref[2 * experts + k : 2 * experts + k + 1] for k in range(2)]
    inverse = tables_ref[2 * experts + 2 : 2 * experts + 3]
    chosen = [
        jnp.sum(hit * weight_grad, axis=0, keepdims=True) * keep for hit, keep in zip(hits, kept)
    ]
    mean = gates[0] * chosen[0] + gates[1] * chosen[1]
    logit_grad = sum(
        gate * (item - mean) * hit for gate, item, hit in zip(gates, chosen, hits)
    ).astype(BF16)

    packed_out[:, :inner] = mm(x_ref[...], d_buf[:inner], NT).astype(BF16)
    kv_columns = slice(inner + width, inner + width + 2 * head)
    packed_out[:, kv_columns] = mm(s_ref[...], d_buf[inner:], NT).astype(BF16)
    padded = jnp.concatenate([logit_grad.astype(F32), jnp.zeros((120, length), F32)], axis=0)
    router_grad = mm(x_ref[...], padded.astype(BF16), NT)
    flush(packed_out, (slice(None), slice(0, kv_columns.stop)))

    grad = mm(query_ref[0], d_buf[:inner]) + mm(router_ref[0], logit_grad)
    source_grad = mm(keyval_ref[0], d_buf[inner:])
    if cross:
        s_out[...] = source_grad
        flush(s_out)
    else:
        grad = grad + source_grad
    gain = gains_ref[:, gain_at : gain_at + 1]
    back, gain_grad = normalize_back(grad, x_ref[...], inverse, gain)
    lane = lax.broadcasted_iota(jnp.int32, router_grad.shape, 1)
    extra = jnp.where(lane == experts, gain_grad, router_grad)
    extra = jnp.where(lane == experts + 1, feed_gain_ref[:, 0:1], extra)
    packed_out[:, kv_columns.stop :] = extra.astype(BF16)
    flush(packed_out, (slice(None), slice(kv_columns.stop, packed_out.shape[1])))
    total = g_ref[...] + back
    if cross:
        g_out[...] = total
    else:
        g_out[...] = total.T


def gelu_parts(values):
    half = 0.5 * (1.0 + lax.erf(values * ROOT_HALF))
    slope = half + values * jnp.exp(-0.5 * values * values) * INV_ROOT_TWO_PI
    return values * half, slope


def hidden_chunks(own, other, axis):
    size = own.shape[axis]
    found = []
    for part, ref in enumerate((own, other)):
        for at in range(0, size, CHUNK):
            found.append(
                (part, slice(at, at + CHUNK), slice(part * size + at, part * size + at + CHUNK))
            )
    return found


def feed_weight_grads(
    grad_low, by_rows, x_ref, wout_refs, hidden_ref, slope_ref, inner_ref, packed_refs
):
    width = x_ref.shape[0]
    size = wout_refs[0].shape[0]
    for part, here, there in reversed(hidden_chunks(wout_refs[0], wout_refs[1], 0)):
        grad = mm(wout_refs[part][here, :], grad_low, NT if by_rows else NN)
        inner = (grad * slope_ref[there].astype(F32)).astype(BF16)
        inner_ref[there] = inner
        packed = packed_refs[part]
        packed[:width, here] = mm(x_ref[...], inner, NT).astype(BF16)
        out_grad = mm(hidden_ref[there], grad_low, NN if by_rows else NT).astype(BF16)
        fold = here.start // (size // 2)
        at = width + here.start - fold * (size // 2)
        packed[at : at + CHUNK, fold * width : (fold + 1) * width] = out_grad
        flush(inner_ref, there)
        if here.start == 0:
            flush(packed)


def feed_rows_grad(win_refs, inner_ref):
    size = win_refs[0].shape[1]
    return mm(win_refs[0][...], inner_ref[:size]) + mm(win_refs[1][...], inner_ref[size:])


def feed_hidden(x, win_refs, hidden_ref, slope_ref):
    for part, here, there in hidden_chunks(win_refs[0], win_refs[1], 1):
        hidden, slope = gelu_parts(mm(win_refs[part][:, here], x, TN))
        hidden_ref[there] = hidden.astype(BF16)
        slope_ref[there] = slope.astype(BF16)
        flush(hidden_ref, there)
        flush(slope_ref, there)


def feed_result(wout_refs, hidden_ref):
    size = wout_refs[0].shape[0]
    return mm(wout_refs[0][...], hidden_ref[:size], TN) + mm(
        wout_refs[1][...], hidden_ref[size:], TN
    )


def feed_encoder_kernel(
    gain_at, h_ref, gains_ref, win_own, win_other, wout_own, wout_other,
    low_out, rows_out, x_out, inverse_out, hidden_out, slope_out,
):
    gain = gains_ref[:, gain_at : gain_at + 1]
    scaled, inverse = normalize(h_ref[...])
    x_out[...] = (scaled * gain).astype(BF16)
    inverse_out[...] = inverse
    flush(x_out)
    feed_hidden(x_out[...], (win_own, win_other), hidden_out, slope_out)
    encoded = h_ref[...] + feed_result((wout_own, wout_other), hidden_out)
    low_out[...] = encoded.astype(BF16)
    rows_out[...] = encoded.T.astype(BF16)


def feed_encoder_weights_kernel(
    cot_ref, s_ref, x_ref, hidden_ref, slope_ref, wout_own, wout_other,
    g_out, inner_out, own_out, other_out, low_buf,
):
    g_out[...] = cot_ref[...].astype(F32).T + s_ref[...]
    low_buf[...] = g_out[...].astype(BF16)
    flush(g_out)
    feed_weight_grads(
        low_buf[...], False, x_ref, (wout_own, wout_other), hidden_ref, slope_ref, inner_out,
        (own_out, other_out),
    )


def feed_encoder_rows_kernel(
    gain_at, g_ref, gains_ref, x_ref, inverse_ref, inner_ref, win_own, win_other,
    g_out, gain_out,
):
    gain = gains_ref[:, gain_at : gain_at + 1]
    grad = feed_rows_grad((win_own, win_other), inner_ref)
    back, gain_grad = normalize_back(grad, x_ref[...], inverse_ref[...], gain)
    g_out[...] = g_ref[...] + back
    gain_out[...] = jnp.broadcast_to(gain_grad, gain_out.shape)


def feed_decoder_weights_kernel(
    gain_at, h_ref, cot_ref, gains_ref, win_own, win_other, wout_own, wout_other,
    x_out, inverse_out, hidden_out, inner_out, own_out, other_out, slope_buf,
):
    gain = gains_ref[:, gain_at : gain_at + 1]
    scaled, inverse = normalize(h_ref[...])
    x_out[...] = (scaled * gain).astype(BF16)
    inverse_out[...] = inverse
    flush(x_out)
    feed_hidden(x_out[...], (win_own, win_other), hidden_out, slope_buf)
    feed_weight_grads(
        cot_ref[...], True, x_out, (wout_own, wout_other), hidden_out, slope_buf, inner_out,
        (own_out, other_out),
    )


def feed_decoder_rows_kernel(
    gain_at, cot_ref, gains_ref, x_ref, inverse_ref, inner_ref, win_own, win_other,
    g_out, gain_out,
):
    gain = gains_ref[:, gain_at : gain_at + 1]
    grad = feed_rows_grad((win_own, win_other), inner_ref)
    back, gain_grad = normalize_back(grad, x_ref[...], inverse_ref[...], gain)
    g_out[...] = cot_ref[...].astype(F32).T + back
    gain_out[...] = jnp.broadcast_to(gain_grad, gain_out.shape)


def feed_decoder_result_kernel(h_ref, hidden_ref, wout_own, wout_other, rows_out):
    result = h_ref[...] + feed_result((wout_own, wout_other), hidden_ref)
    rows_out[...] = result.T.astype(BF16)


def first_kernel(parts, *refs):
    refs = list(refs)
    take = lambda count: [refs.pop(0) for _ in range(count)]
    gains, codes, pairs = take(3)
    given = [take(5) for _ in parts]
    made = [take(8) for _ in parts]
    held = [take(4) for _ in parts]
    for part, ins, outs, scratch in zip(parts, given, made, held):
        attend_forward_kernel(*part, ins[0], gains, codes, pairs, *ins[1:], *outs, *scratch)


def middle_kernel(part, gain_b, gain_e, *refs):
    refs = list(refs)
    take = lambda count: [refs.pop(0) for _ in range(count)]
    gains, codes, pairs, h_ref, d_ref, cot_ref = take(6)
    mixture, feed_b, feed_e = take(4), take(4), take(4)
    encoder, cross = take(6), take(8)
    hidden_out, own_out, other_out, g_out, gain_out = take(5)
    held = take(4)
    x_buf, inverse_buf = refs
    feed_encoder_kernel(gain_b, h_ref, gains, *feed_b, *encoder)
    attend_forward_kernel(
        *part, d_ref, encoder[0], gains, codes, pairs, *mixture, *cross, *held
    )
    for ref in encoder[4:]:
        ref.finish()
    inner_buf, slope_buf = [ref.buffer for ref in encoder[4:]]
    feed_decoder_weights_kernel(
        gain_e, cross[0], cot_ref, gains, *feed_e,
        x_buf, inverse_buf, hidden_out, inner_buf, own_out, other_out, slope_buf,
    )
    feed_decoder_rows_kernel(
        gain_e, cot_ref, gains, x_buf, inverse_buf, inner_buf, *feed_e[:2], g_out, gain_out
    )


def feed_encoder_back_kernel(
    gain_at, cot_ref, s_ref, gains_ref, x_ref, inverse_ref, hidden_ref, slope_ref,
    wout_own, wout_other, win_own, win_other,
    g_out, own_out, other_out, gain_out, low_buf, g_buf, inner_buf,
):
    feed_encoder_weights_kernel(
        cot_ref, s_ref, x_ref, hidden_ref, slope_ref, wout_own, wout_other,
        g_buf, inner_buf, own_out, other_out, low_buf,
    )
    feed_encoder_rows_kernel(
        gain_at, g_buf, gains_ref, x_ref, inverse_ref, inner_buf, win_own, win_other,
        g_out, gain_out,
    )


def unpack_feed_kernel(pieces, place_ref, *refs):
    in_out, out_out, packed_ref = refs[-3:]
    width = in_out.shape[0]
    size = packed_ref.shape[0] // pieces
    packed_ref[: packed_ref.shape[0] // 2] = refs[0][0]
    packed_ref[packed_ref.shape[0] // 2 :] = refs[1][0]
    for piece in range(pieces):
        at = pl.multiple_of(jnp.bitwise_xor(place_ref[0], piece) * size, size)
        rows = packed_ref[pl.ds(at, size), :].astype(F32)
        if piece * size < width:
            in_out[piece * size : (piece + 1) * size] = rows
        else:
            at = piece * size - width
            out_out[at : at + size] = rows[:, :width]
            out_out[width + at : width + at + size] = rows[:, width:]


def unpack_mixture_kernel(pieces, place_ref, low_ref, high_ref, *refs):
    query_out, output_out, keyval_out, router_out, gains_out, extra, packed_ref = refs[-7:]
    size = packed_ref.shape[0] // pieces
    packed_ref[: packed_ref.shape[0] // 2] = low_ref[0]
    packed_ref[packed_ref.shape[0] // 2 :] = high_ref[0]
    inner, width = query_out.shape[1], output_out.shape[1]
    end = inner + width + keyval_out.shape[1]
    experts = router_out.shape[1]
    for piece in range(pieces):
        position = jnp.bitwise_xor(place_ref[0], piece)
        crossed = jnp.where(position >= pieces // 2, place_ref[1], 0)
        at = pl.multiple_of(jnp.bitwise_xor(position, crossed) * size, size)
        rows = packed_ref[pl.ds(at, size), :].astype(F32)
        there = slice(piece * size, (piece + 1) * size)
        query_out[there] = rows[:, :inner]
        output_out[there] = rows[:, inner : inner + width]
        keyval_out[there] = rows[:, inner + width : end]
        extra[there] = rows[:, end:]
    router_out[...] = extra[:, :experts]
    gains_out[...] = extra[...].T[experts : experts + 8]


LEFT = "left"
WHOLE = "whole"
LARGE = 2**17


class Fetched:
    def __init__(self, source, buffer, sem):
        self.copy = pltpu.make_async_copy(source, buffer, sem)
        self.copy.start()
        self.buffer, self.shape, self.waits = buffer, buffer.shape, True

    def ready(self):
        if self.waits:
            self.copy.wait()
            self.waits = False
        return self.buffer

    def __getitem__(self, at):
        return self.ready()[at]


class Stored:
    def __init__(self, place, buffer, sems):
        self.place, self.buffer, self.sems = place, buffer, sems
        self.shape = buffer.shape
        self.copies = []
        self.finished = False

    def __getitem__(self, at):
        return self.buffer[at]

    def __setitem__(self, at, value):
        self.buffer[at] = value

    def flush(self, at=None):
        source, place = self.buffer, self.place
        if at is not None:
            source, place = source.at[at], place.at[at]
        self.copies.append(pltpu.make_async_copy(source, place, self.sems.at[len(self.copies)]))
        self.copies[-1].start()

    def finish(self):
        if self.finished:
            return
        if not self.copies:
            self.flush()
        for copy in self.copies:
            copy.wait()
        self.finished = True


def flush(ref, at=None):
    if isinstance(ref, Stored):
        ref.flush(at)


FLUSHES = 8


def layer_spec(array, layer):
    return (layer, True)


def call(kernel, name, outs, args, in_specs, out_specs, scratch, flops, limit=VMEM_LIMIT):
    shapes = [jax.ShapeDtypeStruct(shape, dtype) for shape, dtype in outs]
    ins, buffers = [], []
    for item, spec in zip(args, in_specs):
        shape = item.shape
        if isinstance(spec, tuple):
            shape = ((1,) if spec[1] else ()) + item.shape[1:]
        size = item.dtype.itemsize
        for extent in shape:
            size *= extent
        mine = isinstance(spec, tuple) or (spec == WHOLE and size >= LARGE)
        ins.append(spec if mine else None)
        if mine:
            buffers.append(pltpu.VMEM(shape, item.dtype))
    stored = [
        spec == WHOLE and item.size * item.dtype.itemsize >= LARGE
        for item, spec in zip(shapes, out_specs)
    ]
    buffers += [pltpu.VMEM(item.shape, item.dtype) for item, mine in zip(shapes, stored) if mine]
    count = len(buffers)
    fetched = sum(item is not None for item in ins)

    def wrapped(*refs):
        refs = list(refs)
        given, made = refs[: len(ins)], refs[len(ins) : len(ins) + len(shapes)]
        rest = refs[len(ins) + len(shapes) :]
        own, held, sems_in, sems_out = rest[: len(scratch)], rest[len(scratch) : -2], rest[-2], rest[-1]
        used = 0
        for k, spec in enumerate(ins):
            if spec is not None:
                source = given[k]
                if isinstance(spec, tuple):
                    source = source.at[pl.ds(spec[0], 1)] if spec[1] else source.at[spec[0]]
                given[k] = Fetched(source, held[used], sems_in.at[used])
                used += 1
        for k, mine in enumerate(stored):
            if mine:
                made[k] = Stored(made[k], held[used], sems_out.at[used - fetched])
                used += 1
        kernel(*given, *made, *own)
        for item in given:
            if isinstance(item, Fetched):
                item.ready()
        for item in made:
            if isinstance(item, Stored):
                item.finish()

    moved = sum(a.size * a.dtype.itemsize for a in args) + sum(
        s.size * s.dtype.itemsize for s in shapes
    )
    vmem, hbm = pl.BlockSpec(memory_space=pltpu.VMEM), pl.BlockSpec(memory_space=pl.ANY)
    return pl.pallas_call(
        wrapped,
        name=name,
        out_shape=shapes,
        in_specs=[hbm if k is not None or s == LEFT else vmem for k, s in zip(ins, in_specs)],
        out_specs=[hbm if k or s == LEFT else vmem for k, s in zip(stored, out_specs)],
        scratch_shapes=list(scratch) + buffers + [
            pltpu.SemaphoreType.DMA((max(fetched, 1),)),
            pltpu.SemaphoreType.DMA((max(count - fetched, 1), FLUSHES)),
        ],
        compiler_params=pltpu.CompilerParams(vmem_limit_bytes=limit),
        cost_estimate=pl.CostEstimate(flops=30 * flops, bytes_accessed=moved, transcendentals=0),
    )(*args)


def body(
    source, target, routes, overflow, pairs, gains, router, query, keyval, output,
    ffn_in, ffn_out, cot_source, cot_target,
):
    _, length, width = source.shape
    experts = router.shape[2]
    head = keyval.shape[2] // 2
    inner = experts * head
    hidden = ffn_in.shape[2] * lax.axis_size("ffn")
    codes = jnp.transpose(routes[0] + experts * overflow[0], (0, 2, 1))
    pair_rows = pairs[0]
    gains_t = gains.T
    swap = [(0, 1), (1, 0)]
    win_other = lax.ppermute(ffn_in, "ffn", swap)
    wout_other = lax.ppermute(ffn_out, "ffn", swap)

    def layer_args(layer):
        arrays = (router, query, keyval, output)
        return arrays, [layer_spec(item, layer) for item in arrays]

    attend_outs = [
        ((width, length), F32),
        ((width, length), BF16),
        ((3 * experts, length), F32),
        ((experts, length, CAPACITY), BF16),
        ((experts, CAPACITY), F32),
        ((experts, 2 * head, CAPACITY), BF16),
        ((inner, length), BF16),
        ((2 * head, length), BF16),
    ]
    attend_specs = [WHOLE] * 3 + [LEFT] + [WHOLE] * 4
    attend_scratch = [
        pltpu.VMEM((experts, length, CAPACITY), BF16),
        pltpu.VMEM((inner, length), BF16),
        pltpu.VMEM((inner, length), BF16),
        pltpu.SemaphoreType.DMA((experts,)),
    ]

    def attend_back(layer, gain_at, grad, saved, keys, feed_gain):
        cross = keys is not None
        _, normed, tables, exponents, linv, slots, heads, kv = saved
        arrays, specs = layer_args(layer)
        args = [grad, gains_t, codes, tables, linv, slots, heads, kv, output, exponents, normed]
        args += ([keys] if cross else []) + list(arrays[:3]) + [feed_gain]
        arg_specs = [WHOLE] * 8 + [specs[3], LEFT] + [WHOLE] * (2 if cross else 1)
        arg_specs += specs[:3] + [WHOLE]
        outs = [((width, length) if cross else (length, width), F32)]
        outs += [((width, length), F32)] if cross else []
        outs += [((width, inner + width + 2 * head + 128), BF16)]
        return call(
            functools.partial(attend_backward_kernel, layer, cross, gain_at, 0, experts),
            f"attend_back{layer}", outs, args, arg_specs, [WHOLE] * len(outs),
            [
                pltpu.VMEM((experts, length, CAPACITY), BF16),
                pltpu.VMEM((inner, length), F32),
                pltpu.VMEM((width, length), BF16),
                pltpu.VMEM((inner + 2 * head, length), BF16),
                pltpu.SemaphoreType.DMA((experts,)),
            ],
            13 * 10**9,
        )

    def half_spec(array, index):
        return (index, False)

    def ffn_args(index):
        arrays = [ffn_in, win_other, ffn_out, wout_other]
        return arrays, [half_spec(item, index) for item in arrays]

    travelling = []

    def boundary(values):
        going = [(item, item.work()) for item in travelling]
        going = [(item, work) for item, work in going if work is not None]
        works = [work for _, work in going if work[1]]
        made = fold(works) if works else []
        ended = [item for item in travelling if item.work() is None and not item.ended]
        brought = [item.inputs for item in ended]
        values, made, brought = lax.optimization_barrier((values, made, brought))
        for item, item.inputs in zip(ended, brought):
            item.ended = True
        for item, work in going:
            item.send(made.pop(0) if work[1] else None)
        return values, not all(item.ended for item in travelling)

    last_made = []

    def event(values, items):
        going = [(item, item.work()) for item in items if item.work() is not None]
        works = [work for _, work in going]
        ended = [item for item in items if item.work() is None and not item.ended]
        tied = (values, [work[1] for work in works], [item.inputs for item in ended], last_made)
        values, inputs, brought, _ = lax.optimization_barrier(tied)
        for item, item.inputs in zip(ended, brought):
            item.ended = True
        if works:
            made = fold([(work[0], given, work[2]) for work, given in zip(works, inputs)])
            last_made[:] = [arrays[0] for arrays in made]
            for (item, _), arrays in zip(going, made):
                item.send(arrays)
        return values

    packed_shape = (2 * width, hidden // 2)
    common = [gains_t, codes, pair_rows]
    layers = [layer_args(layer) for layer in range(3)]
    parts = [(0, False, False, True, 0, 0, 0), (1, True, False, True, 1, 1, 2)]
    saved = call(
        functools.partial(first_kernel, parts), "attend_self", attend_outs * 2,
        common + [source[0], *layers[0][0], target[0], *layers[1][0]],
        [WHOLE] * 3 + [WHOLE, *layers[0][1], WHOLE, *layers[1][1]],
        attend_specs * 2, attend_scratch * 2, 16 * 10**9,
    )
    saved_a, saved_c = saved[:8], saved[8:]
    feed_args = [ffn_args(0), ffn_args(1)]
    made = call(
        functools.partial(middle_kernel, (2, False, True, False, 1, 0, 3), 1, 4), "middle",
        [
            ((width, length), BF16), ((length, width), BF16), ((width, length), BF16),
            ((1, length), F32), ((hidden, length), BF16), ((hidden, length), BF16),
        ] + attend_outs + [
            ((hidden, length), BF16), (packed_shape, BF16), (packed_shape, BF16),
            ((width, length), F32), ((width, 128), F32),
        ],
        common + [saved_a[0], saved_c[0], cot_target[0], *layers[2][0]]
        + feed_args[0][0] + feed_args[1][0],
        [WHOLE] * 6 + layers[2][1] + feed_args[0][1] + feed_args[1][1],
        [WHOLE] * 6 + attend_specs + [WHOLE] * 5,
        attend_scratch + [pltpu.VMEM((width, length), BF16), pltpu.VMEM((1, length), F32)],
        28 * 10**9, MIDDLE_VMEM,
    )
    encoded_low, encoded_rows, normed_b, inverse_b, hidden_b, slope_b = made[:6]
    saved_d = made[6:14]
    hidden_e, own_e, other_e, grad_e, gain_e = made[14:]
    feed_e = Exchange([own_e[None]], other_e[None], 3)
    travelling.append(feed_e)
    grad_e, _ = boundary(grad_e)
    grad_d, source_grad, packed_d = attend_back(2, 3, grad_e, saved_d, encoded_low, gain_e)
    source_grad, _ = boundary(source_grad)
    weights, weight_specs = feed_args[0]
    grad_b, own_b, other_b, gain_b = call(
        functools.partial(feed_encoder_back_kernel, 1), "feed_encoder_back",
        [((width, length), F32), (packed_shape, BF16), (packed_shape, BF16), ((width, 128), F32)],
        [cot_source[0], source_grad, gains_t, normed_b, inverse_b, hidden_b, slope_b]
        + weights[2:] + weights[:2],
        [WHOLE] * 7 + weight_specs[2:] + weight_specs[:2], [WHOLE] * 4,
        [
            pltpu.VMEM((width, length), BF16), pltpu.VMEM((width, length), F32),
            pltpu.VMEM((hidden, length), BF16),
        ],
        10 * 10**9,
    )
    feed_b = Exchange([own_b[None]], other_b[None], 3)
    travelling.append(feed_b)
    (grad_d, grad_b), _ = boundary((grad_d, grad_b))
    grad_target, packed_c = attend_back(1, 2, grad_d, saved_c, None, gain_b)
    mixture_dc = Exchange([packed_c[None], packed_d[None]], scattered=3)
    travelling.append(mixture_dc)
    grad_b, _ = boundary(grad_b)
    grad_source, packed_a = attend_back(0, 0, grad_b, saved_a, None, gain_b)
    mixture_a = Exchange([packed_a[None]], scattered=3)
    travelling.append(mixture_a)
    hidden_e, _ = boundary(hidden_e)
    (decoded_rows,) = call(
        feed_decoder_result_kernel, "feed_decoder_result", [((length, width), BF16)],
        [saved_d[0], hidden_e] + ffn_args(1)[0][2:], [WHOLE] * 2 + ffn_args(1)[1][2:], [WHOLE], [],
        3 * 10**9,
    )

    def unpack_feed(exchange, index, made):
        pieces = exchange.pieces
        shapes = [
            jax.ShapeDtypeStruct((2,) + item.shape[1:], F32) for item in (ffn_in, ffn_out)
        ]
        spec = lambda item: pl.BlockSpec(
            (None,) + item.shape[1:], lambda i: (index, 0, 0), pipeline_mode=pl.Buffered(1)
        )
        return pl.pallas_call(
            functools.partial(unpack_feed_kernel, pieces), name="unpack_feed", grid=(1,),
            out_shape=shapes,
            in_specs=[pl.BlockSpec(memory_space=pltpu.SMEM)] + [pl.BlockSpec(memory_space=pltpu.VMEM)] * 2
            + [pl.BlockSpec(memory_space=pl.ANY)] * len(made),
            out_specs=[spec(item) for item in shapes],
            scratch_shapes=[pltpu.VMEM(packed_shape, BF16)],
            input_output_aliases={3 + k: k for k in range(len(made))},
            compiler_params=pltpu.CompilerParams(vmem_limit_bytes=VMEM_LIMIT),
        )(exchange.place, *exchange.inputs, *made)

    def unpack_mixture(exchange, first, made):
        layers = exchange.inputs[0].shape[0]
        columns = (inner, width, 2 * head, experts)
        shapes = [jax.ShapeDtypeStruct((3, width, size), F32) for size in columns]
        shapes.append(jax.ShapeDtypeStruct((3, 8, width), F32))
        return pl.pallas_call(
            functools.partial(unpack_mixture_kernel, exchange.pieces), name="unpack_mixture",
            grid=(layers,),
            out_shape=shapes,
            in_specs=[
                pl.BlockSpec(memory_space=pltpu.SMEM),
            ] + [
                pl.BlockSpec((1,) + item.shape[1:], lambda i: (i, 0, 0)) for item in exchange.inputs
            ] + [pl.BlockSpec(memory_space=pl.ANY)] * len(made),
            out_specs=[
                pl.BlockSpec((None,) + item.shape[1:], lambda i: (first + i, 0, 0))
                for item in shapes
            ],
            scratch_shapes=[
                pltpu.VMEM((width, 128), F32),
                pltpu.VMEM((width,) + exchange.inputs[0].shape[2:], BF16),
            ],
            input_output_aliases={3 + k: k for k in range(len(made))},
            compiler_params=pltpu.CompilerParams(vmem_limit_bytes=VMEM_LIMIT),
        )(exchange.place, *exchange.inputs, *made)

    unpacks = [
        (feed_e, unpack_feed, 1), (feed_b, unpack_feed, 0),
        (mixture_dc, unpack_mixture, 1), (mixture_a, unpack_mixture, 0),
    ]
    unpacked = {unpack_feed: [], unpack_mixture: []}
    groups = [[feed_e, feed_b], [mixture_dc, mixture_a]]
    held = [decoded_rows, [], []]
    while unpacks:
        for group in groups:
            if not all(item.ended for item in group):
                held = event(held, group)
            for item in unpacks:
                exchange, unpack, index = item
                if exchange.ended:
                    at = 1 + (unpack is unpack_mixture)
                    held[at] = unpack(exchange, index, held[at])
                    unpacks.remove(item)
                    break
    decoded_rows, grads_ffn, merged = held
    gain_rows = merged[4][:, :2].reshape(6, width)
    grad_gains = jnp.concatenate([gain_rows[:3], gain_rows[4:]], axis=0)
    return (
        encoded_rows[None],
        decoded_rows[None],
        grad_source[None],
        grad_target[None],
        grad_gains,
        merged[3],
        merged[0],
        merged[2],
        merged[1],
        grads_ffn[0],
        grads_ffn[1],
    )


DOWN = ("halve", "stack")


class Exchange:
    def __init__(self, arrays, other=None, scattered=3):
        devices, columns = lax.axis_size("batch"), lax.axis_size("ffn")
        batch, column = lax.axis_index("batch"), lax.axis_index("ffn")
        across = [
            (b * columns + c, b * columns + (c ^ 1)) for b in range(devices) for c in range(columns)
        ]
        split = other is None
        steps = [(across, column.astype(jnp.int32))] if split else []
        beside = []
        bits = [1 << k for k in range(devices.bit_length() - 1)]
        orders = [bits, bits[1::-1] + bits[2:]]
        for level in range(len(bits)):
            choice = [orders[c % 2][level] for c in range(columns)]
            pairs = [
                (b * columns + c, (b ^ choice[c]) * columns + c)
                for b in range(devices) for c in range(columns)
            ]
            bit = jnp.where(column % 2 == 0, choice[0], choice[1])
            steps.append((pairs, (jnp.bitwise_and(batch, bit) != 0).astype(jnp.int32)))
            bit = jnp.where(column % 2 == 0, choice[-1], choice[0])
            beside.append((jnp.bitwise_and(batch, bit) != 0).astype(jnp.int32))
        down = scattered + int(split)
        self.pieces = 1 << down
        place = jnp.int32(0)
        for _, upper in steps[:down]:
            place = place * 2 + upper
        own = other_place = jnp.int32(0)
        for (_, upper), upper_beside in zip(steps[int(split) : down], beside):
            own = own * 2 + upper
            other_place = other_place * 2 + upper_beside
        self.place = jnp.stack([place, jnp.bitwise_xor(own, other_place)])
        self.plan = [] if split else [("send", across, None)]
        self.plan += [("halve", pairs, upper) for pairs, upper in steps[:down]]
        if split and len(arrays) > 1:
            self.plan[0] = ("stack",) + self.plan[0][1:]
        self.plan += [("add", pairs, None) for pairs, _ in steps[down:]]
        self.plan += [
            ("join" if k else "add", pairs, None)
            for k, (pairs, _) in enumerate(reversed(steps[:down]))
        ]
        self.at = 0
        self.ended = False
        self.inputs = arrays
        if not split:
            self.kept, self.sent = arrays[0], other

    def work(self):
        if self.at == len(self.plan):
            return None
        kind, _, upper = self.plan[self.at]
        if kind == "send":
            return kind, [], None
        return kind, self.inputs, upper

    def send(self, made):
        _, pairs, _ = self.plan[self.at]
        self.at += 1
        if made:
            self.kept, self.sent = made[0], made[-1]
        self.inputs = [self.kept, lax.ppermute(self.sent, ("batch", "ffn"), pairs)]


def fold_kernel(works, uppers_ref, *refs):
    refs = list(refs)
    take = lambda count: [refs.pop(0) for _ in range(count)]
    inputs = [take(count) for _, count, _, _ in works]
    outputs = [take(1 + (kind in DOWN)) for kind, _, _, _ in works]
    buffers = [take(count) for _, _, _, count in works]
    sems_in, sems_out = refs
    at_in, started = 0, []

    def copy_in(source, target):
        nonlocal at_in
        copy = pltpu.make_async_copy(source, target, sems_in.at[at_in])
        copy.start()
        at_in += 1
        return copy

    at_out = 0

    def copy_out(source, target):
        nonlocal at_out
        copy = pltpu.make_async_copy(source, target, sems_out.at[at_out])
        copy.start()
        at_out += 1
        started.append(copy)

    waits = []
    for at, ((kind, count, rows, _), given, made, held) in enumerate(
        zip(works, inputs, outputs, buffers)
    ):
        copies = []
        if kind in DOWN:
            half = rows // 2
            upper = uppers_ref[at]
            for side, part in enumerate((upper, 1 - upper)):
                there = pl.ds(pl.multiple_of(part * half, half), half)
                for k, source in enumerate(given):
                    if kind == "stack":
                        target = held[side].at[k : k + 1]
                    else:
                        target = held[side * count + k]
                    copies.append(copy_in(source.at[:, there, :], target))
        elif kind == "add":
            for k, source in enumerate(given):
                copies.append(copy_in(source, held[k]))
        else:
            for k, source in enumerate(given):
                copies.append(copy_in(source, held[0].at[:, k * rows : (k + 1) * rows, :]))
        waits.append(copies)
    for (kind, count, rows, _), made, held, copies in zip(works, outputs, buffers, waits):
        for copy in copies:
            copy.wait()
        for side, target in enumerate(made):
            each = 1 if kind == "stack" else count
            part = held[side * each : (side + 1) * each]
            if kind in ("halve", "add") and count == 2:
                part[0][...] = part[0][...] + part[1][...]
            copy_out(part[0], target)
    for copy in started:
        copy.wait()


def fold(works):
    plans, args, outs, scratch, uppers = [], [], [], [], []
    copies_in = copies_out = 0
    for kind, inputs, upper in works:
        layers, rows, columns = inputs[0].shape
        if kind == "stack":
            layers *= len(inputs)
        made = rows // 2 if kind in DOWN else {"add": rows, "join": 2 * rows}[kind]
        sides = 1 + (kind in DOWN)
        held = {"join": 1, "stack": 2}.get(kind, sides * len(inputs))
        plans.append((kind, len(inputs), rows, held))
        args += inputs
        outs += [jax.ShapeDtypeStruct((layers, made, columns), inputs[0].dtype)] * sides
        scratch += [pltpu.VMEM((layers, made, columns), inputs[0].dtype)] * held
        copies_in += sides * len(inputs)
        copies_out += sides
        uppers.append(jnp.int32(0) if upper is None else upper)
    hbm = pl.BlockSpec(memory_space=pl.ANY)
    results = pl.pallas_call(
        functools.partial(fold_kernel, plans),
        name="fold",
        out_shape=outs,
        in_specs=[pl.BlockSpec(memory_space=pltpu.SMEM)] + [hbm] * len(args),
        out_specs=[hbm] * len(outs),
        scratch_shapes=scratch + [
            pltpu.SemaphoreType.DMA((copies_in,)), pltpu.SemaphoreType.DMA((copies_out,)),
        ],
        compiler_params=pltpu.CompilerParams(vmem_limit_bytes=VMEM_LIMIT),
        cost_estimate=pl.CostEstimate(flops=10**6, bytes_accessed=10**6, transcendentals=0),
    )(jnp.stack(uppers), *args)
    found, at = [], 0
    for kind, _, _, _ in plans:
        sides = 1 + (kind in DOWN)
        found.append(list(results[at : at + sides]))
        at += sides
    return found


def solution(mesh):
    tokens = P(("batch", "ffn"), None, None)
    return jax.shard_map(
        body,
        mesh=mesh,
        in_specs=(
            tokens, tokens, P(("batch", "ffn"), None, None, None),
            P(("batch", "ffn"), None, None, None), tokens,
            P(), P(), P(), P(), P(),
            P(None, None, "ffn"), P(None, "ffn", None), tokens, tokens,
        ),
        out_specs=(
            tokens, tokens, tokens, tokens,
            P(), P(), P(), P(), P(),
            P(None, None, "ffn"), P(None, "ffn", None),
        ),
        check_vma=False,
    )
```

```python
import functools

import jax
import jax.numpy as jnp
from jax import lax
from jax.experimental import pallas as pl
from jax.experimental.pallas import tpu as pltpu
from jax.sharding import PartitionSpec as P

CAPACITY = 256
EPSILON = 1e-05
MASKED = -1000000000.0
PENALTY = -(2.0**30)
ROOT_HALF = 0.7071067811865476
INV_ROOT_TWO_PI = 0.3989422804014327
F32 = jnp.float32
BF16 = jnp.bfloat16
NN = ((1,), (0,))
NT = ((1,), (1,))
TN = ((0,), (0,))
CHUNK = 256
FEED_CHUNK = 512
VMEM_LIMIT = 52 * 2**20
MIDDLE_VMEM = 58 * 2**20


def mm(left, right, dims=NN):
    return lax.dot_general(left, right, (dims, ((), ())), preferred_element_type=F32)


def normalize(values):
    centered = values - jnp.mean(values, axis=0, keepdims=True)
    inverse = lax.rsqrt(jnp.mean(centered * centered, axis=0, keepdims=True) + EPSILON)
    return centered * inverse, inverse


def normalize_back(grad, normed, inverse, gain):
    scaled = normed.astype(F32) * (1.0 / gain)
    gain_grad = jnp.sum(grad * scaled, axis=1, keepdims=True)
    grad_scaled = grad * gain
    back = inverse * (
        grad_scaled
        - jnp.mean(grad_scaled, axis=0, keepdims=True)
        - scaled * jnp.mean(grad_scaled * scaled, axis=0, keepdims=True)
    )
    return back, gain_grad


def gain_column(gains_ref, at):
    row = gains_ref[at : at + 1, :]
    return jnp.broadcast_to(row, (8, row.shape[1])).T[:, 0:1]


def column_to_row(column):
    return jnp.broadcast_to(column, (column.shape[0], 128)).T[0:1]


def route_hits(codes_ref, layer, experts):
    length = codes_ref.shape[2]
    expert = lax.broadcasted_iota(jnp.int32, (experts, length), 0)
    hits, kept = [], []
    for pick in range(2):
        code = codes_ref[layer, pick : pick + 1, :]
        dropped = code >= experts
        route = jnp.where(dropped, code - experts, code)
        hits.append(jnp.where(expert == route, 1.0, 0.0))
        kept.append(jnp.where(dropped, 0.0, 1.0))
    return hits, kept


def prefix_before(values):
    length = values.shape[1]
    lane = lax.broadcasted_iota(jnp.int32, values.shape, 1)
    total = values
    step = 1
    while step < length:
        total = total + jnp.where(lane >= step, pltpu.roll(total, step, 1), 0.0)
        step *= 2
    return total - values


def slot_matrix(position_row):
    slot = lax.broadcasted_iota(jnp.int32, (CAPACITY, position_row.shape[1]), 0).astype(F32)
    return jnp.where(slot == position_row, 1.0, 0.0).astype(BF16)


def slot_matrix_t(position_column):
    slot = lax.broadcasted_iota(jnp.int32, (position_column.shape[0], CAPACITY), 1).astype(F32)
    return jnp.where(slot == position_column, 1.0, 0.0).astype(BF16)


def attend_forward_kernel(
    layer, causal, cross, from_rows, query_side, key_side, gain_at, *refs
):
    if cross:
        (v_ref, s_ref, gains_ref, codes_ref, pairs_ref, router_ref, query_ref, keyval_ref,
         output_ref, h_out, x_out, tables_out, e_out, linv_out, slots_out, heads_out, kv_out,
         e_buf, q_buf, hw_buf, sem) = refs
    else:
        (v_ref, gains_ref, codes_ref, pairs_ref, router_ref, query_ref, keyval_ref,
         output_ref, h_out, x_out, tables_out, e_out, linv_out, slots_out, heads_out, kv_out,
         e_buf, q_buf, hw_buf, sem) = refs
        s_ref = x_out
    width, length = x_out.shape
    experts = router_ref.shape[1]
    head = keyval_ref.shape[2] // 2
    gain = gain_column(gains_ref, gain_at)
    inverses = []
    for at in range(0, length, CHUNK):
        cols = slice(at, at + CHUNK)
        part = v_ref[cols, :].astype(F32).T if from_rows else v_ref[:, cols]
        scaled, inverse = normalize(part)
        x_out[:, cols] = (scaled * gain).astype(BF16)
        inverses.append(inverse)
        if from_rows:
            h_out[:, cols] = part
    inverse = jnp.concatenate(inverses, axis=1)
    flush(x_out)

    hits, kept = route_hits(codes_ref, layer, experts)
    rank = prefix_before(hits[0] + hits[1])
    placed = hits[0] * kept[0] + hits[1] * kept[1]
    position = jnp.where(placed > 0.0, rank, -1.0)
    position_t = position.T

    normed = x_out[...]
    logits = mm(router_ref[0], normed)
    picked = [jnp.sum(hit * logits, axis=0, keepdims=True) for hit in hits]
    top = jnp.maximum(picked[0], picked[1])
    raised = [jnp.exp(item - top) for item in picked]
    total = raised[0] + raised[1]
    gates = [item / total for item in raised]
    weights = gates[0] * kept[0] * hits[0] + gates[1] * kept[1] * hits[1]
    tables_out[...] = jnp.concatenate(
        [position, weights, gates[0], gates[1], inverse, jnp.zeros((5, length), F32)], axis=0
    )

    q_buf[...] = (mm(query_ref[0], normed, TN) * (head**-0.5)).astype(BF16)
    kv = mm(keyval_ref[0], s_ref[...], TN).astype(BF16)
    kv_out[...] = kv
    values_t = kv[head:]
    row = lax.broadcasted_iota(jnp.int32, (head, length), 0)
    key_pair = pairs_ref[key_side : key_side + 1, :]
    penalties = jnp.where((row < 8) & (row != key_pair), PENALTY, 0.0)
    keys = jnp.concatenate([kv[:head].astype(F32), penalties], axis=0).T.astype(BF16)
    row = lax.broadcasted_iota(jnp.int32, (16, length), 0)
    token = lax.broadcasted_iota(jnp.int32, (16, length), 1)
    low = jnp.bitwise_and(token, 7)
    query_pair = pairs_ref[query_side : query_side + 1, :]
    extras = jnp.where(row < 8, jnp.where(row == query_pair, 1, 0), 0)
    extras = jnp.where(row == 8, token - low, extras)
    extras = jnp.where(row == 9, low, extras)
    extras = jnp.where(row == 10, 1, extras)
    extras = extras.astype(F32).astype(BF16)

    copies = []

    def scores_of(e):
        rows = slice(e * head, (e + 1) * head)
        placed_t = slot_matrix_t(position_t[:, e : e + 1])
        gathered = mm(jnp.concatenate([q_buf[rows], extras], axis=0), placed_t)
        slots = gathered.astype(BF16)
        slots_out[e, :head] = slots[:head]
        padded = jnp.concatenate(
            [slots, jnp.zeros((2 * head - slots.shape[0], CAPACITY), BF16)], axis=0
        )
        scores = mm(keys, padded)
        if causal:
            limit = (
                gathered[head + 8 : head + 9]
                + gathered[head + 9 : head + 10]
                + (1.0 - gathered[head + 10 : head + 11]) * length
            )
            key_at = lax.broadcasted_iota(jnp.int32, (length, CAPACITY), 0).astype(F32)
            scores = jnp.where(key_at <= limit, scores, MASKED)
        return scores

    ahead = scores_of(0)
    for e in range(experts):
        rows = slice(e * head, (e + 1) * head)
        scores = ahead
        if e + 1 < experts:
            ahead = scores_of(e + 1)
        top = jnp.max(scores, axis=0, keepdims=True)
        exponent = jnp.exp(scores - top)
        linv = 1.0 / jnp.sum(exponent, axis=0, keepdims=True)
        linv_out[e : e + 1] = linv
        exponent = exponent.astype(BF16)
        e_buf[e] = exponent
        copies.append(pltpu.make_async_copy(e_buf.at[e], e_out.at[e], sem.at[e]))
        copies[-1].start()
        attended = (mm(values_t, exponent) * linv).astype(BF16)
        slots_out[e, head:] = attended
        placed_rows = slot_matrix(position[e : e + 1])
        heads = mm(attended, placed_rows)
        heads_out[rows] = heads.astype(BF16)
        hw_buf[rows] = (heads * weights[e : e + 1]).astype(BF16)
    flush(heads_out)
    flush(slots_out)
    for at in range(0, length, length // 2):
        cols = slice(at, at + length // 2)
        branch = mm(output_ref[0], hw_buf[:, cols], TN)
        h_out[:, cols] = (h_out if from_rows else v_ref)[:, cols] + branch
        flush(h_out, (slice(None), cols))
    for copy in copies:
        copy.wait()


def attend_backward_kernel(layer, cross, gain_at, first, last, *refs):
    refs = list(refs)
    take = lambda count: [refs.pop(0) for _ in range(count)]
    (g_ref, gains_ref, codes_ref, tables_ref, linv_ref, slots_ref, heads_ref, kv_ref, output_ref,
     e_in) = take(10)
    experts, head = slots_ref.shape[0], slots_ref.shape[1] // 2
    width, length = g_ref.shape
    inner = experts * head
    finish = last == experts
    if first:
        d_in, kv_grad_in, hits_in = take(3)
    if finish:
        (x_ref,) = take(1)
        s_ref = take(1)[0] if cross else x_ref
        router_ref, query_ref, keyval_ref, feed_gain_ref = take(4)
        if first:
            (packed_in,) = take(1)
        (g_out,) = take(1)
        if cross:
            (s_out,) = take(1)
        (packed_out,) = take(1)
    else:
        d_out, kv_grad_out, hits_out, packed_out = take(4)
    e_buf, gt_buf, gl_buf, d_buf, hw_buf, sem = refs
    copies = []
    for e in range(first, last):
        copies.append(pltpu.make_async_copy(e_in.at[e], e_buf.at[e - first], sem.at[e - first]))
        copies[-1].start()
    position = tables_ref[0:experts]
    weights = tables_ref[experts : 2 * experts]
    position_t = position.T
    mine = slice(first * head, last * head)

    gl_buf[...] = g_ref[...].astype(BF16)
    gt_buf[...] = mm(output_ref[0, mine, :], gl_buf[...])
    keys_t = kv_ref[:head]
    values = kv_ref[head:].astype(F32).T.astype(BF16)
    weight_grads = []
    if first:
        key_grad, value_grad = kv_grad_in[:head], kv_grad_in[head:]
        d_buf[: first * head] = d_in[...]
        weight_grads.append(hits_in[:first])
    else:
        key_grad = jnp.zeros((head, length), F32)
        value_grad = jnp.zeros((head, length), F32)
    def probs_grad_of(e):
        rows = slice(e * head, (e + 1) * head)
        back = gt_buf[(e - first) * head : (e - first + 1) * head]
        weight_grads.append(jnp.sum(back * heads_ref[rows].astype(F32), axis=0, keepdims=True))
        heads_grad = (back * weights[e : e + 1]).astype(BF16)
        placed_t = slot_matrix_t(position_t[:, e : e + 1])
        slot_grad = (mm(heads_grad, placed_t) * linv_ref[e : e + 1]).astype(BF16)
        delta = jnp.sum(
            slot_grad.astype(F32) * slots_ref[e, head:].astype(F32), axis=0, keepdims=True
        )
        return slot_grad, delta, mm(values, slot_grad)

    ahead = probs_grad_of(first)
    for e in range(first, last):
        slot_grad, delta, probs_grad = ahead
        if e + 1 < last:
            ahead = probs_grad_of(e + 1)
        copies[e - first].wait()
        exponent = e_buf[e - first]
        scores_grad = (exponent.astype(F32) * (probs_grad - delta)).astype(BF16)
        query_grad = (mm(keys_t, scores_grad) * (head**-0.5)).astype(BF16)
        rows = slice(e * head, (e + 1) * head)
        d_buf[rows] = mm(query_grad, slot_matrix(position[e : e + 1])).astype(BF16)
        key_grad = key_grad + mm(slots_ref[e, :head], scores_grad, NT)
        value_grad = value_grad + mm(slot_grad, exponent, NT)

    out_columns = slice(inner, inner + width)
    if finish and first:
        packed_out[: first * head, out_columns] = packed_in[...]
    for e in range(first, last):
        rows = slice(e * head, (e + 1) * head)
        held = slice((e - first) * head, (e - first + 1) * head)
        hw_buf[held] = (heads_ref[rows].astype(F32) * weights[e : e + 1]).astype(BF16)
    out_grad = mm(hw_buf[...], gl_buf[...], NT).astype(BF16)
    if finish:
        packed_out[mine, out_columns] = out_grad
    else:
        packed_out[...] = out_grad
    weight_grad = jnp.concatenate(weight_grads, axis=0)
    if not finish:
        d_out[...] = d_buf[mine]
        kv_grad_out[:head] = key_grad
        kv_grad_out[head:] = value_grad
        hits_out[:last] = weight_grad
        hits_out[last:] = jnp.zeros((experts - last, length), F32)
        return

    d_buf[inner : inner + head] = key_grad.astype(BF16)
    d_buf[inner + head : inner + 2 * head] = value_grad.astype(BF16)
    hits, kept = route_hits(codes_ref, layer, experts)
    gates = [tables_ref[2 * experts + k : 2 * experts + k + 1] for k in range(2)]
    inverse = tables_ref[2 * experts + 2 : 2 * experts + 3]
    chosen = [
        jnp.sum(hit * weight_grad, axis=0, keepdims=True) * keep for hit, keep in zip(hits, kept)
    ]
    mean = gates[0] * chosen[0] + gates[1] * chosen[1]
    logit_grad = sum(
        gate * (item - mean) * hit for gate, item, hit in zip(gates, chosen, hits)
    ).astype(BF16)

    packed_out[:, :inner] = mm(x_ref[...], d_buf[:inner], NT).astype(BF16)
    kv_columns = slice(inner + width, inner + width + 2 * head)
    packed_out[:, kv_columns] = mm(s_ref[...], d_buf[inner:], NT).astype(BF16)
    padded = jnp.concatenate([logit_grad.astype(F32), jnp.zeros((120, length), F32)], axis=0)
    router_grad = mm(x_ref[...], padded.astype(BF16), NT)
    flush(packed_out, (slice(None), slice(0, kv_columns.stop)))

    grad = mm(query_ref[0], d_buf[:inner]) + mm(router_ref[0], logit_grad, TN)
    source_grad = mm(keyval_ref[0], d_buf[inner:])
    if cross:
        s_out[...] = source_grad
        flush(s_out)
    else:
        grad = grad + source_grad
    gain = gain_column(gains_ref, gain_at)
    back, gain_grad = normalize_back(grad, x_ref[...], inverse, gain)
    lane = lax.broadcasted_iota(jnp.int32, router_grad.shape, 1)
    extra = jnp.where(lane == experts, gain_grad, router_grad)
    extra = jnp.where(lane == experts + 1, feed_gain_ref[:, 0:1], extra)
    packed_out[:, kv_columns.stop :] = extra.astype(BF16)
    flush(packed_out, (slice(None), slice(kv_columns.stop, packed_out.shape[1])))
    total = g_ref[...] + back
    if cross:
        g_out[...] = total
    else:
        g_out[...] = total.T


def gelu_parts(values):
    half = 0.5 * (1.0 + lax.erf(values * ROOT_HALF))
    slope = half + values * jnp.exp(-0.5 * values * values) * INV_ROOT_TWO_PI
    return values * half, slope


def hidden_chunks(own, other, axis):
    size = own.shape[axis]
    found = []
    for part, ref in enumerate((own, other)):
        for at in range(0, size, FEED_CHUNK):
            found.append(
                (part, slice(at, at + FEED_CHUNK), slice(part * size + at, part * size + at + FEED_CHUNK))
            )
    return found


def feed_weight_grads(
    grad_low, by_rows, x_ref, wout_refs, hidden_ref, slope_ref, inner_ref, packed_refs
):
    width = x_ref.shape[0]
    size = wout_refs[0].shape[0]
    for part, here, there in reversed(hidden_chunks(wout_refs[0], wout_refs[1], 0)):
        grad = mm(wout_refs[part][here, :], grad_low, NT if by_rows else NN)
        inner = (grad * slope_ref[there].astype(F32)).astype(BF16)
        inner_ref[there] = inner
        packed = packed_refs[part]
        packed[:width, here] = mm(x_ref[...], inner, NT).astype(BF16)
        out_grad = mm(hidden_ref[there], grad_low, NN if by_rows else NT).astype(BF16)
        fold = here.start // (size // 2)
        at = width + here.start - fold * (size // 2)
        packed[at : at + FEED_CHUNK, fold * width : (fold + 1) * width] = out_grad
        flush(inner_ref, there)
        if here.start == 0:
            flush(packed)


def feed_rows_grad(win_refs, inner_ref):
    size = win_refs[0].shape[1]
    return mm(win_refs[0][...], inner_ref[:size]) + mm(win_refs[1][...], inner_ref[size:])


def feed_hidden(x, win_refs, hidden_ref, slope_ref):
    for part, here, there in hidden_chunks(win_refs[0], win_refs[1], 1):
        hidden, slope = gelu_parts(mm(win_refs[part][:, here], x, TN))
        hidden_ref[there] = hidden.astype(BF16)
        slope_ref[there] = slope.astype(BF16)
        flush(hidden_ref, there)
        flush(slope_ref, there)


def feed_result(wout_refs, hidden_ref):
    size = wout_refs[0].shape[0]
    return mm(wout_refs[0][...], hidden_ref[:size], TN) + mm(
        wout_refs[1][...], hidden_ref[size:], TN
    )


def feed_encoder_kernel(
    gain_at, h_ref, gains_ref, win_own, win_other, wout_own, wout_other,
    low_out, rows_out, x_out, inverse_out, hidden_out, slope_out,
):
    gain = gain_column(gains_ref, gain_at)
    scaled, inverse = normalize(h_ref[...])
    x_out[...] = (scaled * gain).astype(BF16)
    inverse_out[...] = inverse
    flush(x_out)
    feed_hidden(x_out[...], (win_own, win_other), hidden_out, slope_out)
    encoded = h_ref[...] + feed_result((wout_own, wout_other), hidden_out)
    low_out[...] = encoded.astype(BF16)
    rows_out[...] = encoded.T.astype(BF16)


def feed_encoder_weights_kernel(
    cot_ref, s_ref, x_ref, hidden_ref, slope_ref, wout_own, wout_other,
    g_out, inner_out, own_out, other_out, low_buf,
):
    g_out[...] = cot_ref[...].astype(F32).T + s_ref[...]
    low_buf[...] = g_out[...].astype(BF16)
    flush(g_out)
    feed_weight_grads(
        low_buf[...], False, x_ref, (wout_own, wout_other), hidden_ref, slope_ref, inner_out,
        (own_out, other_out),
    )


def feed_encoder_rows_kernel(
    gain_at, g_ref, gains_ref, x_ref, inverse_ref, inner_ref, win_own, win_other,
    g_out, gain_out,
):
    gain = gain_column(gains_ref, gain_at)
    grad = feed_rows_grad((win_own, win_other), inner_ref)
    back, gain_grad = normalize_back(grad, x_ref[...], inverse_ref[...], gain)
    g_out[...] = g_ref[...] + back
    gain_out[...] = jnp.broadcast_to(gain_grad, gain_out.shape)


def feed_decoder_weights_kernel(
    gain_at, h_ref, cot_ref, gains_ref, win_own, win_other, wout_own, wout_other,
    x_out, inverse_out, hidden_out, inner_out, own_out, other_out, slope_buf,
):
    gain = gain_column(gains_ref, gain_at)
    scaled, inverse = normalize(h_ref[...])
    x_out[...] = (scaled * gain).astype(BF16)
    inverse_out[...] = inverse
    flush(x_out)
    feed_hidden(x_out[...], (win_own, win_other), hidden_out, slope_buf)
    feed_weight_grads(
        cot_ref[...], True, x_out, (wout_own, wout_other), hidden_out, slope_buf, inner_out,
        (own_out, other_out),
    )


def feed_decoder_rows_kernel(
    gain_at, cot_ref, gains_ref, x_ref, inverse_ref, inner_ref, win_own, win_other,
    g_out, gain_out,
):
    gain = gain_column(gains_ref, gain_at)
    grad = feed_rows_grad((win_own, win_other), inner_ref)
    back, gain_grad = normalize_back(grad, x_ref[...], inverse_ref[...], gain)
    g_out[...] = cot_ref[...].astype(F32).T + back
    gain_out[...] = jnp.broadcast_to(gain_grad, gain_out.shape)


def feed_decoder_result_kernel(h_ref, hidden_ref, wout_own, wout_other, rows_out):
    result = h_ref[...] + feed_result((wout_own, wout_other), hidden_ref)
    rows_out[...] = result.T.astype(BF16)


def first_kernel(parts, *refs):
    refs = list(refs)
    take = lambda count: [refs.pop(0) for _ in range(count)]
    gains, codes, pairs = take(3)
    given = [take(5) for _ in parts]
    made = [take(8) for _ in parts]
    held = [take(4) for _ in parts]
    for part, ins, outs, scratch in zip(parts, given, made, held):
        attend_forward_kernel(*part, ins[0], gains, codes, pairs, *ins[1:], *outs, *scratch)


def middle_kernel(part, gain_b, gain_e, *refs):
    refs = list(refs)
    take = lambda count: [refs.pop(0) for _ in range(count)]
    gains, codes, pairs, h_ref, d_ref, cot_ref = take(6)
    mixture, feed_b, feed_e = take(4), take(4), take(4)
    encoder, cross = take(6), take(8)
    hidden_out, own_out, other_out, g_out, gain_out = take(5)
    held = take(4)
    x_buf, inverse_buf = refs
    feed_encoder_kernel(gain_b, h_ref, gains, *feed_b, *encoder)
    attend_forward_kernel(
        *part, d_ref, encoder[0], gains, codes, pairs, *mixture, *cross, *held
    )
    for ref in encoder[4:]:
        ref.finish()
    inner_buf, slope_buf = [ref.buffer for ref in encoder[4:]]
    feed_decoder_weights_kernel(
        gain_e, cross[0], cot_ref, gains, *feed_e,
        x_buf, inverse_buf, hidden_out, inner_buf, own_out, other_out, slope_buf,
    )
    feed_decoder_rows_kernel(
        gain_e, cot_ref, gains, x_buf, inverse_buf, inner_buf, *feed_e[:2], g_out, gain_out
    )


def feed_encoder_back_kernel(
    gain_at, cot_ref, s_ref, gains_ref, x_ref, inverse_ref, hidden_ref, slope_ref,
    wout_own, wout_other, win_own, win_other,
    g_out, own_out, other_out, gain_out, low_buf, g_buf, inner_buf,
):
    feed_encoder_weights_kernel(
        cot_ref, s_ref, x_ref, hidden_ref, slope_ref, wout_own, wout_other,
        g_buf, inner_buf, own_out, other_out, low_buf,
    )
    feed_encoder_rows_kernel(
        gain_at, g_buf, gains_ref, x_ref, inverse_ref, inner_buf, win_own, win_other,
        g_out, gain_out,
    )


def unpack_feed_kernel(pieces, place_ref, *refs):
    in_out, out_out, packed_ref = refs[-3:]
    width = in_out.shape[0]
    size = packed_ref.shape[0] // pieces
    packed_ref[: packed_ref.shape[0] // 2] = refs[0][0]
    packed_ref[packed_ref.shape[0] // 2 :] = refs[1][0]
    for piece in range(pieces):
        at = pl.multiple_of(jnp.bitwise_xor(place_ref[0], piece) * size, size)
        rows = packed_ref[pl.ds(at, size), :].astype(F32)
        if piece * size < width:
            in_out[piece * size : (piece + 1) * size] = rows
        else:
            at = piece * size - width
            out_out[at : at + size] = rows[:, :width]
            out_out[width + at : width + at + size] = rows[:, width:]


def unpack_mixture_kernel(pieces, place_ref, low_ref, high_ref, *refs):
    query_out, output_out, keyval_out, router_out, gains_out, extra, packed_ref = refs[-7:]
    size = packed_ref.shape[0] // pieces
    packed_ref[: packed_ref.shape[0] // 2] = low_ref[0]
    packed_ref[packed_ref.shape[0] // 2 :] = high_ref[0]
    inner, width = query_out.shape[1], output_out.shape[1]
    end = inner + width + keyval_out.shape[1]
    experts = router_out.shape[0]
    for piece in range(pieces):
        position = jnp.bitwise_xor(place_ref[0], piece)
        crossed = jnp.where(position >= pieces // 2, place_ref[1], 0)
        at = pl.multiple_of(jnp.bitwise_xor(position, crossed) * size, size)
        rows = packed_ref[pl.ds(at, size), :].astype(F32)
        there = slice(piece * size, (piece + 1) * size)
        query_out[there] = rows[:, :inner]
        output_out[there] = rows[:, inner : inner + width]
        keyval_out[there] = rows[:, inner + width : end]
        extra[there] = rows[:, end:]
    turned = extra[...].T
    router_out[...] = turned[:experts]
    gains_out[...] = turned[experts : experts + 8]


LEFT = "left"
WHOLE = "whole"
LARGE = 2**17


class Fetched:
    def __init__(self, source, buffer, sem):
        self.copy = pltpu.make_async_copy(source, buffer, sem)
        self.copy.start()
        self.buffer, self.shape, self.waits = buffer, buffer.shape, True

    def ready(self):
        if self.waits:
            self.copy.wait()
            self.waits = False
        return self.buffer

    def __getitem__(self, at):
        return self.ready()[at]


class Stored:
    def __init__(self, place, buffer, sems):
        self.place, self.buffer, self.sems = place, buffer, sems
        self.shape = buffer.shape
        self.copies = []
        self.finished = False

    def __getitem__(self, at):
        return self.buffer[at]

    def __setitem__(self, at, value):
        self.buffer[at] = value

    def flush(self, at=None):
        source, place = self.buffer, self.place
        if at is not None:
            source, place = source.at[at], place.at[at]
        self.copies.append(pltpu.make_async_copy(source, place, self.sems.at[len(self.copies)]))
        self.copies[-1].start()

    def finish(self):
        if self.finished:
            return
        if not self.copies:
            self.flush()
        for copy in self.copies:
            copy.wait()
        self.finished = True


def flush(ref, at=None):
    if isinstance(ref, Stored):
        ref.flush(at)


FLUSHES = 8


def layer_spec(array, layer):
    return (layer, True)


def call(kernel, name, outs, args, in_specs, out_specs, scratch, flops, limit=VMEM_LIMIT):
    shapes = [jax.ShapeDtypeStruct(shape, dtype) for shape, dtype in outs]
    ins, buffers = [], []
    for item, spec in zip(args, in_specs):
        shape = item.shape
        if isinstance(spec, tuple):
            shape = ((1,) if spec[1] else ()) + item.shape[1:]
        size = item.dtype.itemsize
        for extent in shape:
            size *= extent
        mine = isinstance(spec, tuple) or (spec == WHOLE and size >= LARGE)
        ins.append(spec if mine else None)
        if mine:
            buffers.append(pltpu.VMEM(shape, item.dtype))
    stored = [
        spec == WHOLE and item.size * item.dtype.itemsize >= LARGE
        for item, spec in zip(shapes, out_specs)
    ]
    buffers += [pltpu.VMEM(item.shape, item.dtype) for item, mine in zip(shapes, stored) if mine]
    count = len(buffers)
    fetched = sum(item is not None for item in ins)

    def wrapped(*refs):
        refs = list(refs)
        given, made = refs[: len(ins)], refs[len(ins) : len(ins) + len(shapes)]
        rest = refs[len(ins) + len(shapes) :]
        own, held, sems_in, sems_out = rest[: len(scratch)], rest[len(scratch) : -2], rest[-2], rest[-1]
        used = 0
        for k, spec in enumerate(ins):
            if spec is not None:
                source = given[k]
                if isinstance(spec, tuple):
                    source = source.at[pl.ds(spec[0], 1)] if spec[1] else source.at[spec[0]]
                given[k] = Fetched(source, held[used], sems_in.at[used])
                used += 1
        for k, mine in enumerate(stored):
            if mine:
                made[k] = Stored(made[k], held[used], sems_out.at[used - fetched])
                used += 1
        kernel(*given, *made, *own)
        for item in given:
            if isinstance(item, Fetched):
                item.ready()
        for item in made:
            if isinstance(item, Stored):
                item.finish()

    moved = sum(a.size * a.dtype.itemsize for a in args) + sum(
        s.size * s.dtype.itemsize for s in shapes
    )
    vmem, hbm = pl.BlockSpec(memory_space=pltpu.VMEM), pl.BlockSpec(memory_space=pl.ANY)
    return pl.pallas_call(
        wrapped,
        name=name,
        out_shape=shapes,
        in_specs=[hbm if k is not None or s == LEFT else vmem for k, s in zip(ins, in_specs)],
        out_specs=[hbm if k or s == LEFT else vmem for k, s in zip(stored, out_specs)],
        scratch_shapes=list(scratch) + buffers + [
            pltpu.SemaphoreType.DMA((max(fetched, 1),)),
            pltpu.SemaphoreType.DMA((max(count - fetched, 1), FLUSHES)),
        ],
        compiler_params=pltpu.CompilerParams(vmem_limit_bytes=limit),
        cost_estimate=pl.CostEstimate(flops=30 * flops, bytes_accessed=moved, transcendentals=0),
    )(*args)


def body(
    source, target, routes, overflow, pairs, gains, router, query, keyval, output,
    ffn_in, ffn_out, cot_source, cot_target,
):
    _, length, width = source.shape
    experts = router.shape[2]
    head = keyval.shape[2] // 2
    inner = experts * head
    hidden = ffn_in.shape[2] * lax.axis_size("ffn")
    router = jnp.transpose(router, (0, 2, 1))
    codes = jnp.transpose(routes[0] + experts * overflow[0], (0, 2, 1))
    pair_rows = pairs[0]
    swap = [(0, 1), (1, 0)]
    win_other = lax.ppermute(ffn_in, "ffn", swap)
    wout_other = lax.ppermute(ffn_out, "ffn", swap)

    def layer_args(layer):
        arrays = (router, query, keyval, output)
        return arrays, [layer_spec(item, layer) for item in arrays]

    attend_outs = [
        ((width, length), F32),
        ((width, length), BF16),
        ((3 * experts, length), F32),
        ((experts, length, CAPACITY), BF16),
        ((experts, CAPACITY), F32),
        ((experts, 2 * head, CAPACITY), BF16),
        ((inner, length), BF16),
        ((2 * head, length), BF16),
    ]
    attend_specs = [WHOLE] * 3 + [LEFT] + [WHOLE] * 4
    attend_scratch = [
        pltpu.VMEM((experts, length, CAPACITY), BF16),
        pltpu.VMEM((inner, length), BF16),
        pltpu.VMEM((inner, length), BF16),
        pltpu.SemaphoreType.DMA((experts,)),
    ]

    def attend_back(layer, gain_at, grad, saved, keys, feed_gain):
        cross = keys is not None
        _, normed, tables, exponents, linv, slots, heads, kv = saved
        arrays, specs = layer_args(layer)
        args = [grad, gains, codes, tables, linv, slots, heads, kv, output, exponents, normed]
        args += ([keys] if cross else []) + list(arrays[:3]) + [feed_gain]
        arg_specs = [WHOLE] * 8 + [specs[3], LEFT] + [WHOLE] * (2 if cross else 1)
        arg_specs += specs[:3] + [WHOLE]
        outs = [((width, length) if cross else (length, width), F32)]
        outs += [((width, length), F32)] if cross else []
        outs += [((width, inner + width + 2 * head + 128), BF16)]
        return call(
            functools.partial(attend_backward_kernel, layer, cross, gain_at, 0, experts),
            f"attend_back{layer}", outs, args, arg_specs, [WHOLE] * len(outs),
            [
                pltpu.VMEM((experts, length, CAPACITY), BF16),
                pltpu.VMEM((inner, length), F32),
                pltpu.VMEM((width, length), BF16),
                pltpu.VMEM((inner + 2 * head, length), BF16),
                pltpu.VMEM((inner, length), BF16),
                pltpu.SemaphoreType.DMA((experts,)),
            ],
            13 * 10**9,
        )

    def half_spec(array, index):
        return (index, False)

    def ffn_args(index):
        arrays = [ffn_in, win_other, ffn_out, wout_other]
        return arrays, [half_spec(item, index) for item in arrays]

    travelling = []

    def boundary(values):
        going = [(item, item.work()) for item in travelling]
        going = [(item, work) for item, work in going if work is not None]
        works = [work for _, work in going if work[1]]
        made = fold(works) if works else []
        ended = [item for item in travelling if item.work() is None and not item.ended]
        brought = [item.inputs for item in ended]
        values, made, brought = lax.optimization_barrier((values, made, brought))
        for item, item.inputs in zip(ended, brought):
            item.ended = True
        for item, work in going:
            item.send(made.pop(0) if work[1] else None)
        return values, not all(item.ended for item in travelling)

    last_made = []

    def event(values, items):
        going = [(item, item.work()) for item in items if item.work() is not None]
        works = [work for _, work in going]
        ended = [item for item in items if item.work() is None and not item.ended]
        tied = (values, [work[1] for work in works], [item.inputs for item in ended], last_made)
        values, inputs, brought, _ = lax.optimization_barrier(tied)
        for item, item.inputs in zip(ended, brought):
            item.ended = True
        if works:
            made = fold([(work[0], given, work[2]) for work, given in zip(works, inputs)])
            last_made[:] = [arrays[0] for arrays in made]
            for (item, _), arrays in zip(going, made):
                item.send(arrays)
        return values

    packed_shape = (2 * width, hidden // 2)
    common = [gains, codes, pair_rows]
    layers = [layer_args(layer) for layer in range(3)]
    parts = [(0, False, False, True, 0, 0, 0), (1, True, False, True, 1, 1, 2)]
    saved = call(
        functools.partial(first_kernel, parts), "attend_self", attend_outs * 2,
        common + [source[0], *layers[0][0], target[0], *layers[1][0]],
        [WHOLE] * 3 + [WHOLE, *layers[0][1], WHOLE, *layers[1][1]],
        attend_specs * 2, attend_scratch * 2, 16 * 10**9,
    )
    saved_a, saved_c = saved[:8], saved[8:]
    feed_args = [ffn_args(0), ffn_args(1)]
    made = call(
        functools.partial(middle_kernel, (2, False, True, False, 1, 0, 3), 1, 4), "middle",
        [
            ((width, length), BF16), ((length, width), BF16), ((width, length), BF16),
            ((1, length), F32), ((hidden, length), BF16), ((hidden, length), BF16),
        ] + attend_outs + [
            ((hidden, length), BF16), (packed_shape, BF16), (packed_shape, BF16),
            ((width, length), F32), ((width, 128), F32),
        ],
        common + [saved_a[0], saved_c[0], cot_target[0], *layers[2][0]]
        + feed_args[0][0] + feed_args[1][0],
        [WHOLE] * 6 + layers[2][1] + feed_args[0][1] + feed_args[1][1],
        [WHOLE] * 6 + attend_specs + [WHOLE] * 5,
        attend_scratch + [pltpu.VMEM((width, length), BF16), pltpu.VMEM((1, length), F32)],
        28 * 10**9, MIDDLE_VMEM,
    )
    encoded_low, encoded_rows, normed_b, inverse_b, hidden_b, slope_b = made[:6]
    saved_d = made[6:14]
    hidden_e, own_e, other_e, grad_e, gain_e = made[14:]
    feed_e = Exchange([own_e[None]], other_e[None], 3)
    travelling.append(feed_e)
    grad_e, _ = boundary(grad_e)
    grad_d, source_grad, packed_d = attend_back(2, 3, grad_e, saved_d, encoded_low, gain_e)
    source_grad, _ = boundary(source_grad)
    weights, weight_specs = feed_args[0]
    grad_b, own_b, other_b, gain_b = call(
        functools.partial(feed_encoder_back_kernel, 1), "feed_encoder_back",
        [((width, length), F32), (packed_shape, BF16), (packed_shape, BF16), ((width, 128), F32)],
        [cot_source[0], source_grad, gains, normed_b, inverse_b, hidden_b, slope_b]
        + weights[2:] + weights[:2],
        [WHOLE] * 7 + weight_specs[2:] + weight_specs[:2], [WHOLE] * 4,
        [
            pltpu.VMEM((width, length), BF16), pltpu.VMEM((width, length), F32),
            pltpu.VMEM((hidden, length), BF16),
        ],
        10 * 10**9,
    )
    feed_b = Exchange([own_b[None]], other_b[None], 3)
    travelling.append(feed_b)
    (grad_d, grad_b), _ = boundary((grad_d, grad_b))
    grad_target, packed_c = attend_back(1, 2, grad_d, saved_c, None, gain_b)
    mixture_dc = Exchange([packed_c[None], packed_d[None]], scattered=3)
    travelling.append(mixture_dc)
    grad_b, _ = boundary(grad_b)
    grad_source, packed_a = attend_back(0, 0, grad_b, saved_a, None, gain_b)
    mixture_a = Exchange([packed_a[None]], scattered=3)
    travelling.append(mixture_a)
    hidden_e, _ = boundary(hidden_e)
    (decoded_rows,) = call(
        feed_decoder_result_kernel, "feed_decoder_result", [((length, width), BF16)],
        [saved_d[0], hidden_e] + ffn_args(1)[0][2:], [WHOLE] * 2 + ffn_args(1)[1][2:], [WHOLE], [],
        3 * 10**9,
    )

    def unpack_feed(exchange, index, made):
        pieces = exchange.pieces
        shapes = [
            jax.ShapeDtypeStruct((2,) + item.shape[1:], F32) for item in (ffn_in, ffn_out)
        ]
        spec = lambda item: pl.BlockSpec(
            (None,) + item.shape[1:], lambda i: (index, 0, 0), pipeline_mode=pl.Buffered(1)
        )
        return pl.pallas_call(
            functools.partial(unpack_feed_kernel, pieces), name="unpack_feed", grid=(1,),
            out_shape=shapes,
            in_specs=[pl.BlockSpec(memory_space=pltpu.SMEM)] + [pl.BlockSpec(memory_space=pltpu.VMEM)] * 2
            + [pl.BlockSpec(memory_space=pl.ANY)] * len(made),
            out_specs=[spec(item) for item in shapes],
            scratch_shapes=[pltpu.VMEM(packed_shape, BF16)],
            input_output_aliases={3 + k: k for k in range(len(made))},
            compiler_params=pltpu.CompilerParams(vmem_limit_bytes=VMEM_LIMIT),
            cost_estimate=pl.CostEstimate(flops=10**11, bytes_accessed=10**6, transcendentals=0),
        )(exchange.place, *exchange.inputs, *made)

    def unpack_mixture(exchange, first, made):
        layers = exchange.inputs[0].shape[0]
        columns = (inner, width, 2 * head)
        shapes = [jax.ShapeDtypeStruct((3, width, size), F32) for size in columns]
        shapes += [jax.ShapeDtypeStruct((3, rows, width), F32) for rows in (experts, 8)]
        return pl.pallas_call(
            functools.partial(unpack_mixture_kernel, exchange.pieces), name="unpack_mixture",
            grid=(layers,),
            out_shape=shapes,
            in_specs=[
                pl.BlockSpec(memory_space=pltpu.SMEM),
            ] + [
                pl.BlockSpec((1,) + item.shape[1:], lambda i: (i, 0, 0)) for item in exchange.inputs
            ] + [pl.BlockSpec(memory_space=pl.ANY)] * len(made),
            out_specs=[
                pl.BlockSpec((None,) + item.shape[1:], lambda i: (first + i, 0, 0))
                for item in shapes
            ],
            scratch_shapes=[
                pltpu.VMEM((width, 128), F32),
                pltpu.VMEM((width,) + exchange.inputs[0].shape[2:], BF16),
            ],
            input_output_aliases={3 + k: k for k in range(len(made))},
            compiler_params=pltpu.CompilerParams(vmem_limit_bytes=VMEM_LIMIT),
            cost_estimate=pl.CostEstimate(flops=10**11, bytes_accessed=10**6, transcendentals=0),
        )(exchange.place, *exchange.inputs, *made)

    unpacks = [
        (feed_e, unpack_feed, 1), (feed_b, unpack_feed, 0),
        (mixture_dc, unpack_mixture, 1), (mixture_a, unpack_mixture, 0),
    ]
    unpacked = {unpack_feed: [], unpack_mixture: []}
    groups = [[feed_e, feed_b], [mixture_dc, mixture_a]]
    held = [decoded_rows, [], []]
    order = [0, 1, 0, 1, 0, 1, 0, 1, 1, 0, 1, 1, 1]
    while unpacks:
        for group in [groups[k] for k in order]:
            if not all(item.ended for item in group):
                held = event(held, group)
            for item in unpacks:
                exchange, unpack, index = item
                if exchange.ended:
                    at = 1 + (unpack is unpack_mixture)
                    held[at] = unpack(exchange, index, held[at])
                    unpacks.remove(item)
                    break
    decoded_rows, grads_ffn, merged = held
    gain_rows = merged[4][:, :2].reshape(6, width)
    grad_gains = jnp.concatenate([gain_rows[:3], gain_rows[4:]], axis=0)
    return (
        encoded_rows[None],
        decoded_rows[None],
        grad_source[None],
        grad_target[None],
        grad_gains,
        jnp.transpose(merged[3], (0, 2, 1)),
        merged[0],
        merged[2],
        merged[1],
        grads_ffn[0],
        grads_ffn[1],
    )


DOWN = ("halve", "stack")


class Exchange:
    def __init__(self, arrays, other=None, scattered=3):
        devices, columns = lax.axis_size("batch"), lax.axis_size("ffn")
        batch, column = lax.axis_index("batch"), lax.axis_index("ffn")
        across = [
            (b * columns + c, b * columns + (c ^ 1)) for b in range(devices) for c in range(columns)
        ]
        split = other is None
        steps = [(across, column.astype(jnp.int32))] if split else []
        beside = []
        bits = [1 << k for k in range(devices.bit_length() - 1)]
        orders = [bits, bits[1::-1] + bits[2:]]
        for level in range(len(bits)):
            choice = [orders[c % 2][level] for c in range(columns)]
            pairs = [
                (b * columns + c, (b ^ choice[c]) * columns + c)
                for b in range(devices) for c in range(columns)
            ]
            bit = jnp.where(column % 2 == 0, choice[0], choice[1])
            steps.append((pairs, (jnp.bitwise_and(batch, bit) != 0).astype(jnp.int32)))
            bit = jnp.where(column % 2 == 0, choice[-1], choice[0])
            beside.append((jnp.bitwise_and(batch, bit) != 0).astype(jnp.int32))
        down = scattered + int(split)
        self.pieces = 1 << down
        place = jnp.int32(0)
        for _, upper in steps[:down]:
            place = place * 2 + upper
        own = other_place = jnp.int32(0)
        for (_, upper), upper_beside in zip(steps[int(split) : down], beside):
            own = own * 2 + upper
            other_place = other_place * 2 + upper_beside
        self.place = jnp.stack([place, jnp.bitwise_xor(own, other_place)])
        self.plan = [] if split else [("send", across, None)]
        self.plan += [("halve", pairs, upper) for pairs, upper in steps[:down]]
        if split and len(arrays) > 1:
            self.plan[0] = ("stack",) + self.plan[0][1:]
        self.plan += [("add", pairs, None) for pairs, _ in steps[down:]]
        self.plan += [
            ("join" if k else "add", pairs, None)
            for k, (pairs, _) in enumerate(reversed(steps[:down]))
        ]
        self.at = 0
        self.ended = False
        self.inputs = arrays
        if not split:
            self.kept, self.sent = arrays[0], other

    def work(self):
        if self.at == len(self.plan):
            return None
        kind, _, upper = self.plan[self.at]
        if kind == "send":
            return kind, [], None
        return kind, self.inputs, upper

    def send(self, made):
        _, pairs, _ = self.plan[self.at]
        self.at += 1
        if made:
            self.kept, self.sent = made[0], made[-1]
        self.inputs = [self.kept, lax.ppermute(self.sent, ("batch", "ffn"), pairs)]


def fold_kernel(works, uppers_ref, *refs):
    refs = list(refs)
    take = lambda count: [refs.pop(0) for _ in range(count)]
    inputs = [take(count) for _, count, _, _ in works]
    outputs = [take(1 + (kind in DOWN)) for kind, _, _, _ in works]
    buffers = [take(count) for _, _, _, count in works]
    sems_in, sems_out = refs
    at_in, started = 0, []

    def copy_in(source, target):
        nonlocal at_in
        copy = pltpu.make_async_copy(source, target, sems_in.at[at_in])
        copy.start()
        at_in += 1
        return copy

    at_out = 0

    def copy_out(source, target):
        nonlocal at_out
        copy = pltpu.make_async_copy(source, target, sems_out.at[at_out])
        copy.start()
        at_out += 1
        started.append(copy)

    waits = []
    for at, ((kind, count, rows, _), given, made, held) in enumerate(
        zip(works, inputs, outputs, buffers)
    ):
        copies = []
        if kind in DOWN:
            half = rows // 2
            upper = uppers_ref[at]
            for side, part in enumerate((upper, 1 - upper)):
                there = pl.ds(pl.multiple_of(part * half, half), half)
                for k, source in enumerate(given):
                    if kind == "stack":
                        target = held[side].at[k : k + 1]
                    else:
                        target = held[side * count + k]
                    copies.append(copy_in(source.at[:, there, :], target))
        elif kind == "add":
            for k, source in enumerate(given):
                copies.append(copy_in(source, held[k]))
        else:
            for k, source in enumerate(given):
                copies.append(copy_in(source, held[0].at[:, k * rows : (k + 1) * rows, :]))
        waits.append(copies)
    for (kind, count, rows, _), made, held, copies in zip(works, outputs, buffers, waits):
        for copy in copies:
            copy.wait()
        for side, target in enumerate(made):
            each = 1 if kind == "stack" else count
            part = held[side * each : (side + 1) * each]
            if kind in ("halve", "add") and count == 2:
                part[0][...] = part[0][...] + part[1][...]
            copy_out(part[0], target)
    for copy in started:
        copy.wait()


def fold(works):
    plans, args, outs, scratch, uppers = [], [], [], [], []
    copies_in = copies_out = 0
    for kind, inputs, upper in works:
        layers, rows, columns = inputs[0].shape
        if kind == "stack":
            layers *= len(inputs)
        made = rows // 2 if kind in DOWN else {"add": rows, "join": 2 * rows}[kind]
        sides = 1 + (kind in DOWN)
        held = {"join": 1, "stack": 2}.get(kind, sides * len(inputs))
        plans.append((kind, len(inputs), rows, held))
        args += inputs
        outs += [jax.ShapeDtypeStruct((layers, made, columns), inputs[0].dtype)] * sides
        scratch += [pltpu.VMEM((layers, made, columns), inputs[0].dtype)] * held
        copies_in += sides * len(inputs)
        copies_out += sides
        uppers.append(jnp.int32(0) if upper is None else upper)
    hbm = pl.BlockSpec(memory_space=pl.ANY)
    results = pl.pallas_call(
        functools.partial(fold_kernel, plans),
        name="fold",
        out_shape=outs,
        in_specs=[pl.BlockSpec(memory_space=pltpu.SMEM)] + [hbm] * len(args),
        out_specs=[hbm] * len(outs),
        scratch_shapes=scratch + [
            pltpu.SemaphoreType.DMA((copies_in,)), pltpu.SemaphoreType.DMA((copies_out,)),
        ],
        compiler_params=pltpu.CompilerParams(vmem_limit_bytes=VMEM_LIMIT),
        cost_estimate=pl.CostEstimate(flops=10**11, bytes_accessed=10**6, transcendentals=0),
    )(jnp.stack(uppers), *args)
    found, at = [], 0
    for kind, _, _, _ in plans:
        sides = 1 + (kind in DOWN)
        found.append(list(results[at : at + sides]))
        at += sides
    return found


def solution(mesh):
    tokens = P(("batch", "ffn"), None, None)
    return jax.shard_map(
        body,
        mesh=mesh,
        in_specs=(
            tokens, tokens, P(("batch", "ffn"), None, None, None),
            P(("batch", "ffn"), None, None, None), tokens,
            P(), P(), P(), P(), P(),
            P(None, None, "ffn"), P(None, "ffn", None), tokens, tokens,
        ),
        out_specs=(
            tokens, tokens, tokens, tokens,
            P(), P(), P(), P(), P(),
            P(None, None, "ffn"), P(None, "ffn", None),
        ),
        check_vma=False,
    )
```

```python
import functools

import jax
import jax.numpy as jnp
from jax import lax
from jax.experimental import pallas as pl
from jax.experimental.pallas import tpu as pltpu
from jax.sharding import PartitionSpec as P

CAPACITY = 256
EPSILON = 1e-05
MASKED = -1000000000.0
PENALTY = -(2.0**30)
ROOT_HALF = 0.7071067811865476
INV_ROOT_TWO_PI = 0.3989422804014327
F32 = jnp.float32
BF16 = jnp.bfloat16
NN = ((1,), (0,))
NT = ((1,), (1,))
TN = ((0,), (0,))
CHUNK = 256
FEED_CHUNK = 512
VMEM_LIMIT = 52 * 2**20
MIDDLE_VMEM = 58 * 2**20


def mm(left, right, dims=NN):
    return lax.dot_general(left, right, (dims, ((), ())), preferred_element_type=F32)


def normalize(values):
    centered = values - jnp.mean(values, axis=0, keepdims=True)
    inverse = lax.rsqrt(jnp.mean(centered * centered, axis=0, keepdims=True) + EPSILON)
    return centered * inverse, inverse


def normalize_back(grad, normed, inverse, gain):
    scaled = normed.astype(F32) * (1.0 / gain)
    gain_grad = jnp.sum(grad * scaled, axis=1, keepdims=True)
    grad_scaled = grad * gain
    back = inverse * (
        grad_scaled
        - jnp.mean(grad_scaled, axis=0, keepdims=True)
        - scaled * jnp.mean(grad_scaled * scaled, axis=0, keepdims=True)
    )
    return back, gain_grad


def gain_column(gains_ref, at):
    row = gains_ref[at : at + 1, :]
    return jnp.broadcast_to(row, (8, row.shape[1])).T[:, 0:1]


def column_to_row(column):
    return jnp.broadcast_to(column, (column.shape[0], 128)).T[0:1]


def route_hits(codes_ref, layer, experts):
    length = codes_ref.shape[2]
    expert = lax.broadcasted_iota(jnp.int32, (experts, length), 0)
    hits, kept = [], []
    for pick in range(2):
        code = codes_ref[layer, pick : pick + 1, :]
        dropped = code >= experts
        route = jnp.where(dropped, code - experts, code)
        hits.append(jnp.where(expert == route, 1.0, 0.0))
        kept.append(jnp.where(dropped, 0.0, 1.0))
    return hits, kept


def prefix_before(values):
    length = values.shape[1]
    lane = lax.broadcasted_iota(jnp.int32, values.shape, 1)
    total = values
    step = 1
    while step < length:
        total = total + jnp.where(lane >= step, pltpu.roll(total, step, 1), 0.0)
        step *= 2
    return total - values


def slot_matrix(position_row):
    slot = lax.broadcasted_iota(jnp.int32, (CAPACITY, position_row.shape[1]), 0).astype(F32)
    return jnp.where(slot == position_row, 1.0, 0.0).astype(BF16)


def slot_matrix_t(position_column):
    slot = lax.broadcasted_iota(jnp.int32, (position_column.shape[0], CAPACITY), 1).astype(F32)
    return jnp.where(slot == position_column, 1.0, 0.0).astype(BF16)


def attend_forward_kernel(
    layer, causal, cross, from_rows, query_side, key_side, gain_at, *refs
):
    if cross:
        (v_ref, s_ref, gains_ref, codes_ref, pairs_ref, router_ref, query_ref, keyval_ref,
         output_ref, h_out, x_out, tables_out, e_out, linv_out, slots_out, heads_out, kv_out,
         e_buf, q_buf, hw_buf, sem) = refs
    else:
        (v_ref, gains_ref, codes_ref, pairs_ref, router_ref, query_ref, keyval_ref,
         output_ref, h_out, x_out, tables_out, e_out, linv_out, slots_out, heads_out, kv_out,
         e_buf, q_buf, hw_buf, sem) = refs
        s_ref = x_out
    width, length = x_out.shape
    experts = router_ref.shape[1]
    head = keyval_ref.shape[2] // 2
    gain = gain_column(gains_ref, gain_at)
    inverses = []
    for at in range(0, length, CHUNK):
        cols = slice(at, at + CHUNK)
        part = v_ref[cols, :].astype(F32).T if from_rows else v_ref[:, cols]
        scaled, inverse = normalize(part)
        x_out[:, cols] = (scaled * gain).astype(BF16)
        inverses.append(inverse)
        if from_rows:
            h_out[:, cols] = part
    inverse = jnp.concatenate(inverses, axis=1)
    flush(x_out)

    hits, kept = route_hits(codes_ref, layer, experts)
    rank = prefix_before(hits[0] + hits[1])
    placed = hits[0] * kept[0] + hits[1] * kept[1]
    position = jnp.where(placed > 0.0, rank, -1.0)
    position_t = position.T

    normed = x_out[...]
    logits = mm(router_ref[0], normed)
    picked = [jnp.sum(hit * logits, axis=0, keepdims=True) for hit in hits]
    top = jnp.maximum(picked[0], picked[1])
    raised = [jnp.exp(item - top) for item in picked]
    total = raised[0] + raised[1]
    gates = [item / total for item in raised]
    weights = gates[0] * kept[0] * hits[0] + gates[1] * kept[1] * hits[1]
    tables_out[...] = jnp.concatenate(
        [position, weights, gates[0], gates[1], inverse, jnp.zeros((5, length), F32)], axis=0
    )

    q_buf[...] = (mm(query_ref[0], normed, TN) * (head**-0.5)).astype(BF16)
    kv = mm(keyval_ref[0], s_ref[...], TN).astype(BF16)
    kv_out[...] = kv
    values_t = kv[head:]
    row = lax.broadcasted_iota(jnp.int32, (head, length), 0)
    key_pair = pairs_ref[key_side : key_side + 1, :]
    penalties = jnp.where((row < 8) & (row != key_pair), PENALTY, 0.0)
    keys = jnp.concatenate([kv[:head].astype(F32), penalties], axis=0).T.astype(BF16)
    row = lax.broadcasted_iota(jnp.int32, (16, length), 0)
    token = lax.broadcasted_iota(jnp.int32, (16, length), 1)
    low = jnp.bitwise_and(token, 7)
    query_pair = pairs_ref[query_side : query_side + 1, :]
    extras = jnp.where(row < 8, jnp.where(row == query_pair, 1, 0), 0)
    extras = jnp.where(row == 8, token - low, extras)
    extras = jnp.where(row == 9, low, extras)
    extras = jnp.where(row == 10, 1, extras)
    extras = extras.astype(F32).astype(BF16)

    copies = []

    def scores_of(e):
        rows = slice(e * head, (e + 1) * head)
        placed_t = slot_matrix_t(position_t[:, e : e + 1])
        gathered = mm(jnp.concatenate([q_buf[rows], extras], axis=0), placed_t)
        slots = gathered.astype(BF16)
        slots_out[e, :head] = slots[:head]
        padded = jnp.concatenate(
            [slots, jnp.zeros((2 * head - slots.shape[0], CAPACITY), BF16)], axis=0
        )
        scores = mm(keys, padded)
        if causal:
            limit = (
                gathered[head + 8 : head + 9]
                + gathered[head + 9 : head + 10]
                + (1.0 - gathered[head + 10 : head + 11]) * length
            )
            key_at = lax.broadcasted_iota(jnp.int32, (length, CAPACITY), 0).astype(F32)
            scores = jnp.where(key_at <= limit, scores, MASKED)
        return scores

    ahead = scores_of(0)
    for e in range(experts):
        rows = slice(e * head, (e + 1) * head)
        scores = ahead
        if e + 1 < experts:
            ahead = scores_of(e + 1)
        top = jnp.max(scores, axis=0, keepdims=True)
        exponent = jnp.exp(scores - top)
        linv = 1.0 / jnp.sum(exponent, axis=0, keepdims=True)
        linv_out[e : e + 1] = linv
        exponent = exponent.astype(BF16)
        e_buf[e] = exponent
        copies.append(pltpu.make_async_copy(e_buf.at[e], e_out.at[e], sem.at[e]))
        copies[-1].start()
        attended = (mm(values_t, exponent) * linv).astype(BF16)
        slots_out[e, head:] = attended
        placed_rows = slot_matrix(position[e : e + 1])
        heads = mm(attended, placed_rows)
        heads_out[rows] = heads.astype(BF16)
        hw_buf[rows] = (heads * weights[e : e + 1]).astype(BF16)
    flush(heads_out)
    flush(slots_out)
    for at in range(0, length, length // 2):
        cols = slice(at, at + length // 2)
        branch = mm(output_ref[0], hw_buf[:, cols], TN)
        h_out[:, cols] = (h_out if from_rows else v_ref)[:, cols] + branch
        flush(h_out, (slice(None), cols))
    for copy in copies:
        copy.wait()


def attend_backward_kernel(layer, cross, gain_at, first, last, *refs):
    refs = list(refs)
    take = lambda count: [refs.pop(0) for _ in range(count)]
    (g_ref, gains_ref, codes_ref, tables_ref, linv_ref, slots_ref, heads_ref, kv_ref, output_ref,
     e_in) = take(10)
    experts, head = slots_ref.shape[0], slots_ref.shape[1] // 2
    width, length = g_ref.shape
    inner = experts * head
    finish = last == experts
    if first:
        d_in, kv_grad_in, hits_in = take(3)
    if finish:
        (x_ref,) = take(1)
        s_ref = take(1)[0] if cross else x_ref
        router_ref, query_ref, keyval_ref, feed_gain_ref = take(4)
        if first:
            (packed_in,) = take(1)
        (g_out,) = take(1)
        if cross:
            (s_out,) = take(1)
        (packed_out,) = take(1)
    else:
        d_out, kv_grad_out, hits_out, packed_out = take(4)
    e_buf, gt_buf, gl_buf, d_buf, hw_buf, sem = refs
    copies = []
    for e in range(first, last):
        copies.append(pltpu.make_async_copy(e_in.at[e], e_buf.at[e - first], sem.at[e - first]))
        copies[-1].start()
    position = tables_ref[0:experts]
    weights = tables_ref[experts : 2 * experts]
    position_t = position.T
    mine = slice(first * head, last * head)

    gl_buf[...] = g_ref[...].astype(BF16)
    gt_buf[...] = mm(output_ref[0, mine, :], gl_buf[...])
    keys_t = kv_ref[:head]
    values = kv_ref[head:].astype(F32).T.astype(BF16)
    weight_grads = []
    if first:
        key_grad, value_grad = kv_grad_in[:head], kv_grad_in[head:]
        d_buf[: first * head] = d_in[...]
        weight_grads.append(hits_in[:first])
    else:
        key_grad = jnp.zeros((head, length), F32)
        value_grad = jnp.zeros((head, length), F32)
    def probs_grad_of(e):
        rows = slice(e * head, (e + 1) * head)
        back = gt_buf[(e - first) * head : (e - first + 1) * head]
        weight_grads.append(jnp.sum(back * heads_ref[rows].astype(F32), axis=0, keepdims=True))
        heads_grad = (back * weights[e : e + 1]).astype(BF16)
        placed_t = slot_matrix_t(position_t[:, e : e + 1])
        slot_grad = (mm(heads_grad, placed_t) * linv_ref[e : e + 1]).astype(BF16)
        delta = jnp.sum(
            slot_grad.astype(F32) * slots_ref[e, head:].astype(F32), axis=0, keepdims=True
        )
        return slot_grad, delta, mm(values, slot_grad)

    ahead = probs_grad_of(first)
    for e in range(first, last):
        slot_grad, delta, probs_grad = ahead
        if e + 1 < last:
            ahead = probs_grad_of(e + 1)
        copies[e - first].wait()
        exponent = e_buf[e - first]
        scores_grad = (exponent.astype(F32) * (probs_grad - delta)).astype(BF16)
        query_grad = (mm(keys_t, scores_grad) * (head**-0.5)).astype(BF16)
        rows = slice(e * head, (e + 1) * head)
        d_buf[rows] = mm(query_grad, slot_matrix(position[e : e + 1])).astype(BF16)
        key_grad = key_grad + mm(slots_ref[e, :head], scores_grad, NT)
        value_grad = value_grad + mm(slot_grad, exponent, NT)

    out_columns = slice(inner, inner + width)
    if finish and first:
        packed_out[: first * head, out_columns] = packed_in[...]
    for e in range(first, last):
        rows = slice(e * head, (e + 1) * head)
        held = slice((e - first) * head, (e - first + 1) * head)
        hw_buf[held] = (heads_ref[rows].astype(F32) * weights[e : e + 1]).astype(BF16)
    out_grad = mm(hw_buf[...], gl_buf[...], NT).astype(BF16)
    if finish:
        packed_out[mine, out_columns] = out_grad
    else:
        packed_out[...] = out_grad
    weight_grad = jnp.concatenate(weight_grads, axis=0)
    if not finish:
        d_out[...] = d_buf[mine]
        kv_grad_out[:head] = key_grad
        kv_grad_out[head:] = value_grad
        hits_out[:last] = weight_grad
        hits_out[last:] = jnp.zeros((experts - last, length), F32)
        return

    d_buf[inner : inner + head] = key_grad.astype(BF16)
    d_buf[inner + head : inner + 2 * head] = value_grad.astype(BF16)
    hits, kept = route_hits(codes_ref, layer, experts)
    gates = [tables_ref[2 * experts + k : 2 * experts + k + 1] for k in range(2)]
    inverse = tables_ref[2 * experts + 2 : 2 * experts + 3]
    chosen = [
        jnp.sum(hit * weight_grad, axis=0, keepdims=True) * keep for hit, keep in zip(hits, kept)
    ]
    mean = gates[0] * chosen[0] + gates[1] * chosen[1]
    logit_grad = sum(
        gate * (item - mean) * hit for gate, item, hit in zip(gates, chosen, hits)
    ).astype(BF16)

    packed_out[:, :inner] = mm(x_ref[...], d_buf[:inner], NT).astype(BF16)
    kv_columns = slice(inner + width, inner + width + 2 * head)
    packed_out[:, kv_columns] = mm(s_ref[...], d_buf[inner:], NT).astype(BF16)
    padded = jnp.concatenate([logit_grad.astype(F32), jnp.zeros((120, length), F32)], axis=0)
    router_grad = mm(x_ref[...], padded.astype(BF16), NT)
    flush(packed_out, (slice(None), slice(0, kv_columns.stop)))

    grad = mm(query_ref[0], d_buf[:inner]) + mm(router_ref[0], logit_grad, TN)
    source_grad = mm(keyval_ref[0], d_buf[inner:])
    if cross:
        s_out[...] = source_grad
        flush(s_out)
    else:
        grad = grad + source_grad
    gain = gain_column(gains_ref, gain_at)
    back, gain_grad = normalize_back(grad, x_ref[...], inverse, gain)
    lane = lax.broadcasted_iota(jnp.int32, router_grad.shape, 1)
    extra = jnp.where(lane == experts, gain_grad, router_grad)
    extra = jnp.where(lane == experts + 1, feed_gain_ref[:, 0:1], extra)
    packed_out[:, kv_columns.stop :] = extra.astype(BF16)
    flush(packed_out, (slice(None), slice(kv_columns.stop, packed_out.shape[1])))
    total = g_ref[...] + back
    if cross:
        g_out[...] = total
    else:
        g_out[...] = total.T


def gelu_parts(values):
    half = 0.5 * (1.0 + lax.erf(values * ROOT_HALF))
    slope = half + values * jnp.exp(-0.5 * values * values) * INV_ROOT_TWO_PI
    return values * half, slope


def hidden_chunks(own, other, axis):
    size = own.shape[axis]
    found = []
    for part, ref in enumerate((own, other)):
        for at in range(0, size, FEED_CHUNK):
            found.append(
                (part, slice(at, at + FEED_CHUNK), slice(part * size + at, part * size + at + FEED_CHUNK))
            )
    return found


def feed_weight_grads(
    grad_low, by_rows, x_ref, wout_refs, hidden_ref, slope_ref, inner_ref, packed_refs
):
    width = x_ref.shape[0]
    size = wout_refs[0].shape[0]
    for part, here, there in reversed(hidden_chunks(wout_refs[0], wout_refs[1], 0)):
        grad = mm(wout_refs[part][here, :], grad_low, NT if by_rows else NN)
        inner = (grad * slope_ref[there].astype(F32)).astype(BF16)
        inner_ref[there] = inner
        packed = packed_refs[part]
        packed[:width, here] = mm(x_ref[...], inner, NT).astype(BF16)
        out_grad = mm(hidden_ref[there], grad_low, NN if by_rows else NT).astype(BF16)
        fold = here.start // (size // 2)
        at = width + here.start - fold * (size // 2)
        packed[at : at + FEED_CHUNK, fold * width : (fold + 1) * width] = out_grad
        flush(inner_ref, there)
        if here.start == 0:
            flush(packed)


def feed_rows_grad(win_refs, inner_ref):
    size = win_refs[0].shape[1]
    return mm(win_refs[0][...], inner_ref[:size]) + mm(win_refs[1][...], inner_ref[size:])


def feed_hidden(x, win_refs, hidden_ref, slope_ref):
    for part, here, there in hidden_chunks(win_refs[0], win_refs[1], 1):
        hidden, slope = gelu_parts(mm(win_refs[part][:, here], x, TN))
        hidden_ref[there] = hidden.astype(BF16)
        slope_ref[there] = slope.astype(BF16)
        flush(hidden_ref, there)
        flush(slope_ref, there)


def feed_result(wout_refs, hidden_ref):
    size = wout_refs[0].shape[0]
    return mm(wout_refs[0][...], hidden_ref[:size], TN) + mm(
        wout_refs[1][...], hidden_ref[size:], TN
    )


def feed_encoder_kernel(
    gain_at, h_ref, gains_ref, win_own, win_other, wout_own, wout_other,
    low_out, rows_out, x_out, inverse_out, hidden_out, slope_out,
):
    gain = gain_column(gains_ref, gain_at)
    scaled, inverse = normalize(h_ref[...])
    x_out[...] = (scaled * gain).astype(BF16)
    inverse_out[...] = inverse
    flush(x_out)
    feed_hidden(x_out[...], (win_own, win_other), hidden_out, slope_out)
    encoded = h_ref[...] + feed_result((wout_own, wout_other), hidden_out)
    low_out[...] = encoded.astype(BF16)
    rows_out[...] = encoded.T.astype(BF16)


def feed_encoder_weights_kernel(
    cot_ref, s_ref, x_ref, hidden_ref, slope_ref, wout_own, wout_other,
    g_out, inner_out, own_out, other_out, low_buf,
):
    g_out[...] = cot_ref[...].astype(F32).T + s_ref[...]
    low_buf[...] = g_out[...].astype(BF16)
    flush(g_out)
    feed_weight_grads(
        low_buf[...], False, x_ref, (wout_own, wout_other), hidden_ref, slope_ref, inner_out,
        (own_out, other_out),
    )


def feed_encoder_rows_kernel(
    gain_at, g_ref, gains_ref, x_ref, inverse_ref, inner_ref, win_own, win_other,
    g_out, gain_out,
):
    gain = gain_column(gains_ref, gain_at)
    grad = feed_rows_grad((win_own, win_other), inner_ref)
    back, gain_grad = normalize_back(grad, x_ref[...], inverse_ref[...], gain)
    g_out[...] = g_ref[...] + back
    gain_out[...] = jnp.broadcast_to(gain_grad, gain_out.shape)


def feed_decoder_weights_kernel(
    gain_at, h_ref, cot_ref, gains_ref, win_own, win_other, wout_own, wout_other,
    x_out, inverse_out, hidden_out, inner_out, own_out, other_out, slope_buf,
):
    gain = gain_column(gains_ref, gain_at)
    scaled, inverse = normalize(h_ref[...])
    x_out[...] = (scaled * gain).astype(BF16)
    inverse_out[...] = inverse
    flush(x_out)
    feed_hidden(x_out[...], (win_own, win_other), hidden_out, slope_buf)
    feed_weight_grads(
        cot_ref[...], True, x_out, (wout_own, wout_other), hidden_out, slope_buf, inner_out,
        (own_out, other_out),
    )


def feed_decoder_rows_kernel(
    gain_at, cot_ref, gains_ref, x_ref, inverse_ref, inner_ref, win_own, win_other,
    g_out, gain_out,
):
    gain = gain_column(gains_ref, gain_at)
    grad = feed_rows_grad((win_own, win_other), inner_ref)
    back, gain_grad = normalize_back(grad, x_ref[...], inverse_ref[...], gain)
    g_out[...] = cot_ref[...].astype(F32).T + back
    gain_out[...] = jnp.broadcast_to(gain_grad, gain_out.shape)


def feed_decoder_result_kernel(h_ref, hidden_ref, wout_own, wout_other, rows_out):
    result = h_ref[...] + feed_result((wout_own, wout_other), hidden_ref)
    rows_out[...] = result.T.astype(BF16)


def first_kernel(parts, *refs):
    refs = list(refs)
    take = lambda count: [refs.pop(0) for _ in range(count)]
    gains, codes, pairs = take(3)
    given = [take(5) for _ in parts]
    made = [take(8) for _ in parts]
    held = [take(4) for _ in parts]
    for part, ins, outs, scratch in zip(parts, given, made, held):
        attend_forward_kernel(*part, ins[0], gains, codes, pairs, *ins[1:], *outs, *scratch)


def middle_kernel(part, gain_b, gain_e, *refs):
    refs = list(refs)
    take = lambda count: [refs.pop(0) for _ in range(count)]
    gains, codes, pairs, h_ref, d_ref, cot_ref = take(6)
    mixture, feed_b, feed_e = take(4), take(4), take(4)
    encoder, cross = take(6), take(8)
    hidden_out, own_out, other_out, g_out, gain_out = take(5)
    held = take(4)
    x_buf, inverse_buf = refs
    feed_encoder_kernel(gain_b, h_ref, gains, *feed_b, *encoder)
    attend_forward_kernel(
        *part, d_ref, encoder[0], gains, codes, pairs, *mixture, *cross, *held
    )
    for ref in encoder[4:]:
        ref.finish()
    inner_buf, slope_buf = [ref.buffer for ref in encoder[4:]]
    feed_decoder_weights_kernel(
        gain_e, cross[0], cot_ref, gains, *feed_e,
        x_buf, inverse_buf, hidden_out, inner_buf, own_out, other_out, slope_buf,
    )
    feed_decoder_rows_kernel(
        gain_e, cot_ref, gains, x_buf, inverse_buf, inner_buf, *feed_e[:2], g_out, gain_out
    )


def feed_encoder_back_kernel(
    gain_at, cot_ref, s_ref, gains_ref, x_ref, inverse_ref, hidden_ref, slope_ref,
    wout_own, wout_other, win_own, win_other,
    g_out, own_out, other_out, gain_out, low_buf, g_buf, inner_buf,
):
    feed_encoder_weights_kernel(
        cot_ref, s_ref, x_ref, hidden_ref, slope_ref, wout_own, wout_other,
        g_buf, inner_buf, own_out, other_out, low_buf,
    )
    feed_encoder_rows_kernel(
        gain_at, g_buf, gains_ref, x_ref, inverse_ref, inner_buf, win_own, win_other,
        g_out, gain_out,
    )


def unpack_feed_kernel(pieces, place_ref, *refs):
    in_out, out_out, packed_ref = refs[-3:]
    width = in_out.shape[0]
    size = packed_ref.shape[0] // pieces
    packed_ref[: packed_ref.shape[0] // 2] = refs[0][0]
    packed_ref[packed_ref.shape[0] // 2 :] = refs[1][0]
    for piece in range(pieces):
        at = pl.multiple_of(jnp.bitwise_xor(place_ref[0], piece) * size, size)
        rows = packed_ref[pl.ds(at, size), :].astype(F32)
        if piece * size < width:
            in_out[piece * size : (piece + 1) * size] = rows
        else:
            at = piece * size - width
            out_out[at : at + size] = rows[:, :width]
            out_out[width + at : width + at + size] = rows[:, width:]


def unpack_mixture_kernel(pieces, place_ref, low_ref, high_ref, *refs):
    query_out, output_out, keyval_out, router_out, gains_out, extra, packed_ref = refs[-7:]
    size = packed_ref.shape[0] // pieces
    packed_ref[: packed_ref.shape[0] // 2] = low_ref[0]
    packed_ref[packed_ref.shape[0] // 2 :] = high_ref[0]
    inner, width = query_out.shape[1], output_out.shape[1]
    end = inner + width + keyval_out.shape[1]
    experts = router_out.shape[0]
    for piece in range(pieces):
        position = jnp.bitwise_xor(place_ref[0], piece)
        crossed = jnp.where(position >= pieces // 2, place_ref[1], 0)
        at = pl.multiple_of(jnp.bitwise_xor(position, crossed) * size, size)
        rows = packed_ref[pl.ds(at, size), :].astype(F32)
        there = slice(piece * size, (piece + 1) * size)
        query_out[there] = rows[:, :inner]
        output_out[there] = rows[:, inner : inner + width]
        keyval_out[there] = rows[:, inner + width : end]
        extra[there] = rows[:, end:]
    turned = extra[...].T
    router_out[...] = turned[:experts]
    gains_out[...] = turned[experts : experts + 8]


LEFT = "left"
WHOLE = "whole"
LARGE = 2**17


class Fetched:
    def __init__(self, source, buffer, sem):
        self.copy = pltpu.make_async_copy(source, buffer, sem)
        self.copy.start()
        self.buffer, self.shape, self.waits = buffer, buffer.shape, True

    def ready(self):
        if self.waits:
            self.copy.wait()
            self.waits = False
        return self.buffer

    def __getitem__(self, at):
        return self.ready()[at]


class Stored:
    def __init__(self, place, buffer, sems):
        self.place, self.buffer, self.sems = place, buffer, sems
        self.shape = buffer.shape
        self.copies = []
        self.finished = False

    def __getitem__(self, at):
        return self.buffer[at]

    def __setitem__(self, at, value):
        self.buffer[at] = value

    def flush(self, at=None):
        source, place = self.buffer, self.place
        if at is not None:
            source, place = source.at[at], place.at[at]
        self.copies.append(pltpu.make_async_copy(source, place, self.sems.at[len(self.copies)]))
        self.copies[-1].start()

    def finish(self):
        if self.finished:
            return
        if not self.copies:
            self.flush()
        for copy in self.copies:
            copy.wait()
        self.finished = True


def flush(ref, at=None):
    if isinstance(ref, Stored):
        ref.flush(at)


FLUSHES = 8


def layer_spec(array, layer):
    return (layer, True)


def call(kernel, name, outs, args, in_specs, out_specs, scratch, flops, limit=VMEM_LIMIT):
    shapes = [jax.ShapeDtypeStruct(shape, dtype) for shape, dtype in outs]
    ins, buffers = [], []
    for item, spec in zip(args, in_specs):
        shape = item.shape
        if isinstance(spec, tuple):
            shape = ((1,) if spec[1] else ()) + item.shape[1:]
        size = item.dtype.itemsize
        for extent in shape:
            size *= extent
        mine = isinstance(spec, tuple) or (spec == WHOLE and size >= LARGE)
        ins.append(spec if mine else None)
        if mine:
            buffers.append(pltpu.VMEM(shape, item.dtype))
    stored = [
        spec == WHOLE and item.size * item.dtype.itemsize >= LARGE
        for item, spec in zip(shapes, out_specs)
    ]
    buffers += [pltpu.VMEM(item.shape, item.dtype) for item, mine in zip(shapes, stored) if mine]
    count = len(buffers)
    fetched = sum(item is not None for item in ins)

    def wrapped(*refs):
        refs = list(refs)
        given, made = refs[: len(ins)], refs[len(ins) : len(ins) + len(shapes)]
        rest = refs[len(ins) + len(shapes) :]
        own, held, sems_in, sems_out = rest[: len(scratch)], rest[len(scratch) : -2], rest[-2], rest[-1]
        used = 0
        for k, spec in enumerate(ins):
            if spec is not None:
                source = given[k]
                if isinstance(spec, tuple):
                    source = source.at[pl.ds(spec[0], 1)] if spec[1] else source.at[spec[0]]
                given[k] = Fetched(source, held[used], sems_in.at[used])
                used += 1
        for k, mine in enumerate(stored):
            if mine:
                made[k] = Stored(made[k], held[used], sems_out.at[used - fetched])
                used += 1
        kernel(*given, *made, *own)
        for item in given:
            if isinstance(item, Fetched):
                item.ready()
        for item in made:
            if isinstance(item, Stored):
                item.finish()

    moved = sum(a.size * a.dtype.itemsize for a in args) + sum(
        s.size * s.dtype.itemsize for s in shapes
    )
    vmem, hbm = pl.BlockSpec(memory_space=pltpu.VMEM), pl.BlockSpec(memory_space=pl.ANY)
    return pl.pallas_call(
        wrapped,
        name=name,
        out_shape=shapes,
        in_specs=[hbm if k is not None or s == LEFT else vmem for k, s in zip(ins, in_specs)],
        out_specs=[hbm if k or s == LEFT else vmem for k, s in zip(stored, out_specs)],
        scratch_shapes=list(scratch) + buffers + [
            pltpu.SemaphoreType.DMA((max(fetched, 1),)),
            pltpu.SemaphoreType.DMA((max(count - fetched, 1), FLUSHES)),
        ],
        compiler_params=pltpu.CompilerParams(vmem_limit_bytes=limit),
        cost_estimate=pl.CostEstimate(flops=30 * flops, bytes_accessed=moved, transcendentals=0),
    )(*args)


def body(
    source, target, routes, overflow, pairs, gains, router, query, keyval, output,
    ffn_in, ffn_out, cot_source, cot_target,
):
    _, length, width = source.shape
    experts = router.shape[2]
    head = keyval.shape[2] // 2
    inner = experts * head
    hidden = ffn_in.shape[2] * lax.axis_size("ffn")
    router = jnp.transpose(router, (0, 2, 1))
    codes = jnp.transpose(routes[0] + experts * overflow[0], (0, 2, 1))
    pair_rows = pairs[0]
    swap = [(0, 1), (1, 0)]
    win_other = lax.ppermute(ffn_in, "ffn", swap)
    wout_other = lax.ppermute(ffn_out, "ffn", swap)

    def layer_args(layer):
        arrays = (router, query, keyval, output)
        return arrays, [layer_spec(item, layer) for item in arrays]

    attend_outs = [
        ((width, length), F32),
        ((width, length), BF16),
        ((3 * experts, length), F32),
        ((experts, length, CAPACITY), BF16),
        ((experts, CAPACITY), F32),
        ((experts, 2 * head, CAPACITY), BF16),
        ((inner, length), BF16),
        ((2 * head, length), BF16),
    ]
    attend_specs = [WHOLE] * 3 + [LEFT] + [WHOLE] * 4
    attend_scratch = [
        pltpu.VMEM((experts, length, CAPACITY), BF16),
        pltpu.VMEM((inner, length), BF16),
        pltpu.VMEM((inner, length), BF16),
        pltpu.SemaphoreType.DMA((experts,)),
    ]

    def attend_back(layer, gain_at, grad, saved, keys, feed_gain):
        cross = keys is not None
        _, normed, tables, exponents, linv, slots, heads, kv = saved
        arrays, specs = layer_args(layer)
        args = [grad, gains, codes, tables, linv, slots, heads, kv, output, exponents, normed]
        args += ([keys] if cross else []) + list(arrays[:3]) + [feed_gain]
        arg_specs = [WHOLE] * 8 + [specs[3], LEFT] + [WHOLE] * (2 if cross else 1)
        arg_specs += specs[:3] + [WHOLE]
        outs = [((width, length) if cross else (length, width), F32)]
        outs += [((width, length), F32)] if cross else []
        outs += [((width, inner + width + 2 * head + 128), BF16)]
        return call(
            functools.partial(attend_backward_kernel, layer, cross, gain_at, 0, experts),
            f"attend_back{layer}", outs, args, arg_specs, [WHOLE] * len(outs),
            [
                pltpu.VMEM((experts, length, CAPACITY), BF16),
                pltpu.VMEM((inner, length), F32),
                pltpu.VMEM((width, length), BF16),
                pltpu.VMEM((inner + 2 * head, length), BF16),
                pltpu.VMEM((inner, length), BF16),
                pltpu.SemaphoreType.DMA((experts,)),
            ],
            13 * 10**9,
        )

    def half_spec(array, index):
        return (index, False)

    def ffn_args(index):
        arrays = [ffn_in, win_other, ffn_out, wout_other]
        return arrays, [half_spec(item, index) for item in arrays]

    travelling = []

    def boundary(values):
        going = [(item, item.work()) for item in travelling]
        going = [(item, work) for item, work in going if work is not None]
        works = [work for _, work in going if work[1]]
        made = fold(works) if works else []
        ended = [item for item in travelling if item.work() is None and not item.ended]
        brought = [item.inputs for item in ended]
        values, made, brought = lax.optimization_barrier((values, made, brought))
        for item, item.inputs in zip(ended, brought):
            item.ended = True
        for item, work in going:
            item.send(made.pop(0) if work[1] else None)
        return values, not all(item.ended for item in travelling)

    last_made = []

    def event(values, items):
        going = [(item, item.work()) for item in items if item.work() is not None]
        works = [work for _, work in going]
        ended = [item for item in items if item.work() is None and not item.ended]
        tied = (values, [work[1] for work in works], [item.inputs for item in ended], last_made)
        values, inputs, brought, _ = lax.optimization_barrier(tied)
        for item, item.inputs in zip(ended, brought):
            item.ended = True
        if works:
            made = fold([(work[0], given, work[2]) for work, given in zip(works, inputs)])
            last_made[:] = [arrays[0] for arrays in made]
            for (item, _), arrays in zip(going, made):
                item.send(arrays)
        return values

    packed_shape = (2 * width, hidden // 2)
    common = [gains, codes, pair_rows]
    layers = [layer_args(layer) for layer in range(3)]
    parts = [(0, False, False, True, 0, 0, 0), (1, True, False, True, 1, 1, 2)]
    saved = call(
        functools.partial(first_kernel, parts), "attend_self", attend_outs * 2,
        common + [source[0], *layers[0][0], target[0], *layers[1][0]],
        [WHOLE] * 3 + [WHOLE, *layers[0][1], WHOLE, *layers[1][1]],
        attend_specs * 2, attend_scratch * 2, 16 * 10**9,
    )
    saved_a, saved_c = saved[:8], saved[8:]
    feed_args = [ffn_args(0), ffn_args(1)]
    made = call(
        functools.partial(middle_kernel, (2, False, True, False, 1, 0, 3), 1, 4), "middle",
        [
            ((width, length), BF16), ((length, width), BF16), ((width, length), BF16),
            ((1, length), F32), ((hidden, length), BF16), ((hidden, length), BF16),
        ] + attend_outs + [
            ((hidden, length), BF16), (packed_shape, BF16), (packed_shape, BF16),
            ((width, length), F32), ((width, 128), F32),
        ],
        common + [saved_a[0], saved_c[0], cot_target[0], *layers[2][0]]
        + feed_args[0][0] + feed_args[1][0],
        [WHOLE] * 6 + layers[2][1] + feed_args[0][1] + feed_args[1][1],
        [WHOLE] * 6 + attend_specs + [WHOLE] * 5,
        attend_scratch + [pltpu.VMEM((width, length), BF16), pltpu.VMEM((1, length), F32)],
        28 * 10**9, MIDDLE_VMEM,
    )
    encoded_low, encoded_rows, normed_b, inverse_b, hidden_b, slope_b = made[:6]
    saved_d = made[6:14]
    hidden_e, own_e, other_e, grad_e, gain_e = made[14:]
    feed_e = Exchange([own_e[None]], other_e[None], 3)
    travelling.append(feed_e)
    grad_e, _ = boundary(grad_e)
    grad_d, source_grad, packed_d = attend_back(2, 3, grad_e, saved_d, encoded_low, gain_e)
    source_grad, _ = boundary(source_grad)
    weights, weight_specs = feed_args[0]
    grad_b, own_b, other_b, gain_b = call(
        functools.partial(feed_encoder_back_kernel, 1), "feed_encoder_back",
        [((width, length), F32), (packed_shape, BF16), (packed_shape, BF16), ((width, 128), F32)],
        [cot_source[0], source_grad, gains, normed_b, inverse_b, hidden_b, slope_b]
        + weights[2:] + weights[:2],
        [WHOLE] * 7 + weight_specs[2:] + weight_specs[:2], [WHOLE] * 4,
        [
            pltpu.VMEM((width, length), BF16), pltpu.VMEM((width, length), F32),
            pltpu.VMEM((hidden, length), BF16),
        ],
        10 * 10**9,
    )
    feed_b = Exchange([own_b[None]], other_b[None], 3)
    travelling.append(feed_b)
    (grad_d, grad_b), _ = boundary((grad_d, grad_b))
    grad_target, packed_c = attend_back(1, 2, grad_d, saved_c, None, gain_b)
    mixture_dc = Exchange([packed_c[None], packed_d[None]], scattered=3)
    travelling.append(mixture_dc)
    grad_b, _ = boundary(grad_b)
    grad_source, packed_a = attend_back(0, 0, grad_b, saved_a, None, gain_b)
    mixture_a = Exchange([packed_a[None]], scattered=3)
    travelling.append(mixture_a)
    hidden_e, _ = boundary(hidden_e)
    (decoded_rows,) = call(
        feed_decoder_result_kernel, "feed_decoder_result", [((length, width), BF16)],
        [saved_d[0], hidden_e] + ffn_args(1)[0][2:], [WHOLE] * 2 + ffn_args(1)[1][2:], [WHOLE], [],
        3 * 10**9,
    )

    def unpack_feed(exchange, index, made):
        pieces = exchange.pieces
        shapes = [
            jax.ShapeDtypeStruct((2,) + item.shape[1:], F32) for item in (ffn_in, ffn_out)
        ]
        spec = lambda item: pl.BlockSpec(
            (None,) + item.shape[1:], lambda i: (index, 0, 0), pipeline_mode=pl.Buffered(1)
        )
        return pl.pallas_call(
            functools.partial(unpack_feed_kernel, pieces), name="unpack_feed", grid=(1,),
            out_shape=shapes,
            in_specs=[pl.BlockSpec(memory_space=pltpu.SMEM)] + [pl.BlockSpec(memory_space=pltpu.VMEM)] * 2
            + [pl.BlockSpec(memory_space=pl.ANY)] * len(made),
            out_specs=[spec(item) for item in shapes],
            scratch_shapes=[pltpu.VMEM(packed_shape, BF16)],
            input_output_aliases={3 + k: k for k in range(len(made))},
            compiler_params=pltpu.CompilerParams(vmem_limit_bytes=VMEM_LIMIT),
            cost_estimate=pl.CostEstimate(flops=10**11, bytes_accessed=10**6, transcendentals=0),
        )(exchange.place, *exchange.inputs, *made)

    def unpack_mixture(exchange, first, made):
        layers = exchange.inputs[0].shape[0]
        columns = (inner, width, 2 * head)
        shapes = [jax.ShapeDtypeStruct((3, width, size), F32) for size in columns]
        shapes += [jax.ShapeDtypeStruct((3, rows, width), F32) for rows in (experts, 8)]
        return pl.pallas_call(
            functools.partial(unpack_mixture_kernel, exchange.pieces), name="unpack_mixture",
            grid=(layers,),
            out_shape=shapes,
            in_specs=[
                pl.BlockSpec(memory_space=pltpu.SMEM),
            ] + [
                pl.BlockSpec((1,) + item.shape[1:], lambda i: (i, 0, 0)) for item in exchange.inputs
            ] + [pl.BlockSpec(memory_space=pl.ANY)] * len(made),
            out_specs=[
                pl.BlockSpec((None,) + item.shape[1:], lambda i: (first + i, 0, 0))
                for item in shapes
            ],
            scratch_shapes=[
                pltpu.VMEM((width, 128), F32),
                pltpu.VMEM((width,) + exchange.inputs[0].shape[2:], BF16),
            ],
            input_output_aliases={3 + k: k for k in range(len(made))},
            compiler_params=pltpu.CompilerParams(vmem_limit_bytes=VMEM_LIMIT),
            cost_estimate=pl.CostEstimate(flops=10**11, bytes_accessed=10**6, transcendentals=0),
        )(exchange.place, *exchange.inputs, *made)

    unpacks = [
        (feed_e, unpack_feed, 1), (feed_b, unpack_feed, 0),
        (mixture_dc, unpack_mixture, 1), (mixture_a, unpack_mixture, 0),
    ]
    unpacked = {unpack_feed: [], unpack_mixture: []}
    groups = [[feed_e, feed_b], [mixture_dc, mixture_a]]
    held = [decoded_rows, [], []]
    order = [0, 1, 0, 1, 0, 1, 0, 1, 1, 0, 1, 1, 0, 1]
    while unpacks:
        for group in [groups[k] for k in order]:
            if not all(item.ended for item in group):
                held = event(held, group)
            for item in unpacks:
                exchange, unpack, index = item
                if exchange.ended:
                    at = 1 + (unpack is unpack_mixture)
                    held[at] = unpack(exchange, index, held[at])
                    unpacks.remove(item)
                    break
    decoded_rows, grads_ffn, merged = held
    gain_rows = merged[4][:, :2].reshape(6, width)
    grad_gains = jnp.concatenate([gain_rows[:3], gain_rows[4:]], axis=0)
    return (
        encoded_rows[None],
        decoded_rows[None],
        grad_source[None],
        grad_target[None],
        grad_gains,
        jnp.transpose(merged[3], (0, 2, 1)),
        merged[0],
        merged[2],
        merged[1],
        grads_ffn[0],
        grads_ffn[1],
    )


DOWN = ("halve", "stack")


class Exchange:
    def __init__(self, arrays, other=None, scattered=3):
        devices, columns = lax.axis_size("batch"), lax.axis_size("ffn")
        batch, column = lax.axis_index("batch"), lax.axis_index("ffn")
        across = [
            (b * columns + c, b * columns + (c ^ 1)) for b in range(devices) for c in range(columns)
        ]
        split = other is None
        steps = [(across, column.astype(jnp.int32))] if split else []
        beside = []
        bits = [1 << k for k in range(devices.bit_length() - 1)]
        orders = [bits, bits[1::-1] + bits[2:]]
        for level in range(len(bits)):
            choice = [orders[c % 2][level] for c in range(columns)]
            pairs = [
                (b * columns + c, (b ^ choice[c]) * columns + c)
                for b in range(devices) for c in range(columns)
            ]
            bit = jnp.where(column % 2 == 0, choice[0], choice[1])
            steps.append((pairs, (jnp.bitwise_and(batch, bit) != 0).astype(jnp.int32)))
            bit = jnp.where(column % 2 == 0, choice[-1], choice[0])
            beside.append((jnp.bitwise_and(batch, bit) != 0).astype(jnp.int32))
        down = scattered + int(split)
        self.pieces = 1 << down
        place = jnp.int32(0)
        for _, upper in steps[:down]:
            place = place * 2 + upper
        own = other_place = jnp.int32(0)
        for (_, upper), upper_beside in zip(steps[int(split) : down], beside):
            own = own * 2 + upper
            other_place = other_place * 2 + upper_beside
        self.place = jnp.stack([place, jnp.bitwise_xor(own, other_place)])
        self.plan = [] if split else [("send", across, None)]
        self.plan += [("halve", pairs, upper) for pairs, upper in steps[:down]]
        if split and len(arrays) > 1:
            self.plan[0] = ("stack",) + self.plan[0][1:]
        self.plan += [("add", pairs, None) for pairs, _ in steps[down:]]
        self.plan += [
            ("join" if k else "add", pairs, None)
            for k, (pairs, _) in enumerate(reversed(steps[:down]))
        ]
        self.at = 0
        self.ended = False
        self.inputs = arrays
        if not split:
            self.kept, self.sent = arrays[0], other

    def work(self):
        if self.at == len(self.plan):
            return None
        kind, _, upper = self.plan[self.at]
        if kind == "send":
            return kind, [], None
        return kind, self.inputs, upper

    def send(self, made):
        _, pairs, _ = self.plan[self.at]
        self.at += 1
        if made:
            self.kept, self.sent = made[0], made[-1]
        self.inputs = [self.kept, lax.ppermute(self.sent, ("batch", "ffn"), pairs)]


def fold_kernel(works, uppers_ref, *refs):
    refs = list(refs)
    take = lambda count: [refs.pop(0) for _ in range(count)]
    inputs = [take(count) for _, count, _, _ in works]
    outputs = [take(1 + (kind in DOWN)) for kind, _, _, _ in works]
    buffers = [take(count) for _, _, _, count in works]
    sems_in, sems_out = refs
    at_in, started = 0, []

    def copy_in(source, target):
        nonlocal at_in
        copy = pltpu.make_async_copy(source, target, sems_in.at[at_in])
        copy.start()
        at_in += 1
        return copy

    at_out = 0

    def copy_out(source, target):
        nonlocal at_out
        copy = pltpu.make_async_copy(source, target, sems_out.at[at_out])
        copy.start()
        at_out += 1
        started.append(copy)

    waits = []
    for at, ((kind, count, rows, _), given, made, held) in enumerate(
        zip(works, inputs, outputs, buffers)
    ):
        copies = []
        if kind in DOWN:
            half = rows // 2
            upper = uppers_ref[at]
            for side, part in enumerate((upper, 1 - upper)):
                there = pl.ds(pl.multiple_of(part * half, half), half)
                for k, source in enumerate(given):
                    if kind == "stack":
                        target = held[side].at[k : k + 1]
                    else:
                        target = held[side * count + k]
                    copies.append(copy_in(source.at[:, there, :], target))
        elif kind == "add":
            for k, source in enumerate(given):
                copies.append(copy_in(source, held[k]))
        else:
            for k, source in enumerate(given):
                copies.append(copy_in(source, held[0].at[:, k * rows : (k + 1) * rows, :]))
        waits.append(copies)
    for (kind, count, rows, _), made, held, copies in zip(works, outputs, buffers, waits):
        for copy in copies:
            copy.wait()
        for side, target in enumerate(made):
            each = 1 if kind == "stack" else count
            part = held[side * each : (side + 1) * each]
            if kind in ("halve", "add") and count == 2:
                part[0][...] = part[0][...] + part[1][...]
            copy_out(part[0], target)
    for copy in started:
        copy.wait()


def fold(works):
    plans, args, outs, scratch, uppers = [], [], [], [], []
    copies_in = copies_out = 0
    for kind, inputs, upper in works:
        layers, rows, columns = inputs[0].shape
        if kind == "stack":
            layers *= len(inputs)
        made = rows // 2 if kind in DOWN else {"add": rows, "join": 2 * rows}[kind]
        sides = 1 + (kind in DOWN)
        held = {"join": 1, "stack": 2}.get(kind, sides * len(inputs))
        plans.append((kind, len(inputs), rows, held))
        args += inputs
        outs += [jax.ShapeDtypeStruct((layers, made, columns), inputs[0].dtype)] * sides
        scratch += [pltpu.VMEM((layers, made, columns), inputs[0].dtype)] * held
        copies_in += sides * len(inputs)
        copies_out += sides
        uppers.append(jnp.int32(0) if upper is None else upper)
    hbm = pl.BlockSpec(memory_space=pl.ANY)
    results = pl.pallas_call(
        functools.partial(fold_kernel, plans),
        name="fold",
        out_shape=outs,
        in_specs=[pl.BlockSpec(memory_space=pltpu.SMEM)] + [hbm] * len(args),
        out_specs=[hbm] * len(outs),
        scratch_shapes=scratch + [
            pltpu.SemaphoreType.DMA((copies_in,)), pltpu.SemaphoreType.DMA((copies_out,)),
        ],
        compiler_params=pltpu.CompilerParams(vmem_limit_bytes=VMEM_LIMIT),
        cost_estimate=pl.CostEstimate(flops=10**11, bytes_accessed=10**6, transcendentals=0),
    )(jnp.stack(uppers), *args)
    found, at = [], 0
    for kind, _, _, _ in plans:
        sides = 1 + (kind in DOWN)
        found.append(list(results[at : at + sides]))
        at += sides
    return found


def solution(mesh):
    tokens = P(("batch", "ffn"), None, None)
    return jax.shard_map(
        body,
        mesh=mesh,
        in_specs=(
            tokens, tokens, P(("batch", "ffn"), None, None, None),
            P(("batch", "ffn"), None, None, None), tokens,
            P(), P(), P(), P(), P(),
            P(None, None, "ffn"), P(None, "ffn", None), tokens, tokens,
        ),
        out_specs=(
            tokens, tokens, tokens, tokens,
            P(), P(), P(), P(), P(),
            P(None, None, "ffn"), P(None, "ffn", None),
        ),
        check_vma=False,
    )
```

```python
import functools

import jax
import jax.numpy as jnp
from jax import lax
from jax.experimental import pallas as pl
from jax.experimental.pallas import tpu as pltpu
from jax.sharding import PartitionSpec as P

CAPACITY = 256
EPSILON = 1e-05
MASKED = -1000000000.0
PENALTY = -(2.0**30)
ROOT_HALF = 0.7071067811865476
INV_ROOT_TWO_PI = 0.3989422804014327
F32 = jnp.float32
BF16 = jnp.bfloat16
NN = ((1,), (0,))
NT = ((1,), (1,))
TN = ((0,), (0,))
CHUNK = 256
FEED_CHUNK = 512
VMEM_LIMIT = 52 * 2**20
MIDDLE_VMEM = 58 * 2**20


def mm(left, right, dims=NN):
    return lax.dot_general(left, right, (dims, ((), ())), preferred_element_type=F32)


def normalize(values):
    centered = values - jnp.mean(values, axis=0, keepdims=True)
    inverse = lax.rsqrt(jnp.mean(centered * centered, axis=0, keepdims=True) + EPSILON)
    return centered * inverse, inverse


def normalize_back(grad, normed, inverse, gain):
    scaled = normed.astype(F32) * (1.0 / gain)
    gain_grad = jnp.sum(grad * scaled, axis=1, keepdims=True)
    grad_scaled = grad * gain
    back = inverse * (
        grad_scaled
        - jnp.mean(grad_scaled, axis=0, keepdims=True)
        - scaled * jnp.mean(grad_scaled * scaled, axis=0, keepdims=True)
    )
    return back, gain_grad


def gain_column(gains_ref, at):
    row = gains_ref[at : at + 1, :]
    return jnp.broadcast_to(row, (8, row.shape[1])).T[:, 0:1]


def column_to_row(column):
    return jnp.broadcast_to(column, (column.shape[0], 128)).T[0:1]


def route_hits(codes_ref, layer, experts):
    length = codes_ref.shape[2]
    expert = lax.broadcasted_iota(jnp.int32, (experts, length), 0)
    hits, kept = [], []
    for pick in range(2):
        code = codes_ref[layer, pick : pick + 1, :]
        dropped = code >= experts
        route = jnp.where(dropped, code - experts, code)
        hits.append(jnp.where(expert == route, 1.0, 0.0))
        kept.append(jnp.where(dropped, 0.0, 1.0))
    return hits, kept


def prefix_before(values):
    length = values.shape[1]
    lane = lax.broadcasted_iota(jnp.int32, values.shape, 1)
    total = values
    step = 1
    while step < length:
        total = total + jnp.where(lane >= step, pltpu.roll(total, step, 1), 0.0)
        step *= 2
    return total - values


def slot_matrix(position_row):
    slot = lax.broadcasted_iota(jnp.int32, (CAPACITY, position_row.shape[1]), 0).astype(F32)
    return jnp.where(slot == position_row, 1.0, 0.0).astype(BF16)


def slot_matrix_t(position_column):
    slot = lax.broadcasted_iota(jnp.int32, (position_column.shape[0], CAPACITY), 1).astype(F32)
    return jnp.where(slot == position_column, 1.0, 0.0).astype(BF16)


def attend_forward_kernel(
    layer, causal, cross, from_rows, query_side, key_side, gain_at, *refs
):
    if cross:
        (v_ref, s_ref, gains_ref, codes_ref, pairs_ref, router_ref, query_ref, keyval_ref,
         output_ref, h_out, x_out, tables_out, e_out, linv_out, slots_out, heads_out, kv_out,
         e_buf, q_buf, hw_buf, sem) = refs
    else:
        (v_ref, gains_ref, codes_ref, pairs_ref, router_ref, query_ref, keyval_ref,
         output_ref, h_out, x_out, tables_out, e_out, linv_out, slots_out, heads_out, kv_out,
         e_buf, q_buf, hw_buf, sem) = refs
        s_ref = x_out
    width, length = x_out.shape
    experts = router_ref.shape[1]
    head = keyval_ref.shape[2] // 2
    gain = gain_column(gains_ref, gain_at)
    inverses = []
    for at in range(0, length, CHUNK):
        cols = slice(at, at + CHUNK)
        part = v_ref[cols, :].astype(F32).T if from_rows else v_ref[:, cols]
        scaled, inverse = normalize(part)
        x_out[:, cols] = (scaled * gain).astype(BF16)
        inverses.append(inverse)
        if from_rows:
            h_out[:, cols] = part
    inverse = jnp.concatenate(inverses, axis=1)
    flush(x_out)

    hits, kept = route_hits(codes_ref, layer, experts)
    rank = prefix_before(hits[0] + hits[1])
    placed = hits[0] * kept[0] + hits[1] * kept[1]
    position = jnp.where(placed > 0.0, rank, -1.0)
    position_t = position.T

    normed = x_out[...]
    logits = mm(router_ref[0], normed)
    picked = [jnp.sum(hit * logits, axis=0, keepdims=True) for hit in hits]
    top = jnp.maximum(picked[0], picked[1])
    raised = [jnp.exp(item - top) for item in picked]
    total = raised[0] + raised[1]
    gates = [item / total for item in raised]
    weights = gates[0] * kept[0] * hits[0] + gates[1] * kept[1] * hits[1]
    tables_out[...] = jnp.concatenate(
        [position, weights, gates[0], gates[1], inverse, jnp.zeros((5, length), F32)], axis=0
    )

    q_buf[...] = (mm(query_ref[0], normed, TN) * (head**-0.5)).astype(BF16)
    kv = mm(keyval_ref[0], s_ref[...], TN).astype(BF16)
    kv_out[...] = kv
    values_t = kv[head:]
    row = lax.broadcasted_iota(jnp.int32, (head, length), 0)
    key_pair = pairs_ref[key_side : key_side + 1, :]
    penalties = jnp.where((row < 8) & (row != key_pair), PENALTY, 0.0)
    keys = jnp.concatenate([kv[:head].astype(F32), penalties], axis=0).T.astype(BF16)
    row = lax.broadcasted_iota(jnp.int32, (16, length), 0)
    token = lax.broadcasted_iota(jnp.int32, (16, length), 1)
    low = jnp.bitwise_and(token, 7)
    query_pair = pairs_ref[query_side : query_side + 1, :]
    extras = jnp.where(row < 8, jnp.where(row == query_pair, 1, 0), 0)
    extras = jnp.where(row == 8, token - low, extras)
    extras = jnp.where(row == 9, low, extras)
    extras = jnp.where(row == 10, 1, extras)
    extras = extras.astype(F32).astype(BF16)

    copies = []

    def scores_of(e):
        rows = slice(e * head, (e + 1) * head)
        placed_t = slot_matrix_t(position_t[:, e : e + 1])
        gathered = mm(jnp.concatenate([q_buf[rows], extras], axis=0), placed_t)
        slots = gathered.astype(BF16)
        slots_out[e, :head] = slots[:head]
        padded = jnp.concatenate(
            [slots, jnp.zeros((2 * head - slots.shape[0], CAPACITY), BF16)], axis=0
        )
        scores = mm(keys, padded)
        if causal:
            limit = (
                gathered[head + 8 : head + 9]
                + gathered[head + 9 : head + 10]
                + (1.0 - gathered[head + 10 : head + 11]) * length
            )
            key_at = lax.broadcasted_iota(jnp.int32, (length, CAPACITY), 0).astype(F32)
            scores = jnp.where(key_at <= limit, scores, MASKED)
        return scores

    ahead = scores_of(0)
    for e in range(experts):
        rows = slice(e * head, (e + 1) * head)
        scores = ahead
        if e + 1 < experts:
            ahead = scores_of(e + 1)
        top = jnp.max(scores, axis=0, keepdims=True)
        exponent = jnp.exp(scores - top)
        linv = 1.0 / jnp.sum(exponent, axis=0, keepdims=True)
        linv_out[e : e + 1] = linv
        exponent = exponent.astype(BF16)
        e_buf[e] = exponent
        copies.append(pltpu.make_async_copy(e_buf.at[e], e_out.at[e], sem.at[e]))
        copies[-1].start()
        attended = (mm(values_t, exponent) * linv).astype(BF16)
        slots_out[e, head:] = attended
        placed_rows = slot_matrix(position[e : e + 1])
        heads = mm(attended, placed_rows)
        heads_out[rows] = heads.astype(BF16)
        hw_buf[rows] = (heads * weights[e : e + 1]).astype(BF16)
    flush(heads_out)
    flush(slots_out)
    for at in range(0, length, length // 2):
        cols = slice(at, at + length // 2)
        branch = mm(output_ref[0], hw_buf[:, cols], TN)
        h_out[:, cols] = (h_out if from_rows else v_ref)[:, cols] + branch
        flush(h_out, (slice(None), cols))
    for copy in copies:
        copy.wait()


def attend_backward_kernel(layer, cross, gain_at, first, last, *refs):
    refs = list(refs)
    take = lambda count: [refs.pop(0) for _ in range(count)]
    (g_ref, gains_ref, codes_ref, tables_ref, linv_ref, slots_ref, heads_ref, kv_ref, output_ref,
     e_in) = take(10)
    experts, head = slots_ref.shape[0], slots_ref.shape[1] // 2
    width, length = g_ref.shape
    inner = experts * head
    finish = last == experts
    if first:
        d_in, kv_grad_in, hits_in = take(3)
    if finish:
        (x_ref,) = take(1)
        s_ref = take(1)[0] if cross else x_ref
        router_ref, query_ref, keyval_ref, feed_gain_ref = take(4)
        if first:
            (packed_in,) = take(1)
        (g_out,) = take(1)
        if cross:
            (s_out,) = take(1)
        (packed_out,) = take(1)
    else:
        d_out, kv_grad_out, hits_out, packed_out = take(4)
    e_buf, gt_buf, gl_buf, d_buf, hw_buf, sem = refs
    copies = []
    for e in range(first, last):
        copies.append(pltpu.make_async_copy(e_in.at[e], e_buf.at[e - first], sem.at[e - first]))
        copies[-1].start()
    position = tables_ref[0:experts]
    weights = tables_ref[experts : 2 * experts]
    position_t = position.T
    mine = slice(first * head, last * head)

    gl_buf[...] = g_ref[...].astype(BF16)
    gt_buf[...] = mm(output_ref[0, mine, :], gl_buf[...])
    keys_t = kv_ref[:head]
    values = kv_ref[head:].astype(F32).T.astype(BF16)
    weight_grads = []
    if first:
        key_grad, value_grad = kv_grad_in[:head], kv_grad_in[head:]
        d_buf[: first * head] = d_in[...]
        weight_grads.append(hits_in[:first])
    else:
        key_grad = jnp.zeros((head, length), F32)
        value_grad = jnp.zeros((head, length), F32)
    def probs_grad_of(e):
        rows = slice(e * head, (e + 1) * head)
        back = gt_buf[(e - first) * head : (e - first + 1) * head]
        weight_grads.append(jnp.sum(back * heads_ref[rows].astype(F32), axis=0, keepdims=True))
        heads_grad = (back * weights[e : e + 1]).astype(BF16)
        placed_t = slot_matrix_t(position_t[:, e : e + 1])
        slot_grad = (mm(heads_grad, placed_t) * linv_ref[e : e + 1]).astype(BF16)
        delta = jnp.sum(
            slot_grad.astype(F32) * slots_ref[e, head:].astype(F32), axis=0, keepdims=True
        )
        return slot_grad, delta, mm(values, slot_grad)

    ahead = probs_grad_of(first)
    for e in range(first, last):
        slot_grad, delta, probs_grad = ahead
        if e + 1 < last:
            ahead = probs_grad_of(e + 1)
        copies[e - first].wait()
        exponent = e_buf[e - first]
        scores_grad = (exponent.astype(F32) * (probs_grad - delta)).astype(BF16)
        query_grad = (mm(keys_t, scores_grad) * (head**-0.5)).astype(BF16)
        rows = slice(e * head, (e + 1) * head)
        d_buf[rows] = mm(query_grad, slot_matrix(position[e : e + 1])).astype(BF16)
        key_grad = key_grad + mm(slots_ref[e, :head], scores_grad, NT)
        value_grad = value_grad + mm(slot_grad, exponent, NT)

    out_columns = slice(inner, inner + width)
    if finish and first:
        packed_out[: first * head, out_columns] = packed_in[...]
    for e in range(first, last):
        rows = slice(e * head, (e + 1) * head)
        held = slice((e - first) * head, (e - first + 1) * head)
        hw_buf[held] = (heads_ref[rows].astype(F32) * weights[e : e + 1]).astype(BF16)
    out_grad = mm(hw_buf[...], gl_buf[...], NT).astype(BF16)
    if finish:
        packed_out[mine, out_columns] = out_grad
    else:
        packed_out[...] = out_grad
    weight_grad = jnp.concatenate(weight_grads, axis=0)
    if not finish:
        d_out[...] = d_buf[mine]
        kv_grad_out[:head] = key_grad
        kv_grad_out[head:] = value_grad
        hits_out[:last] = weight_grad
        hits_out[last:] = jnp.zeros((experts - last, length), F32)
        return

    d_buf[inner : inner + head] = key_grad.astype(BF16)
    d_buf[inner + head : inner + 2 * head] = value_grad.astype(BF16)
    hits, kept = route_hits(codes_ref, layer, experts)
    gates = [tables_ref[2 * experts + k : 2 * experts + k + 1] for k in range(2)]
    inverse = tables_ref[2 * experts + 2 : 2 * experts + 3]
    chosen = [
        jnp.sum(hit * weight_grad, axis=0, keepdims=True) * keep for hit, keep in zip(hits, kept)
    ]
    mean = gates[0] * chosen[0] + gates[1] * chosen[1]
    logit_grad = sum(
        gate * (item - mean) * hit for gate, item, hit in zip(gates, chosen, hits)
    ).astype(BF16)

    packed_out[:, :inner] = mm(x_ref[...], d_buf[:inner], NT).astype(BF16)
    kv_columns = slice(inner + width, inner + width + 2 * head)
    packed_out[:, kv_columns] = mm(s_ref[...], d_buf[inner:], NT).astype(BF16)
    padded = jnp.concatenate([logit_grad.astype(F32), jnp.zeros((120, length), F32)], axis=0)
    router_grad = mm(x_ref[...], padded.astype(BF16), NT)
    flush(packed_out, (slice(None), slice(0, kv_columns.stop)))

    grad = mm(query_ref[0], d_buf[:inner]) + mm(router_ref[0], logit_grad, TN)
    source_grad = mm(keyval_ref[0], d_buf[inner:])
    if cross:
        s_out[...] = source_grad
        flush(s_out)
    else:
        grad = grad + source_grad
    gain = gain_column(gains_ref, gain_at)
    back, gain_grad = normalize_back(grad, x_ref[...], inverse, gain)
    lane = lax.broadcasted_iota(jnp.int32, router_grad.shape, 1)
    extra = jnp.where(lane == experts, gain_grad, router_grad)
    extra = jnp.where(lane == experts + 1, feed_gain_ref[:, 0:1], extra)
    packed_out[:, kv_columns.stop :] = extra.astype(BF16)
    flush(packed_out, (slice(None), slice(kv_columns.stop, packed_out.shape[1])))
    total = g_ref[...] + back
    if cross:
        g_out[...] = total
    else:
        g_out[...] = total.T


def gelu_parts(values):
    half = 0.5 * (1.0 + lax.erf(values * ROOT_HALF))
    slope = half + values * jnp.exp(-0.5 * values * values) * INV_ROOT_TWO_PI
    return values * half, slope


def hidden_chunks(own, other, axis):
    size = own.shape[axis]
    found = []
    for part, ref in enumerate((own, other)):
        for at in range(0, size, FEED_CHUNK):
            found.append(
                (part, slice(at, at + FEED_CHUNK), slice(part * size + at, part * size + at + FEED_CHUNK))
            )
    return found


def feed_weight_grads(
    grad_low, by_rows, x_ref, wout_refs, hidden_ref, slope_ref, inner_ref, packed_refs
):
    width = x_ref.shape[0]
    size = wout_refs[0].shape[0]
    for part, here, there in reversed(hidden_chunks(wout_refs[0], wout_refs[1], 0)):
        grad = mm(wout_refs[part][here, :], grad_low, NT if by_rows else NN)
        inner = (grad * slope_ref[there].astype(F32)).astype(BF16)
        inner_ref[there] = inner
        packed = packed_refs[part]
        packed[:width, here] = mm(x_ref[...], inner, NT).astype(BF16)
        out_grad = mm(hidden_ref[there], grad_low, NN if by_rows else NT).astype(BF16)
        fold = here.start // (size // 2)
        at = width + here.start - fold * (size // 2)
        packed[at : at + FEED_CHUNK, fold * width : (fold + 1) * width] = out_grad
        flush(inner_ref, there)
        if here.start == 0:
            flush(packed)


def feed_rows_grad(win_refs, inner_ref):
    size = win_refs[0].shape[1]
    return mm(win_refs[0][...], inner_ref[:size]) + mm(win_refs[1][...], inner_ref[size:])


def feed_hidden(x, win_refs, hidden_ref, slope_ref):
    for part, here, there in hidden_chunks(win_refs[0], win_refs[1], 1):
        hidden, slope = gelu_parts(mm(win_refs[part][:, here], x, TN))
        hidden_ref[there] = hidden.astype(BF16)
        slope_ref[there] = slope.astype(BF16)
        flush(hidden_ref, there)
        flush(slope_ref, there)


def feed_result(wout_refs, hidden_ref):
    size = wout_refs[0].shape[0]
    return mm(wout_refs[0][...], hidden_ref[:size], TN) + mm(
        wout_refs[1][...], hidden_ref[size:], TN
    )


def feed_encoder_kernel(
    gain_at, h_ref, gains_ref, win_own, win_other, wout_own, wout_other,
    low_out, rows_out, x_out, inverse_out, hidden_out, slope_out,
):
    gain = gain_column(gains_ref, gain_at)
    scaled, inverse = normalize(h_ref[...])
    x_out[...] = (scaled * gain).astype(BF16)
    inverse_out[...] = inverse
    flush(x_out)
    feed_hidden(x_out[...], (win_own, win_other), hidden_out, slope_out)
    encoded = h_ref[...] + feed_result((wout_own, wout_other), hidden_out)
    low_out[...] = encoded.astype(BF16)
    rows_out[...] = encoded.T.astype(BF16)


def feed_encoder_weights_kernel(
    cot_ref, s_ref, x_ref, hidden_ref, slope_ref, wout_own, wout_other,
    g_out, inner_out, own_out, other_out, low_buf,
):
    g_out[...] = cot_ref[...].astype(F32).T + s_ref[...]
    low_buf[...] = g_out[...].astype(BF16)
    flush(g_out)
    feed_weight_grads(
        low_buf[...], False, x_ref, (wout_own, wout_other), hidden_ref, slope_ref, inner_out,
        (own_out, other_out),
    )


def feed_encoder_rows_kernel(
    gain_at, g_ref, gains_ref, x_ref, inverse_ref, inner_ref, win_own, win_other,
    g_out, gain_out,
):
    gain = gain_column(gains_ref, gain_at)
    grad = feed_rows_grad((win_own, win_other), inner_ref)
    back, gain_grad = normalize_back(grad, x_ref[...], inverse_ref[...], gain)
    g_out[...] = g_ref[...] + back
    gain_out[...] = jnp.broadcast_to(gain_grad, gain_out.shape)


def feed_decoder_weights_kernel(
    gain_at, h_ref, cot_ref, gains_ref, win_own, win_other, wout_own, wout_other,
    x_out, inverse_out, hidden_out, inner_out, own_out, other_out, slope_buf,
):
    gain = gain_column(gains_ref, gain_at)
    scaled, inverse = normalize(h_ref[...])
    x_out[...] = (scaled * gain).astype(BF16)
    inverse_out[...] = inverse
    flush(x_out)
    feed_hidden(x_out[...], (win_own, win_other), hidden_out, slope_buf)
    feed_weight_grads(
        cot_ref[...], True, x_out, (wout_own, wout_other), hidden_out, slope_buf, inner_out,
        (own_out, other_out),
    )


def feed_decoder_rows_kernel(
    gain_at, cot_ref, gains_ref, x_ref, inverse_ref, inner_ref, win_own, win_other,
    g_out, gain_out,
):
    gain = gain_column(gains_ref, gain_at)
    grad = feed_rows_grad((win_own, win_other), inner_ref)
    back, gain_grad = normalize_back(grad, x_ref[...], inverse_ref[...], gain)
    g_out[...] = cot_ref[...].astype(F32).T + back
    gain_out[...] = jnp.broadcast_to(gain_grad, gain_out.shape)


def feed_decoder_result_kernel(h_ref, hidden_ref, wout_own, wout_other, rows_out):
    result = h_ref[...] + feed_result((wout_own, wout_other), hidden_ref)
    rows_out[...] = result.T.astype(BF16)


def first_kernel(parts, *refs):
    refs = list(refs)
    take = lambda count: [refs.pop(0) for _ in range(count)]
    gains, codes, pairs = take(3)
    given = [take(5) for _ in parts]
    made = [take(8) for _ in parts]
    held = [take(4) for _ in parts]
    for part, ins, outs, scratch in zip(parts, given, made, held):
        attend_forward_kernel(*part, ins[0], gains, codes, pairs, *ins[1:], *outs, *scratch)


def middle_kernel(part, gain_b, gain_e, *refs):
    refs = list(refs)
    take = lambda count: [refs.pop(0) for _ in range(count)]
    gains, codes, pairs, h_ref, d_ref, cot_ref = take(6)
    mixture, feed_b, feed_e = take(4), take(4), take(4)
    encoder, cross = take(6), take(8)
    hidden_out, own_out, other_out, g_out, gain_out = take(5)
    held = take(4)
    x_buf, inverse_buf = refs
    feed_encoder_kernel(gain_b, h_ref, gains, *feed_b, *encoder)
    attend_forward_kernel(
        *part, d_ref, encoder[0], gains, codes, pairs, *mixture, *cross, *held
    )
    for ref in encoder[4:]:
        ref.finish()
    inner_buf, slope_buf = [ref.buffer for ref in encoder[4:]]
    feed_decoder_weights_kernel(
        gain_e, cross[0], cot_ref, gains, *feed_e,
        x_buf, inverse_buf, hidden_out, inner_buf, own_out, other_out, slope_buf,
    )
    feed_decoder_rows_kernel(
        gain_e, cot_ref, gains, x_buf, inverse_buf, inner_buf, *feed_e[:2], g_out, gain_out
    )


def feed_encoder_back_kernel(
    gain_at, cot_ref, s_ref, gains_ref, x_ref, inverse_ref, hidden_ref, slope_ref,
    wout_own, wout_other, win_own, win_other,
    g_out, own_out, other_out, gain_out, low_buf, g_buf, inner_buf,
):
    feed_encoder_weights_kernel(
        cot_ref, s_ref, x_ref, hidden_ref, slope_ref, wout_own, wout_other,
        g_buf, inner_buf, own_out, other_out, low_buf,
    )
    feed_encoder_rows_kernel(
        gain_at, g_buf, gains_ref, x_ref, inverse_ref, inner_buf, win_own, win_other,
        g_out, gain_out,
    )


def unpack_feed_kernel(pieces, place_ref, *refs):
    in_out, out_out, packed_ref = refs[-3:]
    width = in_out.shape[0]
    size = packed_ref.shape[0] // pieces
    packed_ref[: packed_ref.shape[0] // 2] = refs[0][0]
    packed_ref[packed_ref.shape[0] // 2 :] = refs[1][0]
    for piece in range(pieces):
        at = pl.multiple_of(jnp.bitwise_xor(place_ref[0], piece) * size, size)
        rows = packed_ref[pl.ds(at, size), :].astype(F32)
        if piece * size < width:
            in_out[piece * size : (piece + 1) * size] = rows
        else:
            at = piece * size - width
            out_out[at : at + size] = rows[:, :width]
            out_out[width + at : width + at + size] = rows[:, width:]


def unpack_mixture_kernel(pieces, place_ref, low_ref, high_ref, *refs):
    query_out, output_out, keyval_out, router_out, gains_out, extra, packed_ref = refs[-7:]
    size = packed_ref.shape[0] // pieces
    packed_ref[: packed_ref.shape[0] // 2] = low_ref[0]
    packed_ref[packed_ref.shape[0] // 2 :] = high_ref[0]
    inner, width = query_out.shape[1], output_out.shape[1]
    end = inner + width + keyval_out.shape[1]
    experts = router_out.shape[0]
    for piece in range(pieces):
        position = jnp.bitwise_xor(place_ref[0], piece)
        crossed = jnp.where(position >= pieces // 2, place_ref[1], 0)
        at = pl.multiple_of(jnp.bitwise_xor(position, crossed) * size, size)
        rows = packed_ref[pl.ds(at, size), :].astype(F32)
        there = slice(piece * size, (piece + 1) * size)
        query_out[there] = rows[:, :inner]
        output_out[there] = rows[:, inner : inner + width]
        keyval_out[there] = rows[:, inner + width : end]
        extra[there] = rows[:, end:]
    turned = extra[...].T
    router_out[...] = turned[:experts]
    gains_out[...] = turned[experts : experts + 8]


LEFT = "left"
WHOLE = "whole"
LARGE = 2**17


class Fetched:
    def __init__(self, source, buffer, sem):
        self.copy = pltpu.make_async_copy(source, buffer, sem)
        self.copy.start()
        self.buffer, self.shape, self.waits = buffer, buffer.shape, True

    def ready(self):
        if self.waits:
            self.copy.wait()
            self.waits = False
        return self.buffer

    def __getitem__(self, at):
        return self.ready()[at]


class Stored:
    def __init__(self, place, buffer, sems):
        self.place, self.buffer, self.sems = place, buffer, sems
        self.shape = buffer.shape
        self.copies = []
        self.finished = False

    def __getitem__(self, at):
        return self.buffer[at]

    def __setitem__(self, at, value):
        self.buffer[at] = value

    def flush(self, at=None):
        source, place = self.buffer, self.place
        if at is not None:
            source, place = source.at[at], place.at[at]
        self.copies.append(pltpu.make_async_copy(source, place, self.sems.at[len(self.copies)]))
        self.copies[-1].start()

    def finish(self):
        if self.finished:
            return
        if not self.copies:
            self.flush()
        for copy in self.copies:
            copy.wait()
        self.finished = True


def flush(ref, at=None):
    if isinstance(ref, Stored):
        ref.flush(at)


FLUSHES = 8


def layer_spec(array, layer):
    return (layer, True)


def call(kernel, name, outs, args, in_specs, out_specs, scratch, flops, limit=VMEM_LIMIT):
    shapes = [jax.ShapeDtypeStruct(shape, dtype) for shape, dtype in outs]
    ins, buffers = [], []
    for item, spec in zip(args, in_specs):
        shape = item.shape
        if isinstance(spec, tuple):
            shape = ((1,) if spec[1] else ()) + item.shape[1:]
        size = item.dtype.itemsize
        for extent in shape:
            size *= extent
        mine = isinstance(spec, tuple) or (spec == WHOLE and size >= LARGE)
        ins.append(spec if mine else None)
        if mine:
            buffers.append(pltpu.VMEM(shape, item.dtype))
    stored = [
        spec == WHOLE and item.size * item.dtype.itemsize >= LARGE
        for item, spec in zip(shapes, out_specs)
    ]
    buffers += [pltpu.VMEM(item.shape, item.dtype) for item, mine in zip(shapes, stored) if mine]
    count = len(buffers)
    fetched = sum(item is not None for item in ins)

    def wrapped(*refs):
        refs = list(refs)
        given, made = refs[: len(ins)], refs[len(ins) : len(ins) + len(shapes)]
        rest = refs[len(ins) + len(shapes) :]
        own, held, sems_in, sems_out = rest[: len(scratch)], rest[len(scratch) : -2], rest[-2], rest[-1]
        used = 0
        for k, spec in enumerate(ins):
            if spec is not None:
                source = given[k]
                if isinstance(spec, tuple):
                    source = source.at[pl.ds(spec[0], 1)] if spec[1] else source.at[spec[0]]
                given[k] = Fetched(source, held[used], sems_in.at[used])
                used += 1
        for k, mine in enumerate(stored):
            if mine:
                made[k] = Stored(made[k], held[used], sems_out.at[used - fetched])
                used += 1
        kernel(*given, *made, *own)
        for item in given:
            if isinstance(item, Fetched):
                item.ready()
        for item in made:
            if isinstance(item, Stored):
                item.finish()

    moved = sum(a.size * a.dtype.itemsize for a in args) + sum(
        s.size * s.dtype.itemsize for s in shapes
    )
    vmem, hbm = pl.BlockSpec(memory_space=pltpu.VMEM), pl.BlockSpec(memory_space=pl.ANY)
    return pl.pallas_call(
        wrapped,
        name=name,
        out_shape=shapes,
        in_specs=[hbm if k is not None or s == LEFT else vmem for k, s in zip(ins, in_specs)],
        out_specs=[hbm if k or s == LEFT else vmem for k, s in zip(stored, out_specs)],
        scratch_shapes=list(scratch) + buffers + [
            pltpu.SemaphoreType.DMA((max(fetched, 1),)),
            pltpu.SemaphoreType.DMA((max(count - fetched, 1), FLUSHES)),
        ],
        compiler_params=pltpu.CompilerParams(vmem_limit_bytes=limit),
        cost_estimate=pl.CostEstimate(flops=30 * flops, bytes_accessed=moved, transcendentals=0),
    )(*args)


def body(
    source, target, routes, overflow, pairs, gains, router, query, keyval, output,
    ffn_in, ffn_out, cot_source, cot_target,
):
    _, length, width = source.shape
    experts = router.shape[2]
    head = keyval.shape[2] // 2
    inner = experts * head
    hidden = ffn_in.shape[2] * lax.axis_size("ffn")
    router = jnp.transpose(router, (0, 2, 1))
    codes = jnp.transpose(routes[0] + experts * overflow[0], (0, 2, 1))
    pair_rows = pairs[0]
    swap = [(0, 1), (1, 0)]
    win_other = lax.ppermute(ffn_in, "ffn", swap)
    wout_other = lax.ppermute(ffn_out, "ffn", swap)

    def layer_args(layer):
        arrays = (router, query, keyval, output)
        return arrays, [layer_spec(item, layer) for item in arrays]

    attend_outs = [
        ((width, length), F32),
        ((width, length), BF16),
        ((3 * experts, length), F32),
        ((experts, length, CAPACITY), BF16),
        ((experts, CAPACITY), F32),
        ((experts, 2 * head, CAPACITY), BF16),
        ((inner, length), BF16),
        ((2 * head, length), BF16),
    ]
    attend_specs = [WHOLE] * 3 + [LEFT] + [WHOLE] * 4
    attend_scratch = [
        pltpu.VMEM((experts, length, CAPACITY), BF16),
        pltpu.VMEM((inner, length), BF16),
        pltpu.VMEM((inner, length), BF16),
        pltpu.SemaphoreType.DMA((experts,)),
    ]

    def attend_back(layer, gain_at, grad, saved, keys, feed_gain):
        cross = keys is not None
        _, normed, tables, exponents, linv, slots, heads, kv = saved
        arrays, specs = layer_args(layer)
        args = [grad, gains, codes, tables, linv, slots, heads, kv, output, exponents, normed]
        args += ([keys] if cross else []) + list(arrays[:3]) + [feed_gain]
        arg_specs = [WHOLE] * 8 + [specs[3], LEFT] + [WHOLE] * (2 if cross else 1)
        arg_specs += specs[:3] + [WHOLE]
        outs = [((width, length) if cross else (length, width), F32)]
        outs += [((width, length), F32)] if cross else []
        outs += [((width, inner + width + 2 * head + 128), BF16)]
        return call(
            functools.partial(attend_backward_kernel, layer, cross, gain_at, 0, experts),
            f"attend_back{layer}", outs, args, arg_specs, [WHOLE] * len(outs),
            [
                pltpu.VMEM((experts, length, CAPACITY), BF16),
                pltpu.VMEM((inner, length), F32),
                pltpu.VMEM((width, length), BF16),
                pltpu.VMEM((inner + 2 * head, length), BF16),
                pltpu.VMEM((inner, length), BF16),
                pltpu.SemaphoreType.DMA((experts,)),
            ],
            13 * 10**9,
        )

    def half_spec(array, index):
        return (index, False)

    def ffn_args(index):
        arrays = [ffn_in, win_other, ffn_out, wout_other]
        return arrays, [half_spec(item, index) for item in arrays]

    travelling = []

    def boundary(values):
        going = [(item, item.work()) for item in travelling]
        going = [(item, work) for item, work in going if work is not None]
        works = [work for _, work in going if work[1]]
        made = fold(works) if works else []
        ended = [item for item in travelling if item.work() is None and not item.ended]
        brought = [item.inputs for item in ended]
        values, made, brought = lax.optimization_barrier((values, made, brought))
        for item, item.inputs in zip(ended, brought):
            item.ended = True
        for item, work in going:
            item.send(made.pop(0) if work[1] else None)
        return values, not all(item.ended for item in travelling)

    last_made = []

    def event(values, items):
        going = [(item, item.work()) for item in items if item.work() is not None]
        works = [work for _, work in going]
        ended = [item for item in items if item.work() is None and not item.ended]
        tied = (values, [work[1] for work in works], [item.inputs for item in ended], last_made)
        values, inputs, brought, _ = lax.optimization_barrier(tied)
        for item, item.inputs in zip(ended, brought):
            item.ended = True
        if works:
            made = fold([(work[0], given, work[2]) for work, given in zip(works, inputs)])
            last_made[:] = [arrays[0] for arrays in made]
            for (item, _), arrays in zip(going, made):
                item.send(arrays)
        return values

    packed_shape = (2 * width, hidden // 2)
    common = [gains, codes, pair_rows]
    layers = [layer_args(layer) for layer in range(3)]
    parts = [(0, False, False, True, 0, 0, 0), (1, True, False, True, 1, 1, 2)]
    saved = call(
        functools.partial(first_kernel, parts), "attend_self", attend_outs * 2,
        common + [source[0], *layers[0][0], target[0], *layers[1][0]],
        [WHOLE] * 3 + [WHOLE, *layers[0][1], WHOLE, *layers[1][1]],
        attend_specs * 2, attend_scratch * 2, 16 * 10**9,
    )
    saved_a, saved_c = saved[:8], saved[8:]
    feed_args = [ffn_args(0), ffn_args(1)]
    made = call(
        functools.partial(middle_kernel, (2, False, True, False, 1, 0, 3), 1, 4), "middle",
        [
            ((width, length), BF16), ((length, width), BF16), ((width, length), BF16),
            ((1, length), F32), ((hidden, length), BF16), ((hidden, length), BF16),
        ] + attend_outs + [
            ((hidden, length), BF16), (packed_shape, BF16), (packed_shape, BF16),
            ((width, length), F32), ((width, 128), F32),
        ],
        common + [saved_a[0], saved_c[0], cot_target[0], *layers[2][0]]
        + feed_args[0][0] + feed_args[1][0],
        [WHOLE] * 6 + layers[2][1] + feed_args[0][1] + feed_args[1][1],
        [WHOLE] * 6 + attend_specs + [WHOLE] * 5,
        attend_scratch + [pltpu.VMEM((width, length), BF16), pltpu.VMEM((1, length), F32)],
        28 * 10**9, MIDDLE_VMEM,
    )
    encoded_low, encoded_rows, normed_b, inverse_b, hidden_b, slope_b = made[:6]
    saved_d = made[6:14]
    hidden_e, own_e, other_e, grad_e, gain_e = made[14:]
    feed_e = Exchange([own_e[None]], other_e[None], 3)
    travelling.append(feed_e)
    grad_e, _ = boundary(grad_e)
    grad_d, source_grad, packed_d = attend_back(2, 3, grad_e, saved_d, encoded_low, gain_e)
    source_grad, _ = boundary(source_grad)
    weights, weight_specs = feed_args[0]
    grad_b, own_b, other_b, gain_b = call(
        functools.partial(feed_encoder_back_kernel, 1), "feed_encoder_back",
        [((width, length), F32), (packed_shape, BF16), (packed_shape, BF16), ((width, 128), F32)],
        [cot_source[0], source_grad, gains, normed_b, inverse_b, hidden_b, slope_b]
        + weights[2:] + weights[:2],
        [WHOLE] * 7 + weight_specs[2:] + weight_specs[:2], [WHOLE] * 4,
        [
            pltpu.VMEM((width, length), BF16), pltpu.VMEM((width, length), F32),
            pltpu.VMEM((hidden, length), BF16),
        ],
        10 * 10**9,
    )
    feed_b = Exchange([own_b[None]], other_b[None], 3)
    travelling.append(feed_b)
    (grad_d, grad_b), _ = boundary((grad_d, grad_b))
    grad_target, packed_c = attend_back(1, 2, grad_d, saved_c, None, gain_b)
    mixture_dc = Exchange([packed_c[None], packed_d[None]], scattered=3)
    travelling.append(mixture_dc)
    grad_b, _ = boundary(grad_b)
    grad_source, packed_a = attend_back(0, 0, grad_b, saved_a, None, gain_b)
    mixture_a = Exchange([packed_a[None]], scattered=3)
    travelling.append(mixture_a)
    hidden_e, _ = boundary(hidden_e)
    (decoded_rows,) = call(
        feed_decoder_result_kernel, "feed_decoder_result", [((length, width), BF16)],
        [saved_d[0], hidden_e] + ffn_args(1)[0][2:], [WHOLE] * 2 + ffn_args(1)[1][2:], [WHOLE], [],
        3 * 10**9,
    )

    def unpack_feed(exchange, index, made):
        pieces = exchange.pieces
        shapes = [
            jax.ShapeDtypeStruct((2,) + item.shape[1:], F32) for item in (ffn_in, ffn_out)
        ]
        spec = lambda item: pl.BlockSpec(
            (None,) + item.shape[1:], lambda i: (index, 0, 0), pipeline_mode=pl.Buffered(1)
        )
        return pl.pallas_call(
            functools.partial(unpack_feed_kernel, pieces), name="unpack_feed", grid=(1,),
            out_shape=shapes,
            in_specs=[pl.BlockSpec(memory_space=pltpu.SMEM)] + [pl.BlockSpec(memory_space=pltpu.VMEM)] * 2
            + [pl.BlockSpec(memory_space=pl.ANY)] * len(made),
            out_specs=[spec(item) for item in shapes],
            scratch_shapes=[pltpu.VMEM(packed_shape, BF16)],
            input_output_aliases={3 + k: k for k in range(len(made))},
            compiler_params=pltpu.CompilerParams(vmem_limit_bytes=VMEM_LIMIT),
            cost_estimate=pl.CostEstimate(flops=10**11, bytes_accessed=10**6, transcendentals=0),
        )(exchange.place, *exchange.inputs, *made)

    def unpack_mixture(exchange, first, made):
        layers = exchange.inputs[0].shape[0]
        columns = (inner, width, 2 * head)
        shapes = [jax.ShapeDtypeStruct((3, width, size), F32) for size in columns]
        shapes += [jax.ShapeDtypeStruct((3, rows, width), F32) for rows in (experts, 8)]
        return pl.pallas_call(
            functools.partial(unpack_mixture_kernel, exchange.pieces), name="unpack_mixture",
            grid=(layers,),
            out_shape=shapes,
            in_specs=[
                pl.BlockSpec(memory_space=pltpu.SMEM),
            ] + [
                pl.BlockSpec((1,) + item.shape[1:], lambda i: (i, 0, 0)) for item in exchange.inputs
            ] + [pl.BlockSpec(memory_space=pl.ANY)] * len(made),
            out_specs=[
                pl.BlockSpec((None,) + item.shape[1:], lambda i: (first + i, 0, 0))
                for item in shapes
            ],
            scratch_shapes=[
                pltpu.VMEM((width, 128), F32),
                pltpu.VMEM((width,) + exchange.inputs[0].shape[2:], BF16),
            ],
            input_output_aliases={3 + k: k for k in range(len(made))},
            compiler_params=pltpu.CompilerParams(vmem_limit_bytes=VMEM_LIMIT),
            cost_estimate=pl.CostEstimate(flops=10**11, bytes_accessed=10**6, transcendentals=0),
        )(exchange.place, *exchange.inputs, *made)

    unpacks = [
        (feed_e, unpack_feed, 1), (feed_b, unpack_feed, 0),
        (mixture_dc, unpack_mixture, 1), (mixture_a, unpack_mixture, 0),
    ]
    unpacked = {unpack_feed: [], unpack_mixture: []}
    groups = [[feed_e, feed_b], [mixture_dc, mixture_a]]
    held = [decoded_rows, [], []]
    order = [0, 1, 0, 1, 0, 1, 0, 1, 0, 1, 1, 0, 1, 1]
    while unpacks:
        for group in [groups[k] for k in order]:
            if not all(item.ended for item in group):
                held = event(held, group)
            for item in unpacks:
                exchange, unpack, index = item
                if exchange.ended:
                    at = 1 + (unpack is unpack_mixture)
                    held[at] = unpack(exchange, index, held[at])
                    unpacks.remove(item)
                    break
    decoded_rows, grads_ffn, merged = held
    gain_rows = merged[4][:, :2].reshape(6, width)
    grad_gains = jnp.concatenate([gain_rows[:3], gain_rows[4:]], axis=0)
    return (
        encoded_rows[None],
        decoded_rows[None],
        grad_source[None],
        grad_target[None],
        grad_gains,
        jnp.transpose(merged[3], (0, 2, 1)),
        merged[0],
        merged[2],
        merged[1],
        grads_ffn[0],
        grads_ffn[1],
    )


DOWN = ("halve", "stack")


class Exchange:
    def __init__(self, arrays, other=None, scattered=3):
        devices, columns = lax.axis_size("batch"), lax.axis_size("ffn")
        batch, column = lax.axis_index("batch"), lax.axis_index("ffn")
        across = [
            (b * columns + c, b * columns + (c ^ 1)) for b in range(devices) for c in range(columns)
        ]
        split = other is None
        steps = [(across, column.astype(jnp.int32))] if split else []
        beside = []
        bits = [1 << k for k in range(devices.bit_length() - 1)]
        orders = [bits, bits[1::-1] + bits[2:]]
        for level in range(len(bits)):
            choice = [orders[c % 2][level] for c in range(columns)]
            pairs = [
                (b * columns + c, (b ^ choice[c]) * columns + c)
                for b in range(devices) for c in range(columns)
            ]
            bit = jnp.where(column % 2 == 0, choice[0], choice[1])
            steps.append((pairs, (jnp.bitwise_and(batch, bit) != 0).astype(jnp.int32)))
            bit = jnp.where(column % 2 == 0, choice[-1], choice[0])
            beside.append((jnp.bitwise_and(batch, bit) != 0).astype(jnp.int32))
        down = scattered + int(split)
        self.pieces = 1 << down
        place = jnp.int32(0)
        for _, upper in steps[:down]:
            place = place * 2 + upper
        own = other_place = jnp.int32(0)
        for (_, upper), upper_beside in zip(steps[int(split) : down], beside):
            own = own * 2 + upper
            other_place = other_place * 2 + upper_beside
        self.place = jnp.stack([place, jnp.bitwise_xor(own, other_place)])
        self.plan = [] if split else [("send", across, None)]
        self.plan += [("halve", pairs, upper) for pairs, upper in steps[:down]]
        if split and len(arrays) > 1:
            self.plan[0] = ("stack",) + self.plan[0][1:]
        self.plan += [("add", pairs, None) for pairs, _ in steps[down:]]
        self.plan += [
            ("join" if k else "add", pairs, None)
            for k, (pairs, _) in enumerate(reversed(steps[:down]))
        ]
        self.at = 0
        self.ended = False
        self.inputs = arrays
        if not split:
            self.kept, self.sent = arrays[0], other

    def work(self):
        if self.at == len(self.plan):
            return None
        kind, _, upper = self.plan[self.at]
        if kind == "send":
            return kind, [], None
        return kind, self.inputs, upper

    def send(self, made):
        _, pairs, _ = self.plan[self.at]
        self.at += 1
        if made:
            self.kept, self.sent = made[0], made[-1]
        self.inputs = [self.kept, lax.ppermute(self.sent, ("batch", "ffn"), pairs)]


def fold_kernel(works, uppers_ref, *refs):
    refs = list(refs)
    take = lambda count: [refs.pop(0) for _ in range(count)]
    inputs = [take(count) for _, count, _, _ in works]
    outputs = [take(1 + (kind in DOWN)) for kind, _, _, _ in works]
    buffers = [take(count) for _, _, _, count in works]
    sems_in, sems_out = refs
    at_in, started = 0, []

    def copy_in(source, target):
        nonlocal at_in
        copy = pltpu.make_async_copy(source, target, sems_in.at[at_in])
        copy.start()
        at_in += 1
        return copy

    at_out = 0

    def copy_out(source, target):
        nonlocal at_out
        copy = pltpu.make_async_copy(source, target, sems_out.at[at_out])
        copy.start()
        at_out += 1
        started.append(copy)

    waits = []
    for at, ((kind, count, rows, _), given, made, held) in enumerate(
        zip(works, inputs, outputs, buffers)
    ):
        copies = []
        if kind in DOWN:
            half = rows // 2
            upper = uppers_ref[at]
            for side, part in enumerate((upper, 1 - upper)):
                there = pl.ds(pl.multiple_of(part * half, half), half)
                for k, source in enumerate(given):
                    if kind == "stack":
                        target = held[side].at[k : k + 1]
                    else:
                        target = held[side * count + k]
                    copies.append(copy_in(source.at[:, there, :], target))
        elif kind == "add":
            for k, source in enumerate(given):
                copies.append(copy_in(source, held[k]))
        else:
            for k, source in enumerate(given):
                copies.append(copy_in(source, held[0].at[:, k * rows : (k + 1) * rows, :]))
        waits.append(copies)
    for (kind, count, rows, _), made, held, copies in zip(works, outputs, buffers, waits):
        for copy in copies:
            copy.wait()
        for side, target in enumerate(made):
            each = 1 if kind == "stack" else count
            part = held[side * each : (side + 1) * each]
            if kind in ("halve", "add") and count == 2:
                part[0][...] = part[0][...] + part[1][...]
            copy_out(part[0], target)
    for copy in started:
        copy.wait()


def fold(works):
    plans, args, outs, scratch, uppers = [], [], [], [], []
    copies_in = copies_out = 0
    for kind, inputs, upper in works:
        layers, rows, columns = inputs[0].shape
        if kind == "stack":
            layers *= len(inputs)
        made = rows // 2 if kind in DOWN else {"add": rows, "join": 2 * rows}[kind]
        sides = 1 + (kind in DOWN)
        held = {"join": 1, "stack": 2}.get(kind, sides * len(inputs))
        plans.append((kind, len(inputs), rows, held))
        args += inputs
        outs += [jax.ShapeDtypeStruct((layers, made, columns), inputs[0].dtype)] * sides
        scratch += [pltpu.VMEM((layers, made, columns), inputs[0].dtype)] * held
        copies_in += sides * len(inputs)
        copies_out += sides
        uppers.append(jnp.int32(0) if upper is None else upper)
    hbm = pl.BlockSpec(memory_space=pl.ANY)
    results = pl.pallas_call(
        functools.partial(fold_kernel, plans),
        name="fold",
        out_shape=outs,
        in_specs=[pl.BlockSpec(memory_space=pltpu.SMEM)] + [hbm] * len(args),
        out_specs=[hbm] * len(outs),
        scratch_shapes=scratch + [
            pltpu.SemaphoreType.DMA((copies_in,)), pltpu.SemaphoreType.DMA((copies_out,)),
        ],
        compiler_params=pltpu.CompilerParams(vmem_limit_bytes=VMEM_LIMIT),
        cost_estimate=pl.CostEstimate(flops=10**11, bytes_accessed=10**6, transcendentals=0),
    )(jnp.stack(uppers), *args)
    found, at = [], 0
    for kind, _, _, _ in plans:
        sides = 1 + (kind in DOWN)
        found.append(list(results[at : at + sides]))
        at += sides
    return found


def solution(mesh):
    tokens = P(("batch", "ffn"), None, None)
    return jax.shard_map(
        body,
        mesh=mesh,
        in_specs=(
            tokens, tokens, P(("batch", "ffn"), None, None, None),
            P(("batch", "ffn"), None, None, None), tokens,
            P(), P(), P(), P(), P(),
            P(None, None, "ffn"), P(None, "ffn", None), tokens, tokens,
        ),
        out_specs=(
            tokens, tokens, tokens, tokens,
            P(), P(), P(), P(), P(),
            P(None, None, "ffn"), P(None, "ffn", None),
        ),
        check_vma=False,
    )
```
